32 devices in a mesh: dp: 8 (over z, x), mp: 4 (over y, core).
Axes of the slice: x: 2, y: 2, z: 4, core: 2. Of those that a mesh axis runs over, the one named last changes fastest.
Arguments:
- tokens: bfloat16 [16384, 768], P('dp'), may hold values from -6 to 6
- lengths: int32 [32], P('dp'), may hold values from 60 to 512, as said below
- query_weight: bfloat16 [768, 768], P(None, 'mp'), may hold values from -0.21875 to 0.21875
- query_bias: bfloat16 [768], P('mp'), may hold values from -3 to 3
- key_weight: bfloat16 [768, 768], P(None, 'mp'), may hold values from -0.21875 to 0.21875
- value_weight: bfloat16 [768, 768], P(None, 'mp'), may hold values from -0.21875 to 0.21875
- value_bias: bfloat16 [768], P('mp'), may hold values from -3 to 3
- out_weight: bfloat16 [768, 768], P('mp'), may hold values from -0.875 to 0.875
- out_bias: bfloat16 [768], replicated, may hold values from -2 to 2
- attn_gain: bfloat16 [768], replicated, may hold values from 0.5 to 1.5
- attn_shift: bfloat16 [768], replicated, may hold values from -2 to 2
- up_weight: bfloat16 [768, 3072], P(None, 'mp'), may hold values from -0.21875 to 0.21875
- up_bias: bfloat16 [3072], P('mp'), may hold values from -3 to 3
- down_weight: bfloat16 [3072, 768], P('mp'), may hold values from -0.109375 to 0.109375
- down_bias: bfloat16 [768], replicated, may hold values from -2 to 2
- ffn_gain: bfloat16 [768], replicated, may hold values from 0.5 to 1.5
- ffn_shift: bfloat16 [768], replicated, may hold values from -2 to 2
- cotangent: bfloat16 [16384, 768], P('dp'), may hold values from -6 to 6
Outputs:
- layer_out: bfloat16 [16384, 768], P('dp')
- tokens_grad: bfloat16 [16384, 768], P('dp')
- query_weight_grad: float32 [768, 768], P(None, 'mp')
- query_bias_grad: float32 [768], P('mp')
- key_weight_grad: float32 [768, 768], P(None, 'mp')
- value_weight_grad: float32 [768, 768], P(None, 'mp')
- value_bias_grad: float32 [768], P('mp')
- out_weight_grad: float32 [768, 768], P('mp')
- out_bias_grad: float32 [768], replicated
- attn_gain_grad: float32 [768], replicated
- attn_shift_grad: float32 [768], replicated
- up_weight_grad: float32 [768, 3072], P(None, 'mp')
- up_bias_grad: float32 [3072], P('mp')
- down_weight_grad: float32 [3072, 768], P('mp')
- down_bias_grad: float32 [768], replicated
- ffn_gain_grad: float32 [768], replicated
- ffn_shift_grad: float32 [768], replicated
The draws below stay inside these ranges and needn't reach their ends.
Inputs may be any that keep to these rules, and one draw needn't show every extreme that they name: `lengths`: in every draw some table has all 512 tokens live and some has the fewest allowed.
All inputs are finite; a program needn't handle non-finite values.
Results may differ from the reference program's by a relative error of at most 0.022.
Values may be sent and summed in bfloat16 or wider, within the bound.
A program may use at most 128 MiB of HBM per device.

```python
import jax
import jax.numpy as jnp
from jax import lax

D = 768
HD = 64
FF = 3072
SEQ = 512
TAB_DEV = 4
TABLES = 32
N_DP = 8
N_MP = 4


def draw_lengths(key, part):
    key = jax.random.fold_in(key, 7)
    floor_len = max(SEQ * 15 // 128, 1)
    range_key, order_key = jax.random.split(key)
    lengths_drawn = jax.random.randint(range_key, (TABLES,), floor_len, SEQ + 1, dtype=jnp.int32)
    shuffled = jax.random.permutation(order_key, TABLES)
    lengths_drawn = lengths_drawn.at[shuffled[0]].set(SEQ)
    lengths_drawn = lengths_drawn.at[shuffled[1]].set(floor_len)
    return lengths_drawn


def block_scale(own_key, shape, cuts, smallest, largest):
    loudness = 1.0
    for axis_at, blocks in cuts:
        steps = jax.random.uniform(jax.random.fold_in(jax.random.fold_in(own_key, 6), axis_at), (blocks,), jnp.float32, smallest / len(cuts), largest / len(cuts))
        loudness = loudness * jnp.repeat(jnp.exp(steps), shape[axis_at] // blocks).reshape((-1,) + (1,) * (len(shape) - 1 - axis_at))
    return loudness


def normal_values(stream_key, dims, width, reach, cuts=(), kind=jnp.bfloat16):
    factor_of = block_scale(stream_key, dims, cuts, -0.22, 0.18) if cuts else 1.0
    drawn = jax.random.normal(stream_key, dims, jnp.float32) * width * factor_of
    return jnp.minimum(jnp.maximum(drawn, -reach), reach).astype(kind)


def setup_inputs(seed: int = 0) -> dict:
    seeds = jax.random.split(jax.random.key(seed), 19)
    tokens = normal_values(seeds[0], (TABLES * SEQ, D), 1.0, 6.0, ((0, 8),))
    lengths = draw_lengths(jax.random.fold_in(seeds[18], 71), 0)
    query_weight = normal_values(seeds[2], (D, D), D ** -0.5, 0.21875, ((1, 4),))
    query_bias = normal_values(seeds[3], (D,), 0.5, 3.0, ((0, 4),))
    key_weight = normal_values(seeds[4], (D, D), D ** -0.5, 0.21875, ((1, 4),))
    value_weight = normal_values(seeds[5], (D, D), D ** -0.5, 0.21875, ((1, 4),))
    value_bias = normal_values(seeds[6], (D,), 0.5, 3.0, ((0, 4),))
    out_weight = normal_values(seeds[7], (D, D), (D // 16) ** -0.5, 0.875, ((0, 4),))
    out_bias = normal_values(seeds[8], (D,), 0.3, 2.0)
    attn_gain = jnp.clip(1.0 + 0.1 * jax.random.normal(seeds[9], (D,), jnp.float32), 0.5, 1.5).astype(jnp.bfloat16)
    attn_shift = normal_values(seeds[10], (D,), 0.3, 2.0)
    up_weight = normal_values(seeds[11], (D, FF), D ** -0.5, 0.21875, ((1, 4),))
    up_bias = normal_values(seeds[12], (FF,), 0.5, 3.0, ((0, 4),))
    down_weight = normal_values(seeds[13], (FF, D), FF ** -0.5, 0.109375, ((0, 4),))
    down_bias = normal_values(seeds[14], (D,), 0.3, 2.0)
    ffn_gain = jnp.clip(1.0 + 0.1 * jax.random.normal(seeds[15], (D,), jnp.float32), 0.5, 1.5).astype(jnp.bfloat16)
    ffn_shift = normal_values(seeds[16], (D,), 0.3, 2.0)
    cotangent = normal_values(seeds[17], (TABLES * SEQ, D), 1.0, 6.0, ((0, 8),))
    return {"tokens": tokens, "lengths": lengths, "query_weight": query_weight, "query_bias": query_bias, "key_weight": key_weight, "value_weight": value_weight, "value_bias": value_bias, "out_weight": out_weight, "out_bias": out_bias, "attn_gain": attn_gain, "attn_shift": attn_shift, "up_weight": up_weight, "up_bias": up_bias, "down_weight": down_weight, "down_bias": down_bias, "ffn_gain": ffn_gain, "ffn_shift": ffn_shift, "cotangent": cotangent}


EPS = 1e-06

@jax.custom_vjp
def low(v):
    return lax.optimization_barrier(v.astype(jnp.bfloat16)).astype(jnp.float32)

@jax.custom_vjp
def low_back(v):
    return v

def low_keep(v):
    return (low(v), None)

def low_pass(kept, grad):
    return (grad,)

def back_keep(v):
    return (v, None)

def back_low(kept, grad):
    return (low(grad),)
low.defvjp(low_keep, low_pass)
low_back.defvjp(back_keep, back_low)

def both_ways(values):
    return low(low_back(values))

def product(left, right):
    return jnp.dot(left, right, precision=lax.Precision.HIGHEST)

def normalize(mixed_rows, gain_row, shift_row):
    center = mixed_rows - lax.optimization_barrier(jnp.mean(mixed_rows, axis=-1, keepdims=True))
    spread = lax.optimization_barrier(jnp.mean(center * center, axis=-1, keepdims=True))
    return center * lax.rsqrt(spread + EPS) * gain_row + shift_row

def attend_table(pieces):
    queries, key_rows, value_rows, length = pieces
    row_count = queries.shape[0]
    query_heads = queries.reshape(row_count, -1, HD).transpose(1, 0, 2)
    key_heads = key_rows.reshape(row_count, -1, HD).transpose(1, 0, 2)
    value_heads = value_rows.reshape(row_count, -1, HD).transpose(1, 0, 2)
    scores = jnp.einsum('hqd,hkd->hqk', query_heads, key_heads, precision=lax.Precision.HIGHEST) * HD ** (-0.5)
    scores = low_back(scores)
    live_keys = jnp.arange(row_count) < length
    scores = jnp.where(live_keys[None, None, :], scores, -1e+30)
    row_top = lax.optimization_barrier(jnp.max(scores, axis=-1, keepdims=True))
    exponent = jnp.exp(scores - row_top)
    prob_rows = low(exponent / lax.optimization_barrier(jnp.sum(exponent, axis=-1, keepdims=True)))
    attended = jnp.einsum('hqk,hkd->hqd', prob_rows, value_heads, precision=lax.Precision.HIGHEST)
    return attended.transpose(1, 0, 2).reshape(row_count, -1)

def forward(param_set, tokens_f, lengths):
    query_weight, query_bias, key_weight, value_weight, value_bias, out_weight, out_bias, attn_gain, attn_shift, up_weight, up_bias, down_weight, down_bias, ffn_gain, ffn_shift = param_set
    table_count = lengths.shape[0]
    group_width = D // N_MP
    ffn_width = FF // N_MP
    attention = jnp.zeros_like(tokens_f)
    for group_index in range(N_MP):
        group_cols = slice(group_index * group_width, (group_index + 1) * group_width)
        group_tokens = low_back(tokens_f)
        queries = both_ways(product(group_tokens, query_weight[:, group_cols]) + query_bias[group_cols])
        key_rows = both_ways(product(group_tokens, key_weight[:, group_cols]))
        value_rows = both_ways(product(group_tokens, value_weight[:, group_cols]) + value_bias[group_cols])
        attended = lax.map(jax.checkpoint(attend_table), (queries.reshape(table_count, SEQ, group_width), key_rows.reshape(table_count, SEQ, group_width), value_rows.reshape(table_count, SEQ, group_width), lengths))
        attended = both_ways(attended.reshape(-1, group_width))
        attention = attention + both_ways(product(attended, out_weight[group_cols, :]))
    mixed_rows = tokens_f + attention + out_bias
    first_norm = normalize(mixed_rows, attn_gain, attn_shift)
    first_low = low(first_norm)
    down_total = jnp.zeros_like(tokens_f)
    for group_index in range(N_MP):
        group_cols = slice(group_index * ffn_width, (group_index + 1) * ffn_width)
        group_rows = low_back(first_low)
        hidden = low_back(product(group_rows, up_weight[:, group_cols]) + up_bias[group_cols])
        activated = low(jax.nn.gelu(hidden, approximate=False))
        down_total = down_total + both_ways(product(activated, down_weight[group_cols, :]))
    second_in = first_norm + down_total + down_bias
    return normalize(second_in, ffn_gain, ffn_shift)

def reference(tokens, lengths, query_weight, query_bias, key_weight, value_weight, value_bias, out_weight, out_bias, attn_gain, attn_shift, up_weight, up_bias, down_weight, down_bias, ffn_gain, ffn_shift, cotangent):
    params = tuple((array_item.astype(jnp.float32) for array_item in (query_weight, query_bias, key_weight, value_weight, value_bias, out_weight, out_bias, attn_gain, attn_shift, up_weight, up_bias, down_weight, down_bias, ffn_gain, ffn_shift)))
    row_total = TAB_DEV * SEQ

    def step_block(running, pieces):
        block_tokens, block_lengths, block_cot = pieces
        layer_rows, pullback = jax.vjp(lambda param_set, inputs: forward(param_set, inputs, block_lengths), params, block_tokens.astype(jnp.float32))
        param_grads, input_grad = pullback(block_cot.astype(jnp.float32))
        running = jax.tree.map(jnp.add, running, param_grads)
        return (running, (layer_rows.astype(jnp.bfloat16), input_grad.astype(jnp.bfloat16)))
    zero_grads = jax.tree.map(jnp.zeros_like, params)
    summed, (layer_rows, input_rows) = lax.scan(step_block, zero_grads, (tokens.reshape(N_DP, row_total, D), lengths.reshape(N_DP, TAB_DEV), cotangent.reshape(N_DP, row_total, D)))
    return (layer_rows.reshape(N_DP * row_total, D), input_rows.reshape(N_DP * row_total, D), summed[0], summed[1], summed[2], summed[3], summed[4], summed[5], summed[6], summed[7], summed[8], summed[9], summed[10], summed[11], summed[12], summed[13], summed[14])
```

```python
import jax
import jax.numpy as jnp
from jax import lax
from jax.sharding import PartitionSpec as P

HD = 64
EPS = 1e-06
BF = jnp.bfloat16
F32 = jnp.float32


def mm(a, b, ca, cb):
    return lax.dot_general(a, b, (((ca,), (cb,)), ((), ())), preferred_element_type=F32)


def split_heads(row_block):
    return row_block.reshape(row_block.shape[0], -1, HD).transpose(1, 0, 2)


def join_heads(head_block):
    return head_block.transpose(1, 0, 2).reshape(head_block.shape[1], -1)


def norm_parts(rows):
    center = rows - jnp.mean(rows, axis=-1, keepdims=True)
    inv = lax.rsqrt(jnp.mean(center * center, axis=-1, keepdims=True) + EPS)
    return center * inv, inv


def norm_back(up, normed, inv, gain):
    c = up * gain
    return inv * (
        c
        - jnp.mean(c, axis=-1, keepdims=True)
        - normed * jnp.mean(c * normed, axis=-1, keepdims=True)
    )


def attend_forward(pieces):
    q, k, v, length = pieces
    s = jnp.einsum("hqd,hkd->hqk", split_heads(q), split_heads(k), preferred_element_type=F32)
    live = lax.iota(jnp.int32, k.shape[0]) < length
    s = jnp.where(live[None, None, :], s, -1e30)
    e = jnp.exp(s - jnp.max(s, axis=-1, keepdims=True)).astype(BF)
    rinv = 1.0 / jnp.sum(e.astype(F32), axis=-1, keepdims=True)
    o = jnp.einsum("hqk,hkd->hqd", e, split_heads(v), preferred_element_type=F32) * rinv
    return join_heads(o).astype(BF), e, rinv


def attend_back(pieces):
    q, k, v, e, rinv, o, do = pieces
    qh, kh, vh = split_heads(q), split_heads(k), split_heads(v)
    doh = split_heads(do).astype(F32) * rinv
    d = jnp.sum(doh * split_heads(o).astype(F32), axis=-1, keepdims=True)
    dol = doh.astype(BF)
    dv = jnp.einsum("hqk,hqd->hkd", e, dol, preferred_element_type=F32)
    dp = jnp.einsum("hqd,hkd->hqk", dol, vh, preferred_element_type=F32)
    ds = (e.astype(F32) * (dp - d)).astype(BF)
    dq = jnp.einsum("hqk,hkd->hqd", ds, kh, preferred_element_type=F32) * HD ** (-0.5)
    dk = jnp.einsum("hqk,hqd->hkd", ds, qh, preferred_element_type=F32)
    return join_heads(dq).astype(BF), join_heads(dk).astype(BF), join_heads(dv).astype(BF)


def shards(
    tokens, lengths, wq, bq, wk, wv, bv, wo, bo, g1, s1, wu, bu, wd, bd, g2, s2, cot
):
    n = lengths.shape[0]
    rows = tokens.shape[0]
    seq = rows // n
    m = lax.axis_index("mp")
    own = lambda a: lax.dynamic_slice_in_dim(a, m * seq, seq, 0)
    f = lambda a: a.astype(F32)

    def by_table(a):
        return a.reshape(n, seq, a.shape[1])

    q = ((mm(tokens, wq, 1, 0) + f(bq)).astype(BF) * HD ** (-0.5)).astype(BF)
    k = mm(tokens, wk, 1, 0).astype(BF)
    v = (mm(tokens, wv, 1, 0) + f(bv)).astype(BF)
    att, e, rinv = lax.map(attend_forward, (by_table(q), by_table(k), by_table(v), lengths))
    att_own = lax.all_to_all(att, "mp", 0, 0)
    wo_all = lax.all_gather(wo, "mp")
    wu_all = lax.all_gather(wu, "mp")
    wd_all = lax.all_gather(wd, "mp")
    bu_all = lax.all_gather(f(bu), "mp")
    mixed = (
        f(own(tokens))
        + jnp.einsum("qtk,qkd->td", att_own, wo_all, preferred_element_type=F32)
        + f(bo)
    )
    n1, i1 = norm_parts(mixed)
    first = n1 * f(g1) + f(s1)
    first_low = first.astype(BF)
    hidden = (
        jnp.einsum("td,qdf->qtf", first_low, wu_all, preferred_element_type=F32)
        + bu_all[:, None, :]
    )
    act, gelu_pull = jax.vjp(lambda h: jax.nn.gelu(h, approximate=False), hidden)
    act = act.astype(BF)
    second = first + jnp.einsum("qtf,qfd->td", act, wd_all, preferred_element_type=F32) + f(bd)
    n2, i2 = norm_parts(second)
    out_own = (n2 * f(g2) + f(s2)).astype(BF)
    c_own = f(own(cot))
    d2 = norm_back(c_own, n2, i2, f(g2))
    d2l = d2.astype(BF)
    dg2, ds2, dbd = jnp.sum(c_own * n2, 0), jnp.sum(c_own, 0), jnp.sum(d2, 0)
    dwd = jnp.einsum("qtf,td->qfd", act, d2l, preferred_element_type=F32)
    dact = jnp.einsum("td,qfd->qtf", d2l, wd_all, preferred_element_type=F32)
    dh = gelu_pull(dact)[0].astype(BF)
    dbu = jnp.sum(f(dh), axis=1)
    dwu = jnp.einsum("td,qtf->qdf", first_low, dh, preferred_element_type=F32)
    d1 = d2 + jnp.einsum("qtf,qdf->td", dh, wu_all, preferred_element_type=F32)
    dg1, ds1 = jnp.sum(d1 * n1, 0), jnp.sum(d1, 0)
    dm = norm_back(d1, n1, i1, f(g1))
    dbo = jnp.sum(dm, 0)
    dml = dm.astype(BF)
    dwo = jnp.einsum("qtk,td->qkd", att_own, dml, preferred_element_type=F32)
    datt = jnp.einsum("td,qkd->qtk", dml, wo_all, preferred_element_type=F32).astype(BF)
    datt = lax.all_to_all(datt, "mp", 0, 0)
    dq, dk, dv = lax.map(
        attend_back, (by_table(q), by_table(k), by_table(v), e, rinv, att, datt)
    )
    dq, dk, dv = (a.reshape(rows, -1) for a in (dq, dk, dv))
    dbq, dbv = jnp.sum(f(dq), 0), jnp.sum(f(dv), 0)
    dwq, dwk, dwv = (mm(tokens, a, 0, 0) for a in (dq, dk, dv))
    back = (mm(dq, wq, 1, 1) + mm(dk, wk, 1, 1) + mm(dv, wv, 1, 1)).astype(BF)
    back = jnp.sum(f(lax.all_to_all(back.reshape(n, seq, -1), "mp", 0, 0)), 0)
    tg_own = (dm + back).astype(BF)
    layer_out = lax.all_gather(out_own, "mp", tiled=True)
    tokens_grad = lax.all_gather(tg_own, "mp", tiled=True)
    low = lambda a: a.astype(BF)
    ffn = lax.psum_scatter(jnp.stack([low(dwu), low(dwd)], 1), "mp", scatter_dimension=0)
    dwo = lax.psum_scatter(low(dwo), "mp", scatter_dimension=0)
    dbu = lax.psum_scatter(dbu, "mp", scatter_dimension=0)
    dwq, dwk, dwv, dwo, ffn = lax.psum((low(dwq), low(dwk), low(dwv), dwo, ffn), "dp")
    dbq, dbv, dbu = lax.psum((dbq, dbv, dbu), "dp")
    dbo, dg1, ds1, dbd, dg2, ds2 = lax.psum((dbo, dg1, ds1, dbd, dg2, ds2), ("dp", "mp"))
    return (
        layer_out, tokens_grad, f(dwq), dbq, f(dwk), f(dwv), dbv, f(dwo), dbo, dg1, ds1,
        f(ffn[0]), dbu, f(ffn[1]), dbd, dg2, ds2,
    )


def solution(mesh):
    row, col, one, rep = P("dp", None), P(None, "mp"), P("mp"), P()
    low = P("mp", None)
    in_specs = (
        row, P("dp"), col, one, col, col, one, low, rep, rep, rep, col, one, low, rep, rep, rep, row,
    )
    out_specs = (
        row, row, col, one, col, col, one, low, rep, rep, rep, col, one, low, rep, rep, rep,
    )
    return jax.shard_map(shards, mesh=mesh, in_specs=in_specs, out_specs=out_specs, check_vma=False)
```

```python
import functools

import jax
import jax.numpy as jnp
from jax import lax
from jax.experimental import pallas as pl
from jax.experimental.pallas import tpu as pltpu
from jax.sharding import PartitionSpec as P

HD = 64
EPS = 1e-06
BF = jnp.bfloat16
F32 = jnp.float32
MESH = pl.DeviceIdType.MESH


def mm(a, b, ca, cb):
    return lax.dot_general(a, b, (((ca,), (cb,)), ((), ())), preferred_element_type=F32)


def flip(v, b):
    return v + b - 2 * b * lax.rem(v // b, 2)


def gelu_pair(h):
    x = h * 0.7071067811865476
    e = jnp.exp(-(x * x))
    t = 1.0 / (1.0 + 0.3275911 * jnp.abs(x))
    poly = t * (
        0.254829592
        + t * (-0.284496736 + t * (1.421413741 + t * (-1.453152027 + t * 1.061405429)))
    )
    tail = 0.5 * poly * e
    phi = jnp.where(h > 0, 1.0 - tail, tail)
    return h * phi, phi + h * e * 0.3989422804014327


def norm_rows(x):
    center = x - jnp.mean(x, axis=-1, keepdims=True)
    inv = lax.rsqrt(jnp.mean(center * center, axis=-1, keepdims=True) + EPS)
    return center * inv, inv


class Comm:
    def __init__(self, nbits):
        self.dp, self.mp = lax.axis_index("dp"), lax.axis_index("mp")
        self.nbits = nbits

    def mpeer(self, k):
        v = self.mp
        for b in (1, 2):
            if k & b:
                v = flip(v, b)
        return (self.dp, v)

    def dpeer(self, bit):
        return (flip(self.dp, 1 << bit), self.mp)

    def barrier(self):
        bar = pltpu.get_barrier_semaphore()
        peers = [self.mpeer(k) for k in (1, 2, 3)] + [self.dpeer(b) for b in range(self.nbits)]
        for p in peers:
            pl.semaphore_signal(bar, inc=1, device_id=p, device_id_type=MESH)
        pl.semaphore_wait(bar, len(peers))


def rcopy(src, dst, ss, rs, dev):
    return pltpu.make_async_remote_copy(
        src_ref=src, dst_ref=dst, send_sem=ss, recv_sem=rs, device_id=dev, device_id_type=MESH
    )


def fwd_kernel(nbits, names, *refs):
    r = dict(zip(names, refs))
    ln, vec, tok = r["len"], r["vec"], r["tok"]
    TOK, WT, QT, KT, VT, ET, RI = (r[k] for k in ("TOK", "WT", "QT", "KT", "VT", "ET", "RI"))
    ATQ, ATO, N1, I1, FL, ACT, GP = (r[k] for k in ("ATQ", "ATO", "N1", "I1", "FL", "ACT", "GP"))
    WA = (r["WOA"], r["UA"], r["DA"])
    VA, FIRST, ACC, N2, I2 = (r[k] for k in ("VA", "FIRST", "ACC", "N2", "I2"))
    wsrc = (r["wo"], r["wu"], r["wd"])
    c = Comm(nbits)
    m = c.mp
    seq, d = TOK.shape[1], TOK.shape[2]
    hw = VT.shape[1]
    nh = hw // HD
    aug = QT.shape[2]

    lc = []
    for i, k in enumerate(("wq", "wk", "wv")):
        lc.append(pltpu.make_async_copy(r[k], r["W3"].at[i], r["ls"].at[i]))
    ta = [c.mpeer(k)[1] for k in (2, 3, 1, 0)]
    for i in range(4):
        lc.append(pltpu.make_async_copy(tok.at[ta[i]], TOK.at[ta[i]], r["ls"].at[3 + i]))
    for i in range(3):
        lc.append(pltpu.make_async_copy(wsrc[i], WA[i].at[m], r["ls"].at[7 + i]))
    for x in lc:
        x.start()
    c.barrier()

    ss, rs = r["gs"], r["gr"]
    yq = c.mpeer(2)[1]
    x0, z0 = lax.rem(c.dp, 2), lax.rem(c.dp // 2, 2)
    pc = [x0 + 2 * z0, (1 - x0) + 2 * z0, x0 + 2 * (1 - z0)]

    def rows(a, p):
        n = WA[a].shape[1] // 4
        return pl.ds(pl.multiple_of(p * n, n), n)

    yd, sd, xd, zd = c.mpeer(2), c.mpeer(1), c.dpeer(0), c.dpeer(1)
    G = {}
    for a in range(3):
        W = WA[a]
        G[a, "y"] = rcopy(wsrc[a].at[rows(a, pc[0])], W.at[m, rows(a, pc[0])], ss.at[a, 0], rs.at[a, 0], yd)
        G[a, "s"] = rcopy(wsrc[a], W.at[m], ss.at[a, 1], rs.at[a, 1], sd)

        def w(p, half=None):
            at = rows(a, p)
            if half is None:
                return W.at[yq, at]
            return W.at[yq, at, half * (d // 2) : (half + 1) * (d // 2)]

        G[a, "x"] = rcopy(w(pc[0]), w(pc[0]), ss.at[a, 2], rs.at[a, 2], xd)
        G[a, "z"] = rcopy(w(pc[0]), w(pc[0]), ss.at[a, 3], rs.at[a, 3], zd)
        G[a, "dz"] = rcopy(w(pc[1], 0), w(pc[1], 0), ss.at[a, 4], rs.at[a, 4], zd)
        G[a, "dx"] = rcopy(w(pc[2], 1), w(pc[2], 1), ss.at[a, 5], rs.at[a, 5], xd)
        G[a, "t"] = rcopy(W.at[yq], W.at[yq], ss.at[a, 6], rs.at[a, 6], sd)
    for a in range(3):
        G[a, "y"].start()
    for a in range(3):
        G[a, "s"].start()
    V = [rcopy(vec, VA.at[m], r["vs"].at[k - 1], r["vr"].at[k - 1], c.mpeer(k)) for k in (1, 2, 3)]
    for x in V:
        x.start()
    VA[m] = vec[...]

    def g_y(a):
        G[a, "y"].wait_recv()
        G[a, "x"].start()
        G[a, "z"].start()

    def g_xz(a):
        G[a, "x"].wait_recv()
        G[a, "dz"].start()
        G[a, "z"].wait_recv()
        G[a, "dx"].start()

    def g_t(a):
        G[a, "dx"].wait_recv()
        G[a, "dz"].wait_recv()
        G[a, "t"].start()

    for i in range(3):
        lc[i].wait()
        WT[i * hw : (i + 1) * hw, :] = r["W3"][i].T
    bias = vec[...].T[0 : 3 * hw, 7:8]

    sub = lax.broadcasted_iota(jnp.int32, (aug - HD, seq), 0)
    lane = lax.broadcasted_iota(jnp.int32, (aug - HD, seq), 1)
    ones = jnp.where(sub == 0, 1.0, 0.0).astype(BF)
    A = []

    def attend(s):
        t = ta[s]
        lc[3 + s].wait()
        x = TOK[t]
        qkv = (mm(WT[...], x, 1, 1) + bias).astype(BF)
        dead = jnp.where(sub == 0, jnp.where(lane < ln[t], 0.0, -1e30), 0.0).astype(BF)
        for h in range(nh):
            at = slice(h * HD, (h + 1) * HD)
            QT[t, h, 0:HD] = qkv[h * HD : (h + 1) * HD] * jnp.asarray(HD**-0.5, BF)
            QT[t, h, HD:aug] = ones
            KT[t, h, 0:HD] = qkv[hw + h * HD : hw + (h + 1) * HD]
            KT[t, h, HD:aug] = dead
        VT[t] = qkv[2 * hw : 3 * hw]
        for h in range(nh):
            at = slice(h * HD, (h + 1) * HD)
            sc = mm(KT[t, h], QT[t, h], 0, 0)
            e = jnp.exp(sc - jnp.max(sc, axis=0, keepdims=True))
            ri = 1.0 / jnp.sum(e, axis=0, keepdims=True)
            el = e.astype(BF)
            ET[t, h] = el
            RI[t, h : h + 1] = ri
            o = mm(VT[t, at], el, 1, 0) * ri
            ATQ[t, at] = o.astype(BF)
        if s < 3:
            cp = rcopy(ATQ.at[t], ATO.at[m], r["as"].at[s], r["ar"].at[s], c.mpeer((2, 3, 1)[s]))
            cp.start()
            A.append(cp)
        else:
            ATO[m] = ATQ[t]

    attend(0)
    g_y(0)
    attend(1)
    g_xz(0)
    g_y(1)
    attend(2)
    g_t(0)
    g_xz(1)
    attend(3)
    g_y(2)

    f = lambda i: vec[i : i + 1]
    WO = WA[0]
    G[0, "s"].wait_recv()
    lc[7].wait()
    for cp in A:
        cp.wait_recv()
    G[0, "t"].wait_recv()
    mixed = TOK[m].astype(F32) + f(0)
    for q in range(4):
        mixed += mm(ATO[q], WO[q], 0, 0)
    n1, i1 = norm_rows(mixed)
    N1[...] = n1
    I1[...] = i1
    first = n1 * f(1) + f(2)
    FIRST[...] = first
    FL[...] = first.astype(BF)

    for x in V:
        x.wait_recv()
    cw = d // 3

    def ffn(k):
        q = c.mpeer(k)[1]

        def chunk(j, _):
            at = pl.ds(pl.multiple_of(j * cw, 128), cw)
            h = mm(FL[...], WA[1][q, :, at], 1, 0) + VA[q, 6:7, at]
            g, gp = gelu_pair(h)
            ACT[q, :, at] = g.astype(BF)
            GP[q, :, at] = gp.astype(BF)
            return 0

        lax.fori_loop(0, 3, chunk, 0)

    def ffn2(k):
        q = c.mpeer(k)[1]
        y = mm(ACT[q], WA[2][q], 1, 0)
        if k == 0:
            ACC[...] = y
        else:
            ACC[...] += y

    lc[8].wait()
    ffn(0)
    g_t(1)
    lc[9].wait()
    ffn2(0)
    g_xz(2)
    G[1, "s"].wait_recv()
    ffn(1)
    G[2, "s"].wait_recv()
    ffn2(1)
    g_t(2)
    ffn(2)
    ffn2(2)
    G[1, "t"].wait_recv()
    ffn(3)
    G[2, "t"].wait_recv()
    ffn2(3)
    second = FIRST[...] + ACC[...] + f(3)
    n2, i2 = norm_rows(second)
    N2[...] = n2
    I2[...] = i2
    for a in range(3):
        for k in ("y", "s", "x", "z", "dz", "dx", "t"):
            G[a, k].wait_send()
    for x in V + A:
        x.wait_send()
    outs = [n for n in names if n.startswith("o_")]
    cps = [pltpu.make_async_copy(r[n[2:]], r[n], r["os"].at[i]) for i, n in enumerate(outs)]
    for x in cps:
        x.start()
    for x in cps:
        x.wait()


def forward(tok4, lengths, vec, wq, wk, wv, wo, wu, wd, nbits):
    nt, seq, d = tok4.shape
    hw = wq.shape[1]
    ff = wu.shape[1]
    nh = hw // HD
    V = pltpu.VMEM
    S = jax.ShapeDtypeStruct
    DMA = pltpu.SemaphoreType.DMA
    scratch = {
        "TOK": V((nt, seq, d), BF),
        "W3": V((3, d, hw), BF),
        "WT": V((3 * hw, d), BF),
        "QT": V((nt, nh, HD + 16, seq), BF),
        "KT": V((nt, nh, HD + 16, seq), BF),
        "VT": V((nt, hw, seq), BF),
        "ET": V((nt, nh, seq, seq), BF),
        "RI": V((nt, 8, seq), F32),
        "ATQ": V((nt, hw, seq), BF),
        "ATO": V((nt, hw, seq), BF),
        "N1": V((seq, d), F32),
        "I1": V((seq, 1), F32),
        "FIRST": V((seq, d), F32),
        "FL": V((seq, d), BF),
        "ACT": V((nt, seq, ff), BF),
        "GP": V((nt, seq, ff), BF),
        "WOA": V((nt, hw, d), BF),
        "UA": V((nt, d, ff), BF),
        "DA": V((nt, ff, d), BF),
        "VA": V((nt, 8, d), F32),
        "ACC": V((seq, d), F32),
        "N2": V((seq, d), F32),
        "I2": V((seq, 1), F32),
        "ls": DMA((10,)),
        "gs": DMA((3, 7)),
        "gr": DMA((3, 7)),
        "vs": DMA((3,)),
        "vr": DMA((3,)),
        "as": DMA((3,)),
        "ar": DMA((3,)),
        "os": DMA((24,)),
    }
    ins = {"len": lengths, "vec": vec, "tok": tok4, "wq": wq, "wk": wk, "wv": wv, "wo": wo, "wu": wu, "wd": wd}
    specs = [pl.BlockSpec(memory_space=pltpu.SMEM), pl.BlockSpec(memory_space=V)]
    specs += [pl.BlockSpec(memory_space=pl.ANY)] * (len(ins) - 2)
    outs = [
        "QT", "KT", "VT", "ET", "RI", "ATQ", "ATO", "N1", "I1", "FL", "ACT", "GP", "WOA", "UA", "DA", "N2", "I2",
    ]
    names = list(ins) + ["o_" + n for n in outs] + list(scratch)
    res = pl.pallas_call(
        functools.partial(fwd_kernel, nbits, names),
        out_shape=[S(scratch[n].shape, scratch[n].dtype) for n in outs],
        in_specs=specs,
        out_specs=[pl.BlockSpec(memory_space=pl.ANY)] * len(outs),
        scratch_shapes=list(scratch.values()),
        compiler_params=pltpu.CompilerParams(
            collective_id=0, has_side_effects=True, vmem_limit_bytes=60 * 2**20
        ),
    )(*ins.values())
    return dict(zip(outs, res))


def norm_back(up, normed, inv, gain):
    c = up * gain
    return inv * (
        c
        - jnp.mean(c, axis=-1, keepdims=True)
        - normed * jnp.mean(c * normed, axis=-1, keepdims=True)
    )


def shards(
    tokens, lengths, wq, bq, wk, wv, bv, wo, bo, g1, s1, wu, bu, wd, bd, g2, s2, cot
):
    n = lengths.shape[0]
    rows, d = tokens.shape
    seq = rows // n
    hw = wq.shape[1]
    m = lax.axis_index("mp")
    nd = lax.axis_size("dp")
    own = lambda a: lax.dynamic_slice_in_dim(a, m * seq, seq, 0)
    f = lambda a: a.astype(F32)
    zero = jnp.zeros((hw,), F32)
    vec = jnp.stack(
        [f(a) for a in (bo, g1, s1, bd, g2, s2, bu)] + [jnp.concatenate([f(bq), zero, f(bv), zero])]
    )
    tok4 = tokens.reshape(n, seq, d)
    F = forward(tok4, lengths, vec, wq, wk, wv, wo, wu, wd, nd.bit_length() - 1)
    n1, i1, n2, i2, first_low = F["N1"], F["I1"], F["N2"], F["I2"], F["FL"]
    att_own, act, gp = F["ATO"], F["ACT"], F["GP"]
    out_own = (n2 * f(g2) + f(s2)).astype(BF)
    c_own = f(own(cot))
    d2 = norm_back(c_own, n2, i2, f(g2))
    d2l = d2.astype(BF)
    dg2, ds2, dbd = jnp.sum(c_own * n2, 0), jnp.sum(c_own, 0), jnp.sum(d2, 0)
    dwd = jnp.einsum("qtf,td->qfd", act, d2l, preferred_element_type=F32)
    dact = jnp.einsum("td,qfd->qtf", d2l, F["DA"], preferred_element_type=F32)
    dh = (dact * f(gp)).astype(BF)
    dbu = jnp.sum(f(dh), axis=1)
    dwu = jnp.einsum("td,qtf->qdf", first_low, dh, preferred_element_type=F32)
    d1 = d2 + jnp.einsum("qtf,qdf->td", dh, F["UA"], preferred_element_type=F32)
    dg1, ds1 = jnp.sum(d1 * n1, 0), jnp.sum(d1, 0)
    dm = norm_back(d1, n1, i1, f(g1))
    dbo = jnp.sum(dm, 0)
    dml = dm.astype(BF)
    dwo = jnp.einsum("qkt,td->qkd", att_own, dml, preferred_element_type=F32)
    datt = jnp.einsum("td,qkd->qkt", dml, F["WOA"], preferred_element_type=F32).astype(BF)
    datt = lax.all_to_all(datt, "mp", 0, 0)
    hs = (n, hw // HD, HD, seq)
    doh = f(datt).reshape(hs) * F["RI"][:, : hw // HD, None, :]
    dd = jnp.sum(doh * f(F["ATQ"]).reshape(hs), axis=2, keepdims=True)
    dol = doh.astype(BF)
    e = F["ET"]
    q, k, v = F["QT"][:, :, :HD], F["KT"][:, :, :HD], F["VT"].reshape(hs)
    es = functools.partial(jnp.einsum, preferred_element_type=F32)
    dv = es("thkq,thdq->thdk", e, dol)
    dp = es("thdk,thdq->thkq", v, dol)
    ds = (f(e) * (dp - dd)).astype(BF)
    dq = es("thkq,thdk->thdq", ds, k) * HD**-0.5
    dk = es("thkq,thdq->thdk", ds, q)
    dq, dk, dv = (a.reshape(n, hw, seq).astype(BF) for a in (dq, dk, dv))
    dbq, dbv = jnp.sum(f(dq), (0, 2)), jnp.sum(f(dv), (0, 2))
    dwq, dwk, dwv = (es("tsd,tws->dw", tok4, a) for a in (dq, dk, dv))
    back = (es("tws,dw->tsd", dq, wq) + es("tws,dw->tsd", dk, wk) + es("tws,dw->tsd", dv, wv)).astype(BF)
    back = jnp.sum(f(lax.all_to_all(back, "mp", 0, 0)), 0)
    tg_own = (dm + back).astype(BF)
    layer_out = lax.all_gather(out_own, "mp", tiled=True)
    tokens_grad = lax.all_gather(tg_own, "mp", tiled=True)
    low = lambda a: a.astype(BF)
    ffn = lax.psum_scatter(jnp.stack([low(dwu), low(dwd)], 1), "mp", scatter_dimension=0)
    dwo = lax.psum_scatter(low(dwo), "mp", scatter_dimension=0)
    dbu = lax.psum_scatter(dbu, "mp", scatter_dimension=0)
    dwq, dwk, dwv, dwo, ffn = lax.psum((low(dwq), low(dwk), low(dwv), dwo, ffn), "dp")
    dbq, dbv, dbu = lax.psum((dbq, dbv, dbu), "dp")
    dbo, dg1, ds1, dbd, dg2, ds2 = lax.psum((dbo, dg1, ds1, dbd, dg2, ds2), ("dp", "mp"))
    return (
        layer_out, tokens_grad, f(dwq), dbq, f(dwk), f(dwv), dbv, f(dwo), dbo, dg1, ds1,
        f(ffn[0]), dbu, f(ffn[1]), dbd, dg2, ds2,
    )


def solution(mesh):
    row, col, one, rep = P("dp", None), P(None, "mp"), P("mp"), P()
    low = P("mp", None)
    in_specs = (
        row, P("dp"), col, one, col, col, one, low, rep, rep, rep, col, one, low, rep, rep, rep, row,
    )
    out_specs = (
        row, row, col, one, col, col, one, low, rep, rep, rep, col, one, low, rep, rep, rep,
    )
    return jax.shard_map(shards, mesh=mesh, in_specs=in_specs, out_specs=out_specs, check_vma=False)
```

```python
import functools

import jax
import jax.numpy as jnp
from jax import lax
from jax.experimental import pallas as pl
from jax.experimental.pallas import tpu as pltpu
from jax.sharding import PartitionSpec as P

HD = 64
EPS = 1e-06
BF = jnp.bfloat16
F32 = jnp.float32
MESH = pl.DeviceIdType.MESH


def mm(a, b, ca, cb):
    return lax.dot_general(a, b, (((ca,), (cb,)), ((), ())), preferred_element_type=F32)


def flip(v, b):
    return v + b - 2 * b * lax.rem(v // b, 2)


def gelu_pair(h):
    x = h * 0.7071067811865476
    e = jnp.exp(-(x * x))
    t = 1.0 / (1.0 + 0.3275911 * jnp.abs(x))
    poly = t * (
        0.254829592
        + t * (-0.284496736 + t * (1.421413741 + t * (-1.453152027 + t * 1.061405429)))
    )
    tail = 0.5 * poly * e
    phi = jnp.where(h > 0, 1.0 - tail, tail)
    return h * phi, phi + h * e * 0.3989422804014327


def add_rows(dst, src, n):
    step = 48

    def body(i, _):
        at = pl.ds(pl.multiple_of(i * step, 16), step)
        a, b = dst.at[at], src.at[at]
        a[...] = (a[...].astype(F32) + b[...].astype(F32)).astype(BF)
        return 0

    lax.fori_loop(0, n // step, body, 0)


def norm_rows(x):
    center = x - jnp.mean(x, axis=-1, keepdims=True)
    inv = lax.rsqrt(jnp.mean(center * center, axis=-1, keepdims=True) + EPS)
    return center * inv, inv


class Comm:
    def __init__(self, nbits):
        self.dp, self.mp = lax.axis_index("dp"), lax.axis_index("mp")
        self.nbits = nbits

    def mpeer(self, k):
        v = self.mp
        for b in (1, 2):
            if k & b:
                v = flip(v, b)
        return (self.dp, v)

    def dpeer(self, bit):
        return (flip(self.dp, 1 << bit), self.mp)

    def barrier(self):
        bar = pltpu.get_barrier_semaphore()
        peers = [self.mpeer(k) for k in (1, 2, 3)] + [self.dpeer(b) for b in range(self.nbits)]
        for p in peers:
            pl.semaphore_signal(bar, inc=1, device_id=p, device_id_type=MESH)
        pl.semaphore_wait(bar, len(peers))


def rcopy(src, dst, ss, rs, dev):
    return pltpu.make_async_remote_copy(
        src_ref=src, dst_ref=dst, send_sem=ss, recv_sem=rs, device_id=dev, device_id_type=MESH
    )


class Unit:
    def __init__(self, c, view, rows, order, slots, ss, rs, out, loc):
        self.stages = []
        self.sent = []
        y = c.mp // 2
        hs = [0, 1] if "y" in order else [0]
        own = 0
        off, n = 0, rows
        pend = []
        k = 0
        spans = []

        def put(a, b, dev):
            nonlocal k
            cp = rcopy(a, b, ss.at[k], rs.at[k], dev)
            k += 1
            return cp

        steps = []
        for i, ax in enumerate(order):
            if ax == "y":
                cps = [put(view(1 - y, off, n), slots[i].at[0], c.mpeer(2))]
                hs, own = [y], y
                adds = [(view(y, off, n), slots[i].at[0], n)]
            else:
                b = "xz".index(ax)
                bit = lax.rem(c.dp // (1 << b), 2)
                spans.append((b, off, n))
                n //= 2
                mine, theirs = off + bit * n, off + (1 - bit) * n
                cps, adds = [], []
                for j, h in enumerate(hs):
                    cps.append(put(view(h, theirs, n), slots[i].at[j], c.dpeer(b)))
                    adds.append((view(h, mine, n), slots[i].at[j], n))
                off = mine
            steps.append((cps, adds, False))
        for b in range(2, c.nbits):
            sl = slots[len(order) + b - 2]
            steps.append(([put(view(own, off, n), sl.at[0], c.dpeer(b))], [(view(own, off, n), sl.at[0], n)], True))
        (b2, _, _), (b1, o1, _) = spans
        mine = view(own, off, n)
        bit = lax.rem(c.dp // (1 << b1), 2)
        theirs = o1 + (1 - bit) * n
        first = put(mine, out(off, n), c.dpeer(b1))
        second = put(mine, out(off, n), c.dpeer(b2))
        third = put(out(theirs, n), out(theirs, n), c.dpeer(b2))
        self.local = pltpu.make_async_copy(mine, out(off, n), loc)
        steps.append(([first, second], [], False))
        steps.append(([third], [], False))
        self.steps = steps
        self.at = 0
        self.hold = second

    def go(self):
        last = len(self.steps)
        if self.at > 0:
            cps, adds, both = self.steps[self.at - 1]
            for cp in cps:
                if cp is not self.hold:
                    cp.wait_recv()
                if both:
                    cp.wait_send()
                else:
                    self.sent.append(cp)
            for a in adds:
                add_rows(*a)
        if self.at < last:
            for cp in self.steps[self.at][0]:
                cp.start()
            if self.at == last - 2:
                self.local.start()
        else:
            self.hold.wait_recv()
        self.at += 1

    def drain(self):
        for cp in self.sent:
            cp.wait_send()
        self.local.wait()


class Swap:
    def __init__(self, ref, slots, ss, rs, peers):
        self.ref, self.slots = ref, slots
        self.cps = [rcopy(ref, slots.at[i], ss.at[i], rs.at[i], p) for i, p in enumerate(peers)]
        self.at = 0

    def go(self):
        if self.at > 0:
            self.cps[self.at - 1].wait()
            self.ref[...] += self.slots[self.at - 1]
        if self.at < len(self.cps):
            self.cps[self.at].start()
        self.at += 1

    def end(self):
        while self.at <= len(self.cps):
            self.go()


def layer_kernel(nbits, names, *refs):
    r = dict(zip(names, refs))
    ln, vec, tok = r["len"], r["vec"], r["tok"]
    TOK, WT, QT, KT, VT, ET, RI = (r[k] for k in ("TOK", "WT", "QT", "KT", "VT", "ET", "RI"))
    ATQ, ATO, N1, I1, FL, ACT, GP = (r[k] for k in ("ATQ", "ATO", "N1", "I1", "FL", "ACT", "GP"))
    WA = (r["WOA"], r["UA"], r["DA"])
    VA, ACC, COT, SA, SFL, SAT = (r[k] for k in ("VA", "ACC", "COT", "SA", "SFL", "SAT"))
    D2L, SD2, SH, DOT, DTS, SG, BQ = (r[k] for k in ("D2L", "SD2", "SH", "DOT", "DTS", "SG", "BQ"))
    wsrc = (r["wo"], r["wu"], r["wd"])
    c = Comm(nbits)
    m = c.mp
    seq, d = TOK.shape[1], TOK.shape[2]
    hw = VT.shape[1]
    nh = hw // HD
    aug = QT.shape[2]

    lc = []
    for i, k in enumerate(("wq", "wk", "wv")):
        lc.append(pltpu.make_async_copy(r[k], r["W3"].at[i], r["ls"].at[i]))
    ta = [c.mpeer(k)[1] for k in (2, 3, 1, 0)]
    for i in range(4):
        lc.append(pltpu.make_async_copy(tok.at[ta[i]], TOK.at[ta[i]], r["ls"].at[3 + i]))
    for i in range(3):
        lc.append(pltpu.make_async_copy(wsrc[i], WA[i].at[m], r["ls"].at[7 + i]))
    lc.append(pltpu.make_async_copy(r["cot"].at[m], COT, r["ls"].at[10]))
    for x in lc:
        x.start()
    c.barrier()
    cb, yb = lax.rem(m, 2), m // 2
    sd = c.mpeer(1)
    C = [rcopy(ATO.at[1 - cb + 2 * h], SAT.at[h], r["cs"].at[h], r["cr"].at[h], sd) for h in (0, 1)]
    C.append(rcopy(FL, SFL, r["cs"].at[2], r["cr"].at[2], sd))
    for i, h in enumerate((yb, 1 - yb)):
        C.append(rcopy(ACT.at[1 - cb + 2 * h], SA.at[h], r["cs"].at[3 + i], r["cr"].at[3 + i], sd))

    ss, rs = r["gs"], r["gr"]
    yq = c.mpeer(2)[1]
    x0, z0 = lax.rem(c.dp, 2), lax.rem(c.dp // 2, 2)
    pc = [x0 + 2 * z0, (1 - x0) + 2 * z0, x0 + 2 * (1 - z0)]

    def rows(a, p):
        n = WA[a].shape[1] // 4
        return pl.ds(pl.multiple_of(p * n, n), n)

    yd, sd, xd, zd = c.mpeer(2), c.mpeer(1), c.dpeer(0), c.dpeer(1)
    G = {}
    for a in range(3):
        W = WA[a]
        G[a, "y"] = rcopy(wsrc[a].at[rows(a, pc[0])], W.at[m, rows(a, pc[0])], ss.at[a, 0], rs.at[a, 0], yd)
        G[a, "s"] = rcopy(wsrc[a], W.at[m], ss.at[a, 1], rs.at[a, 1], sd)

        def w(p, half=None):
            at = rows(a, p)
            if half is None:
                return W.at[yq, at]
            return W.at[yq, at, half * (d // 2) : (half + 1) * (d // 2)]

        G[a, "x"] = rcopy(w(pc[0]), w(pc[0]), ss.at[a, 2], rs.at[a, 2], xd)
        G[a, "z"] = rcopy(w(pc[0]), w(pc[0]), ss.at[a, 3], rs.at[a, 3], zd)
        G[a, "dz"] = rcopy(w(pc[1], 0), w(pc[1], 0), ss.at[a, 4], rs.at[a, 4], zd)
        G[a, "dx"] = rcopy(w(pc[2], 1), w(pc[2], 1), ss.at[a, 5], rs.at[a, 5], xd)
        G[a, "t"] = rcopy(W.at[yq], W.at[yq], ss.at[a, 6], rs.at[a, 6], sd)
    for a in range(3):
        G[a, "y"].start()
    for a in range(3):
        G[a, "s"].start()
    V = [rcopy(vec, VA.at[m], r["vs"].at[k - 1], r["vr"].at[k - 1], c.mpeer(k)) for k in (1, 2, 3)]
    for x in V:
        x.start()
    VA[m] = vec[...]

    def g_y(a):
        G[a, "y"].wait_recv()
        G[a, "x"].start()
        G[a, "z"].start()

    def g_xz(a):
        G[a, "x"].wait_recv()
        G[a, "dz"].start()
        G[a, "z"].wait_recv()
        G[a, "dx"].start()

    def g_t(a):
        G[a, "dx"].wait_recv()
        G[a, "dz"].wait_recv()
        G[a, "t"].start()

    for i in range(3):
        lc[i].wait()
        WT[i * hw : (i + 1) * hw, :] = r["W3"][i].T
    bias = vec[...].T[0 : 3 * hw, 7:8]

    sub = lax.broadcasted_iota(jnp.int32, (aug - HD, seq), 0)
    lane = lax.broadcasted_iota(jnp.int32, (aug - HD, seq), 1)
    ones = jnp.where(sub == 0, 1.0, 0.0).astype(BF)
    A = []

    def attend(s):
        t = ta[s]
        lc[3 + s].wait()
        x = TOK[t]
        qkv = (mm(WT[...], x, 1, 1) + bias).astype(BF)
        dead = jnp.where(sub == 0, jnp.where(lane < ln[t], 0.0, -1e30), 0.0).astype(BF)
        for h in range(nh):
            at = slice(h * HD, (h + 1) * HD)
            QT[t, h, 0:HD] = qkv[h * HD : (h + 1) * HD] * jnp.asarray(HD**-0.5, BF)
            QT[t, h, HD:aug] = ones
            KT[t, h, 0:HD] = qkv[hw + h * HD : hw + (h + 1) * HD]
            KT[t, h, HD:aug] = dead
        VT[t] = qkv[2 * hw : 3 * hw]
        for h in range(nh):
            at = slice(h * HD, (h + 1) * HD)
            sc = mm(KT[t, h], QT[t, h], 0, 0)
            e = jnp.exp(sc - jnp.max(sc, axis=0, keepdims=True))
            ri = 1.0 / jnp.sum(e, axis=0, keepdims=True)
            el = e.astype(BF)
            ET[t, h] = el
            RI[t, h : h + 1] = ri
            o = mm(VT[t, at], el, 1, 0) * ri
            ATQ[t, at] = o.astype(BF)
        if s < 3:
            cp = rcopy(ATQ.at[t], ATO.at[m], r["as"].at[s], r["ar"].at[s], c.mpeer((2, 3, 1)[s]))
            cp.start()
            A.append(cp)
        else:
            ATO[m] = ATQ[t]

    attend(0)
    g_y(0)
    attend(1)
    g_xz(0)
    g_y(1)
    attend(2)
    g_t(0)
    g_xz(1)
    attend(3)
    g_y(2)

    f = lambda i: vec[i : i + 1]
    WO = WA[0]
    G[0, "s"].wait_recv()
    lc[7].wait()
    for cp in A:
        cp.wait_recv()
    G[0, "t"].wait_recv()
    mixed = TOK[m].astype(F32) + f(0)
    for q in range(4):
        mixed += mm(ATO[q], WO[q], 0, 0)
    ACC[...] = mixed
    C[0].start()
    C[1].start()
    nr = 64

    def norm1(i, _):
        at = pl.ds(pl.multiple_of(i * nr, nr), nr)
        n1, i1 = norm_rows(ACC[at])
        N1[at] = n1
        I1[at] = i1
        FL[at] = (n1 * f(1) + f(2)).astype(BF)
        return 0

    lax.fori_loop(0, seq // nr, norm1, 0)
    C[2].start()

    for x in V:
        x.wait_recv()
    cw = d // 3

    def ffn(k):
        q = c.mpeer(k)[1]

        def chunk(j, _):
            at = pl.ds(pl.multiple_of(j * cw, 128), cw)
            h = mm(FL[...], WA[1][q, :, at], 1, 0) + VA[q, 6:7, at]
            g, gp = gelu_pair(h)
            ACT[q, :, at] = g.astype(BF)
            GP[q, :, at] = gp.astype(BF)
            return 0

        lax.fori_loop(0, 3, chunk, 0)

    def ffn2(k):
        q = c.mpeer(k)[1]
        y = mm(ACT[q], WA[2][q], 1, 0)
        if k == 0:
            ACC[...] = y
        else:
            ACC[...] += y

    lc[8].wait()
    ffn(0)
    g_t(1)
    lc[9].wait()
    ffn2(0)
    g_xz(2)
    G[1, "s"].wait_recv()
    ffn(1)
    C[3].start()
    G[2, "s"].wait_recv()
    ffn2(1)
    g_t(2)
    ffn(2)
    ffn2(2)
    G[1, "t"].wait_recv()
    ffn(3)
    C[4].start()
    G[2, "t"].wait_recv()
    ffn2(3)
    lc[10].wait()

    def fold(x):
        return jnp.sum(x.reshape(x.shape[0] // 8, 8, x.shape[1]), axis=0)

    zero = jnp.zeros((8, d), F32)

    def norm2(i, sums):
        at = pl.ds(pl.multiple_of(i * nr, nr), nr)
        n2, i2 = norm_rows(N1[at] * f(1) + f(2) + ACC[at] + f(3))
        ct = COT[at].astype(F32)
        COT[at] = (n2 * f(4) + f(5)).astype(BF)
        cg = ct * f(4)
        cn = ct * n2
        d2 = i2 * (
            cg
            - jnp.mean(cg, axis=-1, keepdims=True)
            - n2 * jnp.mean(cg * n2, axis=-1, keepdims=True)
        )
        ACC[at] = d2
        D2L[at] = d2.astype(BF)
        return sums[0] + fold(d2), sums[1] + fold(cn), sums[2] + fold(ct)

    sums = lax.fori_loop(0, seq // nr, norm2, (zero,) * 3)
    SG[...] = jnp.zeros(SG.shape, F32)
    for i in range(3):
        SG[3 + i : 4 + i] = jnp.sum(sums[i], axis=0, keepdims=True)
    yd = c.mpeer(2)
    bs, br = r["bs"], r["br"]
    E = [rcopy(D2L, SD2, bs.at[0], br.at[0], sd)]
    E[0].start()
    LO, TG, LOB = r["o_LO"], r["o_TG"], COT

    def spread(OUT, base):
        loc = pltpu.make_async_copy(LOB, OUT.at[m], r["os"].at[base // 3])
        y = rcopy(LOB, OUT.at[m], r["ps"].at[base], r["pr"].at[base], yd)
        s = rcopy(LOB, OUT.at[m], r["ps"].at[base + 1], r["pr"].at[base + 1], sd)
        t = rcopy(OUT.at[yq], OUT.at[yq], r["ps"].at[base + 2], r["pr"].at[base + 2], sd)
        y.start()
        s.start()
        loc.start()
        return loc, y, s, t

    L = spread(LO, 0)

    def d_hidden(k):
        q = c.mpeer(k)[1]

        def chunk(j, _):
            at = pl.ds(pl.multiple_of(j * cw, 128), cw)
            dh = (mm(D2L[...], DA[q, at, :], 1, 1) * GP[q, :, at].astype(F32)).astype(BF)
            GP[q, :, at] = dh
            SG[pl.ds(8 + q, 1), at] = jnp.sum(dh.astype(F32), axis=0, keepdims=True)
            return 0

        lax.fori_loop(0, 3, chunk, 0)
        if k in (1, 3):
            h = yb if k == 1 else 1 - yb
            cp = rcopy(GP.at[q], SH.at[h], bs.at[1 + k // 2], br.at[1 + k // 2], sd)
            cp.start()
            E.append(cp)

    UA, DA = WA[1], WA[2]
    GD, GU, GO = r["GD"], r["GU"], r["GO"]
    half = d // 2

    def weight_grad(G, left, right, sleft, sright, i):
        at = slice(i * half, (i + 1) * half)

        def body(h, _):
            q = cb + 2 * h
            G[h, at] = (left(q, h, at, right) + sleft(q, h, at, sright)).astype(BF)
            return 0

        lax.fori_loop(0, 2, body, 0)

    def view(G, base):
        def at(h, off, n):
            if isinstance(off, int):
                return G.at[h, base + off : base + off + n]
            return G.at[h, pl.ds(pl.multiple_of(base + off, 16), n)]

        return at

    us, ur = r["us"], r["ur"]
    nex = nbits - 2

    def rows_of(O, base):
        def at(off, n):
            return O.at[pl.ds(pl.multiple_of(base + off, 16), n)]

        return at

    def unit(j, G, base, rows, order, slots, out, at):
        return Unit(
            c, view(G, base), rows, order, slots, us.at[j], ur.at[j], rows_of(out, at), r["os"].at[2 + j]
        )

    def ffn_slots(j, order):
        n = half
        h = 2
        res = []
        for i, ax in enumerate(order):
            if ax == "y":
                h = 1
            else:
                n //= 2
            res.append(r["R%d%d" % (j, i)])
        return res + [r["X%d" % j].at[e] for e in range(nex)]

    orders = ORDERS
    d_hidden(1)
    E[0].wait_recv()
    C[3].wait_recv()
    C[4].wait_recv()
    U = []
    for i in range(2):
        weight_grad(
            GD,
            lambda q, h, at, _: mm(ACT[q, :, at], D2L[...], 0, 0), None,
            lambda q, h, at, _: mm(SA[h, :, at], SD2[...], 0, 0), None, i,
        )
        U.append(unit(i, GD, i * half, half, orders[i], ffn_slots(i, orders[i]), r["o_OD"], i * half))
        U[-1].go()
    d_hidden(3)
    d_hidden(0)
    d_hidden(2)
    for x in E[1:]:
        x.wait_recv()
    C[2].wait_recv()
    for i in range(2):
        weight_grad(
            GU,
            lambda q, h, at, _: mm(FL[:, at], GP[q], 0, 0), None,
            lambda q, h, at, _: mm(SFL[:, at], SH[h], 0, 0), None, i,
        )
        U.append(unit(2 + i, GU, i * half, half, orders[2 + i], ffn_slots(2 + i, orders[2 + i]), r["o_OU"], i * half))
        U[-1].go()

    def d_first(q, _):
        ACC[...] += mm(GP[q], UA[q], 1, 1)
        return 0

    lax.fori_loop(0, 4, d_first, 0)
    for x in E + C[3:5]:
        x.wait_send()
    for a in range(3):
        for k in ("y", "s", "x", "z", "dz", "dx", "t"):
            G[a, k].wait_send()
    DML = D2L

    def norm1_back(i, sums):
        at = pl.ds(pl.multiple_of(i * nr, nr), nr)
        d1, n1 = ACC[at], N1[at]
        cg = d1 * f(1)
        dm = I1[at] * (
            cg
            - jnp.mean(cg, axis=-1, keepdims=True)
            - n1 * jnp.mean(cg * n1, axis=-1, keepdims=True)
        )
        ACC[at] = dm
        DML[at] = dm.astype(BF)
        return sums[0] + fold(dm), sums[1] + fold(d1 * n1), sums[2] + fold(d1)

    sums = lax.fori_loop(0, seq // nr, norm1_back, (zero,) * 3)
    for i in range(3):
        SG[i : 1 + i] = jnp.sum(sums[i], axis=0, keepdims=True)
    M = rcopy(DML, SD2, bs.at[3], br.at[3], sd)
    M.start()
    dps = [c.dpeer(b) for b in range(nbits)]
    S = Swap(SG, r["SGR"], r["ws"], r["wr"], [sd, yd] + dps)
    S.go()
    H = {}
    for k in (2, 3, 1, 0):
        q = c.mpeer(k)[1]
        g = mm(WO[q], DML[...], 1, 1).astype(BF)
        if k == 0:
            DOT[m] = g
        else:
            DTS[q] = g
            H[k] = rcopy(DTS.at[q], DOT.at[m], r["hs"].at[k - 1], r["hr"].at[k - 1], c.mpeer(k))
            H[k].start()
    M.wait_recv()
    C[0].wait_recv()
    C[1].wait_recv()
    for h in (0, 1):
        q = cb + 2 * h
        GO[h] = (mm(ATO[q], DML[...], 1, 0) + mm(SAT[h], SD2[...], 1, 0)).astype(BF)
    oslots = [r["R40"], r["R41"], r["R42"]] + [r["X4"].at[e] for e in range(nex)]
    U.append(unit(4, GO, 0, hw, ("x", "z", "y"), oslots, r["o_OO"], 0))
    U[4].go()

    BQ[...] = jnp.zeros(BQ.shape, F32)
    eight = jnp.ones((8, seq), BF)
    XS = {}

    def attend_back(k):
        t = c.mpeer(k)[1]
        if k:
            H[k].wait_recv()

        def head(h, _):
            at = pl.ds(pl.multiple_of(h * HD, HD), HD)
            g = DOT[t, at].astype(F32) * RI[t, pl.ds(h, 1)]
            dd = jnp.sum(g * ATQ[t, at].astype(F32), axis=0, keepdims=True)
            gl = g.astype(BF)
            e = ET[t, h]
            ds = (e.astype(F32) * (mm(VT[t, at], gl, 0, 0) - dd)).astype(BF)
            dq = mm(KT[t, h, 0:HD], ds, 1, 0) * HD**-0.5
            dk = mm(QT[t, h, 0:HD], ds, 1, 1)
            dv = mm(gl, e, 1, 1)
            for i, x in enumerate((dq, dk, dv)):
                DA[t, pl.ds(pl.multiple_of(i * hw + h * HD, HD), HD), 0:seq] = x.astype(BF)
            return 0

        lax.fori_loop(0, nh, head, 0)
        g = DA[t, 0 : 3 * hw, 0:seq]
        BQ[:, 0 : 3 * hw] += mm(eight, g, 1, 1)
        dx = mm(g, WT[...], 0, 0)
        if k == 0:
            ACC[...] += dx
        elif k == 2:
            XS[3].wait_recv()
            ACT[t] = (dx + UA[0, 0:seq].astype(F32)).astype(BF)
        else:
            ACT[t] = dx.astype(BF)
        if k:
            dst = UA.at[{3: 0, 2: 1, 1: 2}[k], 0:seq]
            XS[k] = rcopy(ACT.at[t], dst, r["xs"].at[k - 1], r["xr"].at[k - 1], yd if k == 2 else sd)
            XS[k].start()

    attend_back(0)
    U[0].go()
    U[1].go()
    S.go()
    attend_back(3)
    U[4].go()
    U[1].go()
    U[0].go()
    S.go()
    attend_back(2)
    U[4].go()
    U[2].go()
    U[3].go()
    S.go()
    attend_back(1)
    S.go()

    def qkv_grad(i, _):
        at = pl.ds(pl.multiple_of(i * hw, 16), hw)
        g = mm(DA[0, at, 0:seq], TOK[0], 1, 0)
        for t in range(1, 4):
            g += mm(DA[t, at, 0:seq], TOK[t], 1, 0)
        UA[3, at] = g.astype(BF)
        return 0

    lax.fori_loop(0, 3, qkv_grad, 0)
    n3 = 3 * hw
    qslots = [GP.at[0:1, 0 : n3 // 2], GP.at[1:2, 0 : n3 // 4]]
    qslots += [GP.at[2:3, e * (n3 // 4) : (e + 1) * (n3 // 4)] for e in range(min(nex, 3))]
    qslots += [GP.at[3:4, e * (n3 // 4) : (e + 1) * (n3 // 4)] for e in range(max(nex - 3, 0))]
    U[4].go()
    Q = Unit(
        c, lambda h, off, n: view(UA, 0)(3, off, n), n3, ("x", "z"), qslots, us.at[5], ur.at[5],
        rows_of(r["o_OQ"], 0), r["os"].at[7],
    )
    Q.go()
    B = Swap(BQ, r["BQR"], r["zs"], r["zr"], dps)
    B.go()
    L[1].wait_recv()
    L[3].start()
    for x in L[:3]:
        (x.wait if x is L[0] else x.wait_send)()
    XS[1].wait_recv()
    XS[2].wait_recv()

    def finish(i, _):
        at = pl.ds(pl.multiple_of(i * nr, nr), nr)
        LOB[at] = (ACC[at] + UA[1, at].astype(F32) + UA[2, at].astype(F32)).astype(BF)
        return 0

    lax.fori_loop(0, seq // nr, finish, 0)
    T = spread(TG, 3)
    U.append(Q)
    live = True
    while live:
        live = False
        for u in U + [S, B]:
            n = len(u.steps) if isinstance(u, Unit) else len(u.cps)
            if u.at <= n:
                u.go()
                live = True
    r["o_OS"][...] = SG[...]
    r["o_OB"][...] = BQ[...]
    T[1].wait_recv()
    T[3].start()
    T[0].wait()
    for x in (T[1], T[2], T[3], L[3]):
        x.wait_send()
    for x in (T[2], T[3], L[2], L[3]):
        x.wait_recv()
    for x in V + A + C[:3] + [M] + list(H.values()) + list(XS.values()):
        x.wait_send()
    for u in U:
        u.drain()


ORDERS = (("z", "x", "y"), ("x", "y", "z"), ("z", "x", "y"), ("x", "y", "z"))


def layer(tok4, cot4, lengths, vec, wq, wk, wv, wo, wu, wd, nbits):
    nt, seq, d = tok4.shape
    hw = wq.shape[1]
    ff = wu.shape[1]
    nh = hw // HD
    V = pltpu.VMEM
    S = jax.ShapeDtypeStruct
    DMA = pltpu.SemaphoreType.DMA
    nex = nbits - 2
    scratch = {
        "TOK": V((nt, seq, d), BF),
        "W3": V((3, d, hw), BF),
        "WT": V((3 * hw, d), BF),
        "QT": V((nt, nh, HD + 16, seq), BF),
        "KT": V((nt, nh, HD + 16, seq), BF),
        "VT": V((nt, hw, seq), BF),
        "ET": V((nt, nh, seq, seq), BF),
        "RI": V((nt, 8, seq), F32),
        "ATQ": V((nt, hw, seq), BF),
        "ATO": V((nt, hw, seq), BF),
        "N1": V((seq, d), F32),
        "I1": V((seq, 1), F32),
        "FL": V((seq, d), BF),
        "ACT": V((nt, seq, ff), BF),
        "GP": V((nt, seq, ff), BF),
        "WOA": V((nt, hw, d), BF),
        "UA": V((nt, d, ff), BF),
        "DA": V((nt, ff, d), BF),
        "VA": V((nt, 8, d), F32),
        "ACC": V((seq, d), F32),
        "COT": V((seq, d), BF),
        "SA": V((2, seq, ff), BF),
        "SH": V((2, seq, ff), BF),
        "SFL": V((seq, d), BF),
        "SD2": V((seq, d), BF),
        "D2L": V((seq, d), BF),
        "SAT": V((2, hw, seq), BF),
        "DOT": V((nt, hw, seq), BF),
        "DTS": V((nt, hw, seq), BF),
        "SG": V((16, d), F32),
        "SGR": V((nbits + 2, 16, d), F32),
        "BQ": V((8, d), F32),
        "BQR": V((nbits, 8, d), F32),
        "GD": V((2, ff, d), BF),
        "GU": V((2, d, ff), BF),
        "GO": V((2, hw, d), BF),
        "ls": DMA((11,)),
        "gs": DMA((3, 7)),
        "gr": DMA((3, 7)),
        "vs": DMA((3,)),
        "vr": DMA((3,)),
        "as": DMA((3,)),
        "ar": DMA((3,)),
        "cs": DMA((5,)),
        "cr": DMA((5,)),
        "bs": DMA((4,)),
        "br": DMA((4,)),
        "ps": DMA((6,)),
        "pr": DMA((6,)),
        "us": DMA((6, 8 + nex)),
        "ur": DMA((6, 8 + nex)),
        "hs": DMA((3,)),
        "hr": DMA((3,)),
        "xs": DMA((3,)),
        "xr": DMA((3,)),
        "ws": DMA((nbits + 2,)),
        "wr": DMA((nbits + 2,)),
        "zs": DMA((nbits,)),
        "zr": DMA((nbits,)),
        "os": DMA((8,)),
    }
    for j, (rows, order) in enumerate([(ff // 2, o) for o in ORDERS] + [(hw, ("x", "z", "y"))]):
        n, h = rows, 2
        for i, ax in enumerate(order):
            if ax == "y":
                h = 1
            else:
                n //= 2
            scratch["R%d%d" % (j, i)] = V((h, n, d), BF)
        scratch["X%d" % j] = V((max(nex, 1), 1, n, d), BF)
    ins = {
        "len": lengths, "vec": vec, "tok": tok4, "cot": cot4,
        "wq": wq, "wk": wk, "wv": wv, "wo": wo, "wu": wu, "wd": wd,
    }
    A = pl.BlockSpec(memory_space=pl.ANY)
    B = pl.BlockSpec(memory_space=V)
    specs = [pl.BlockSpec(memory_space=pltpu.SMEM), B] + [A] * (len(ins) - 2)
    outs = {
        "LO": (S((nt, seq, d), BF), A),
        "TG": (S((nt, seq, d), BF), A),
        "OU": (S((d, ff), BF), A),
        "OD": (S((ff, d), BF), A),
        "OO": (S((hw, d), BF), A),
        "OQ": (S((3 * hw, d), BF), A),
        "OS": (S((16, d), F32), B),
        "OB": (S((8, d), F32), B),
    }
    names = list(ins) + ["o_" + n for n in outs] + list(scratch)

    def kernel(*refs):
        layer_kernel(nbits, names, *refs)

    res = pl.pallas_call(
        kernel,
        out_shape=[o[0] for o in outs.values()],
        in_specs=specs,
        out_specs=[o[1] for o in outs.values()],
        scratch_shapes=list(scratch.values()),
        compiler_params=pltpu.CompilerParams(
            collective_id=0, has_side_effects=True, vmem_limit_bytes=60 * 2**20
        ),
    )(*ins.values())
    return dict(zip(outs, res))


def shards(
    tokens, lengths, wq, bq, wk, wv, bv, wo, bo, g1, s1, wu, bu, wd, bd, g2, s2, cot
):
    n = lengths.shape[0]
    rows, d = tokens.shape
    seq = rows // n
    hw = wq.shape[1]
    m = lax.axis_index("mp")
    nbits = lax.axis_size("dp").bit_length() - 1
    f = lambda a: a.astype(F32)
    zero = jnp.zeros((hw,), F32)
    vec = jnp.stack(
        [f(a) for a in (bo, g1, s1, bd, g2, s2, bu)] + [jnp.concatenate([f(bq), zero, f(bv), zero])]
    )
    o = layer(
        tokens.reshape(n, seq, d), cot.reshape(n, seq, d), lengths, vec, wq, wk, wv, wo, wu, wd, nbits
    )
    q, sg, b = f(o["OQ"]), o["OS"], o["OB"][0]
    dbu = lax.dynamic_index_in_dim(sg, 8 + m, 0, False)
    return (
        o["LO"].reshape(rows, d), o["TG"].reshape(rows, d),
        q[:hw].T, b[:hw], q[hw : 2 * hw].T, q[2 * hw :].T, b[2 * hw : 3 * hw],
        f(o["OO"]), sg[0], sg[1], sg[2], f(o["OU"]), dbu, f(o["OD"]), sg[3], sg[4], sg[5],
    )


def solution(mesh):
    row, col, one, rep = P("dp", None), P(None, "mp"), P("mp"), P()
    low = P("mp", None)
    in_specs = (
        row, P("dp"), col, one, col, col, one, low, rep, rep, rep, col, one, low, rep, rep, rep, row,
    )
    out_specs = (
        row, row, col, one, col, col, one, low, rep, rep, rep, col, one, low, rep, rep, rep,
    )
    return jax.shard_map(shards, mesh=mesh, in_specs=in_specs, out_specs=out_specs, check_vma=False)
```

```python
import jax
import jax.numpy as jnp
from jax import lax
from jax.experimental import pallas as pl
from jax.experimental.pallas import tpu as pltpu
from jax.sharding import PartitionSpec as P

HD = 64
EPS = 1e-06
BF = jnp.bfloat16
F32 = jnp.float32
MESH = pl.DeviceIdType.MESH


DOWN = ("xyz", "zxy", "xzy")
UP = ("zyx", "zyx", "xyz", "zyx")
OUT = "xzy"
QKV = "xz"
GATHER = ((0, 1), (1, 2), (2, 2))


class Step:
    def __init__(self, lead, join):
        self.lead, self.join = lead, join

    def __getattr__(self, name):
        return lambda *at: self.lead + name + "".join(self.join + str(a) for a in at)


step, send, end = Step("", "."), Step(">", "."), Step("", "/")
SCHEDULE = (
    step.start(), send.gy0(), send.gs0(), send.gy1(), send.gs1(), send.gs2(), step.qkv(0),
    step.head(0, 0), step.head(0, 1), step.head(0, 2), send.gy2(), step.qkv(1), step.head(1, 0),
    step.head(1, 1), step.gy(0), send.gx0(), send.gz0(), send.gy3(), step.head(1, 2), step.qkv(2),
    step.head(2, 0), step.head(2, 1), step.gy(1), send.gx1(), send.gz1(), step.head(2, 2),
    send.at1(), send.at2(), step.gx(0), send.gdz0(), step.gz(0), send.gdx0(), step.qkv(3),
    step.head(3, 0), send.gy4(), step.gy(2), send.gx2(), send.gz2(), step.head(3, 1),
    step.head(3, 2), step.gy(3), send.gx3(), send.gz3(), step.gt(0), send.gt0(), step.gx(1),
    step.gz(1), send.at0(), send.gdx1(), send.gdz1(), step.gx(2), send.gdz2(), step.gz(2),
    send.gdx2(), step.gy(4), send.gx4(), send.gz4(), step.gx(3), step.gz(3), step.gt(1),
    send.gt1(), send.gdz3(), send.gdx3(), step.proj(), step.norm1(), step.gt(2), send.gt2(),
    step.ffn(0, 0), step.ffn(0, 1), step.ffn(0, 2), step.down(0), step.ffn(1, 0), step.gt(3),
    send.gt3(), step.gx(4), send.gdz4(), step.gz(4), send.gdx4(), step.ffn(1, 1), step.ffn(1, 2),
    send.sa1(), step.down(1), step.ffn(2, 0), step.ffn(2, 1), step.ffn(2, 2), step.gt(4),
    send.gt4(), step.down(2), step.ffn(3, 0), step.ffn(3, 1), step.ffn(3, 2), send.sa3(),
    step.down(3), step.norm2(), send.lo(), send.d2(), send.los(), step.dh(1), send.sh1(),
    step.gd(0), send.GD0(0, 1), send.GD0(0, 0), step.gd(1), send.GD1(0, 0), send.GD1(0, 1),
    step.gd(2), step.dh(3), send.sh3(), step.dh(0), step.dh(2), step.gu(0), step.gu(1),
    send.GD2(0, 0), send.GD2(0, 1), step.gu(2), step.gu(3), send.GU0(0, 0), send.GU0(0, 1),
    step.d1(0), end.GD0(1), send.GD0(1, 0), step.d1(1), step.d1(2), end.GD1(1), step.d1(3),
    step.lo_fwd(), send.lof(), step.norm1b(), send.dm(), step.datt(1), send.h1(), step.datt(2),
    send.h2(), step.datt(3), send.h3(), step.datt(0), send.S(0), send.GU3(0, 0), send.GD1(1, 1),
    send.GU2(0, 0), send.GU3(0, 1), end.S(1), end.GD0(2), step.go(), step.ab(0, 0), end.GU0(1),
    end.GD2(1), step.ab(0, 1), send.GU2(0, 1), step.ab(0, 2), step.dx(0), send.GD0(2, 0),
    send.GO(0, 1), send.xc0(), send.GD2(1, 0), step.ab(1, 0), send.S(1), send.GU0(1, 0),
    step.ab(1, 1), end.GU3(1), step.ab(1, 2), send.GO(0, 0), send.GU3(1, 0), step.across(0),
    send.GD2(1, 1), step.dx(1), send.xc1(), send.GU1(0, 0), step.ab(2, 0), send.GD1(1, 0),
    end.GU2(1), end.S(2), end.GD0(3), step.ab(2, 1), send.GU2(1, 0), send.GD0(3, 0),
    step.across(1), step.ab(2, 2), step.dx(2), send.xy1(), send.S(2), send.xc2(), end.GU0(2),
    send.GU0(2, 0), end.GD2(2), step.ab(3, 0), send.GU1(0, 1), step.ab(3, 1), end.GO(1),
    send.GO(1, 1), end.GD1(2), step.across(2), end.GU3(2), send.GU3(2, 0), step.ab(3, 2),
    send.GD2(2, 0), end.S(3), step.dx(3), send.xc3(), end.GU0(3), end.GD0(4), send.GD0(4, 1),
    step.gq(0), send.GU0(3, 0), send.S(3), end.GU2(2), step.gq(1), step.gq(2), send.GQ(0, 0),
    send.B(0), step.across(3), end.GU3(3), send.xy3(), send.GU2(2, 0), end.GU1(1), send.GD0(4, 0),
    end.GD2(3), end.S(4), end.B(1), send.S(4), end.GU0(4), send.GU0(4, 0), send.GU0(4, 1),
    send.B(1), end.GU2(3), send.GU2(3, 0), send.GD1(2, 0), end.GD0(5), send.GD0(5, 0),
    send.GO(1, 0), end.S(5), end.B(2), send.B(2), end.GU0(5), send.GU0(5, 0), send.xy0(),
    send.GU3(3, 0), end.GU2(4), send.GU2(4, 1), send.GU2(4, 0), end.GD1(3), end.GO(2), end.B(3),
    end.GD0(6), send.GD1(3, 0), end.GQ(1), end.GU0(6), send.GO(2, 0), send.GQ(1, 0), end.GU3(4),
    send.GU3(4, 0), send.GD2(3, 0), step.settle(1), send.xt1(), end.GU2(5), send.GU2(5, 0),
    step.settle(3), send.xt3(), send.GU1(1, 0), end.GU3(5), end.GD1(4), send.GD1(4, 0), end.GO(3),
    send.GO(3, 0), end.GU2(6), send.GU3(4, 1), send.GU3(5, 0), end.GD2(4), send.GD2(4, 1),
    send.xy2(), end.GD1(5), end.GQ(2), end.GU1(2), send.GU1(2, 0), send.GQ(2, 0), send.GD1(5, 0),
    end.GO(4), send.GO(4, 1), end.GU3(6), send.GO(4, 0), end.GU1(3), send.GD2(4, 0),
    step.settle(0), send.xt0(), step.settle(2), send.xt2(), send.GU1(3, 0), end.GO(5),
    send.GO(5, 0), send.GD1(4, 1), end.GQ(3), send.GQ(3, 0), send.GQ(3, 1), end.GD2(5),
    send.GD2(5, 0), end.GO(6), end.GU1(4), send.GU1(4, 1), end.GD1(6), send.GU1(4, 0), end.GD2(6),
    end.GQ(4), send.GQ(4, 0), end.GU1(5), send.GU1(5, 0), end.GU1(6), end.GQ(5),
)


def mm(a, b, ca, cb):
    return lax.dot_general(a, b, (((ca,), (cb,)), ((), ())), preferred_element_type=F32)


def flip(v, b):
    return v + b - 2 * b * lax.rem(v // b, 2)


def gelu_pair(h):
    x = h * 0.7071067811865476
    e = jnp.exp(-(x * x))
    t = 1.0 / (1.0 + 0.3275911 * jnp.abs(x))
    poly = t * (
        0.254829592
        + t * (-0.284496736 + t * (1.421413741 + t * (-1.453152027 + t * 1.061405429)))
    )
    tail = 0.5 * poly * e
    phi = jnp.where(h > 0, 1.0 - tail, tail)
    return h * phi, phi + h * e * 0.3989422804014327


def add_rows(dst, src, n):
    step = 48 if n % 48 == 0 else 64

    def body(i, _):
        at = pl.ds(pl.multiple_of(i * step, 16), step)
        a, b = dst.at[at], src.at[at]
        a[...] = (a[...].astype(F32) + b[...].astype(F32)).astype(BF)
        return 0

    lax.fori_loop(0, n // step, body, 0)


def norm_rows(x):
    center = x - jnp.mean(x, axis=-1, keepdims=True)
    inv = lax.rsqrt(jnp.mean(center * center, axis=-1, keepdims=True) + EPS)
    return center * inv, inv


class Comm:
    def __init__(self, nbits):
        self.dp, self.mp = lax.axis_index("dp"), lax.axis_index("mp")
        self.nbits = nbits

    def mpeer(self, k):
        v = self.mp
        for b in (1, 2):
            if k & b:
                v = flip(v, b)
        return (self.dp, v)

    def dpeer(self, bit):
        return (flip(self.dp, 1 << bit), self.mp)

    def barrier(self):
        bar = pltpu.get_barrier_semaphore()
        peers = [self.mpeer(k) for k in (1, 2, 3)] + [self.dpeer(b) for b in range(self.nbits)]
        for p in peers:
            pl.semaphore_signal(bar, inc=1, device_id=p, device_id_type=MESH)
        pl.semaphore_wait(bar, len(peers))


def rcopy(src, dst, ss, rs, dev):
    return pltpu.make_async_remote_copy(
        src_ref=src, dst_ref=dst, send_sem=ss, recv_sem=rs, device_id=dev, device_id_type=MESH
    )


class Unit:
    def __init__(self, c, view, rows, order, slots, ss, rs, out, loc):
        y = c.mp // 2
        hs, own = ([0, 1], 0) if "y" in order else ([0], 0)
        off, n, k = 0, rows, 0
        spans = []

        def put(a, b, dev):
            nonlocal k
            cp = rcopy(a, b, ss.at[k], rs.at[k], dev)
            k += 1
            return cp

        self.steps = steps = []
        for i, ax in enumerate(order):
            if ax == "y":
                cps = [put(view(1 - y, off, n), slots[i].at[0], c.mpeer(2))]
                hs, own = [y], y
                adds = [(view(y, off, n), slots[i].at[0], n)]
            else:
                b = "xz".index(ax)
                bit = lax.rem(c.dp // (1 << b), 2)
                spans.append((b, off, n))
                n //= 2
                mine, theirs = off + bit * n, off + (1 - bit) * n
                cps, adds = [], []
                for j, h in enumerate(hs):
                    cps.append(put(view(h, theirs, n), slots[i].at[j], c.dpeer(b)))
                    adds.append((view(h, mine, n), slots[i].at[j], n))
                off = mine
            steps.append((cps, adds))
        mine = view(own, off, n)
        self.swaps = []
        for b in range(2, c.nbits):
            sl = slots[len(order) + b - 2].at[0]
            self.swaps.append((put(mine, sl, c.dpeer(b)), (mine, sl, n)))
        steps.append(([self.swaps[0][0]] if self.swaps else [], []))
        (b2, _, _), (b1, o1, _) = spans
        bit = lax.rem(c.dp // (1 << b1), 2)
        theirs = o1 + (1 - bit) * n
        self.local = pltpu.make_async_copy(mine, out(off, n), loc)
        first = put(mine, out(off, n), c.dpeer(b1))
        self.hold = put(mine, out(off, n), c.dpeer(b2))
        third = put(out(theirs, n), out(theirs, n), c.dpeer(b2))
        steps.append(([first, self.hold], []))
        steps.append(([third], []))

    def send(self, i, j):
        cps = self.steps[i][0]
        if j < len(cps):
            cps[j].start()

    def finish(self, i):
        cps, adds = self.steps[i]
        last = len(self.steps)
        if i == last - 3:
            for e, (cp, add) in enumerate(self.swaps):
                if e:
                    cp.start()
                cp.wait()
                add_rows(*add)
            self.local.start()
            return
        for cp in cps:
            if cp is not self.hold:
                cp.wait_recv()
        for a in adds:
            add_rows(*a)
        if i == last - 1:
            self.hold.wait_recv()

    def drain(self):
        for i, (cps, _) in enumerate(self.steps):
            if i != len(self.steps) - 3:
                for cp in cps:
                    cp.wait_send()
        self.local.wait()


class Swap:
    def __init__(self, ref, slots, ss, rs, peers, count):
        self.ref, self.slots, self.count = ref, slots, count
        self.cps = [rcopy(ref, slots.at[i], ss.at[i], rs.at[i], p) for i, p in enumerate(peers)]

    def send(self, i):
        self.cps[i].start()

    def finish(self, i):
        self.cps[i].wait()
        self.ref[...] += self.slots[i]
        if i == self.count - 1:
            for e in range(self.count, len(self.cps)):
                self.cps[e].start()
                self.cps[e].wait()
                self.ref[...] += self.slots[e]


def layer_kernel(nbits, names, *refs):
    r = dict(zip(names, refs))
    ln, vec, tok = r["len"], r["VEC"], r["tok"]
    TOK, WT, QT, KT, VT, ET, RI = (r[k] for k in ("TOK", "WT", "QT", "KT", "VT", "ET", "RI"))
    ATQ, ATO, N1, I1, FL, ACT, GP = (r[k] for k in ("ATQ", "ATO", "N1", "I1", "FL", "ACT", "GP"))
    VA, ACC, COT, SA, SFL, SAT = (r[k] for k in ("VA", "ACC", "COT", "SA", "SFL", "SAT"))
    D2L, SD2, SH, DOT, DTS, SG, BQ = (r[k] for k in ("D2L", "SD2", "SH", "DOT", "DTS", "SG", "BQ"))
    GD, GU, GO, GQ, LO, TG = (r[k] for k in ("GD", "GU", "GO", "GQ", "o_LO", "o_TG"))
    WA = WO, UA, DA = (r["WOA"], r["UA"], r["DA"])
    DML, LOB = D2L, COT
    wsrc = (r["wo"], r["wu"], r["wd"])
    c = Comm(nbits)
    m = c.mp
    cb, yb = lax.rem(m, 2), m // 2
    seq, d = TOK.shape[1], TOK.shape[2]
    hw = VT.shape[1]
    nh = hw // HD
    aug = QT.shape[2]
    hf = seq // 2
    cw = d // 3
    nr = 64
    yd, sd, xd, zd = c.mpeer(2), c.mpeer(1), c.dpeer(0), c.dpeer(1)
    qk = [c.mpeer(k)[1] for k in range(4)]
    yq = qk[2]
    f = lambda i: vec[i : i + 1]
    act, msg, loc = {}, {}, {}
    waited = set()

    def need(*ks):
        for k in ks:
            if k not in waited:
                waited.add(k)
                msg[k].wait_recv()

    def put(k, src, dst, dev):
        i = len(msg)
        msg[k] = rcopy(src, dst, r["ms"].at[i], r["mr"].at[i], dev)

    def local(k, src, dst):
        loc[k] = pltpu.make_async_copy(src, dst, r["ls"].at[len(loc)])

    ta = [qk[k] for k in (2, 3, 1, 0)]
    for i, k in enumerate(("wq", "wk", "wv")):
        local(k, r[k], WT.at[i * hw : (i + 1) * hw])
    for i in range(4):
        local("tok%d" % i, tok.at[ta[i]], TOK.at[ta[i]])
    for i in range(3):
        local("own%d" % i, wsrc[i], WA[i].at[m])
    local("cot", r["cot"].at[m], COT)
    loads = list(loc)

    x0, z0 = lax.rem(c.dp, 2), lax.rem(c.dp // 2, 2)
    pc = [x0 + 2 * z0, (1 - x0) + 2 * z0, x0 + 2 * (1 - z0)]
    parts = [(a, i, n) for a, n in GATHER for i in range(n)]
    of = lambda a: [p for p in range(len(parts)) if parts[p][0] == a]

    def gather(p):
        a, i, n = parts[p]
        W = WA[a]
        whole = W.shape[1] // n
        quarter = whole // 4

        def at(k):
            return pl.ds(pl.multiple_of(i * whole + pc[k] * quarter, 16), quarter)

        def w(k, half=None):
            if half is None:
                return W.at[yq, at(k)]
            return W.at[yq, at(k), half * (d // 2) : (half + 1) * (d // 2)]

        full = W.at[yq, i * whole : (i + 1) * whole]
        put("gy%d" % p, wsrc[a].at[at(0)], W.at[m, at(0)], yd)
        put("gx%d" % p, w(0), w(0), xd)
        put("gz%d" % p, w(0), w(0), zd)
        put("gdz%d" % p, w(1, 0), w(1, 0), zd)
        put("gdx%d" % p, w(2, 1), w(2, 1), xd)
        put("gt%d" % p, full, full, sd)
        act["gy.%d" % p] = lambda: need("gy%d" % p)
        act["gx.%d" % p] = lambda: need("gx%d" % p)
        act["gz.%d" % p] = lambda: need("gz%d" % p)
        act["gt.%d" % p] = lambda: need("gdx%d" % p, "gdz%d" % p)

    for p in range(len(parts)):
        gather(p)
    for a in range(3):
        put("gs%d" % a, wsrc[a], WA[a].at[m], sd)
    for k in (1, 2, 3):
        put("v%d" % k, vec, VA.at[m], c.mpeer(k))
    got = lambda a: ["gt%d" % p for p in of(a)]

    def start():
        for k in loads:
            loc[k].start()
        vec[...] = jnp.zeros(vec.shape, F32)
        for i, k in enumerate(("bo", "g1", "s1", "bd", "g2", "s2", "bu")):
            vec[i : i + 1] = r[k][...].astype(F32).reshape(1, d)
        vec[7:8, 0:hw] = r["bq"][...].astype(F32).reshape(1, hw)
        vec[8:9, 0:hw] = r["bv"][...].astype(F32).reshape(1, hw)
        VA[m] = vec[...]
        sub = lax.broadcasted_iota(jnp.int32, (aug - HD, seq), 0)
        ones = jnp.where(sub == 0, 1.0, 0.0).astype(BF)
        cols = vec[...].T[0:hw]
        r["BC"][0:hw] = cols[:, 7:8]
        r["BC"][hw : 2 * hw] = jnp.zeros((hw, 1), F32)
        r["BC"][2 * hw : 3 * hw] = cols[:, 8:9]
        for t in range(4):
            for h in range(nh):
                QT[t, h, HD:aug] = ones
        c.barrier()
        for k in (1, 2, 3):
            msg["v%d" % k].start()
        for k in ("wq", "wk", "wv"):
            loc[k].wait()

    act["start"] = start

    def qkv(s):
        t = ta[s]
        loc["tok%d" % s].wait()
        g = (mm(WT[...], TOK[t], 1, 1) + r["BC"][...]).astype(BF)
        sub = lax.broadcasted_iota(jnp.int32, (aug - HD, seq), 0)
        lane = lax.broadcasted_iota(jnp.int32, (aug - HD, seq), 1)
        dead = jnp.where(sub == 0, jnp.where(lane < ln[t], 0.0, -1e30), 0.0).astype(BF)
        for h in range(nh):
            QT[t, h, 0:HD] = g[h * HD : (h + 1) * HD] * jnp.asarray(HD**-0.5, BF)
            KT[t, h, 0:HD] = g[hw + h * HD : hw + (h + 1) * HD]
            KT[t, h, HD:aug] = dead
        VT[t] = g[2 * hw : 3 * hw]

    def head(s, h):
        t = ta[s]
        at = slice(h * HD, (h + 1) * HD)
        sc = mm(KT[t, h], QT[t, h], 0, 0)
        e = jnp.exp(sc - jnp.max(sc, axis=0, keepdims=True))
        ri = 1.0 / jnp.sum(e, axis=0, keepdims=True)
        el = e.astype(BF)
        ET[t, h] = el
        RI[t, h : h + 1] = ri
        o = (mm(VT[t, at], el, 1, 0) * ri).astype(BF)
        ATQ[t, at] = o
        if s == 3:
            ATO[m, at] = o

    for s in range(4):
        act["qkv.%d" % s] = lambda s=s: qkv(s)
        for h in range(nh):
            act["head.%d.%d" % (s, h)] = lambda s=s, h=h: head(s, h)
        if s < 3:
            put("at%d" % s, ATQ.at[ta[s]], ATO.at[m], c.mpeer((2, 3, 1)[s]))

    for h in (0, 1):
        put("sat%d" % h, ATO.at[1 - cb + 2 * h], SAT.at[h], sd)
    put("sfl", FL, SFL, sd)
    for k, h in ((1, yb), (3, 1 - yb)):
        put("sa%d" % k, ACT.at[1 - cb + 2 * h], SA.at[h], sd)

    def proj():
        need("gs0", "at0", "at1", "at2", *got(0))
        loc["own0"].wait()
        mixed = TOK[m].astype(F32) + f(0)
        for q in range(4):
            mixed += mm(ATO[q], WO[q], 0, 0)
        ACC[...] = mixed
        msg["sat0"].start()
        msg["sat1"].start()

    def norm1():
        def body(i, _):
            at = pl.ds(pl.multiple_of(i * nr, nr), nr)
            n1, i1 = norm_rows(ACC[at])
            N1[at] = n1
            I1[at] = i1
            FL[at] = (n1 * f(1) + f(2)).astype(BF)
            return 0

        lax.fori_loop(0, seq // nr, body, 0)
        msg["sfl"].start()
        need("v1", "v2", "v3")

    act["proj"], act["norm1"] = proj, norm1

    def ffn(k, j):
        if j == 0:
            if k == 0:
                loc["own1"].wait()
            elif k == 1:
                need("gs1")
            elif k == 3:
                need(*got(1))
        q = qk[k]
        at = slice(j * cw, (j + 1) * cw)
        h = mm(FL[...], UA[q, :, at], 1, 0) + VA[q, 6:7, at]
        g, gp = gelu_pair(h)
        ACT[q, :, at] = g.astype(BF)
        GP[q, :, at] = gp.astype(BF)

    def down(k):
        if k == 0:
            loc["own2"].wait()
        elif k == 1:
            need("gs2")
        elif k == 3:
            need(*got(2))
        y = mm(ACT[qk[k]], DA[qk[k]], 1, 0)
        if k == 0:
            ACC[...] = y
        else:
            ACC[...] += y

    for k in range(4):
        for j in range(3):
            act["ffn.%d.%d" % (k, j)] = lambda k=k, j=j: ffn(k, j)
        act["down.%d" % k] = lambda k=k: down(k)

    def fold(x):
        return jnp.sum(x.reshape(x.shape[0] // 8, 8, x.shape[1]), axis=0)

    zero = jnp.zeros((8, d), F32)

    def norm2():
        loc["cot"].wait()

        def body(i, sums):
            at = pl.ds(pl.multiple_of(i * nr, nr), nr)
            n2, i2 = norm_rows(N1[at] * f(1) + f(2) + ACC[at] + f(3))
            ct = COT[at].astype(F32)
            LOB[at] = (n2 * f(4) + f(5)).astype(BF)
            cg = ct * f(4)
            d2 = i2 * (
                cg
                - jnp.mean(cg, axis=-1, keepdims=True)
                - n2 * jnp.mean(cg * n2, axis=-1, keepdims=True)
            )
            ACC[at] = d2
            D2L[at] = d2.astype(BF)
            return sums[0] + fold(d2), sums[1] + fold(ct * n2), sums[2] + fold(ct)

        sums = lax.fori_loop(0, seq // nr, body, (zero,) * 3)
        SG[...] = jnp.zeros(SG.shape, F32)
        for i in range(3):
            SG[3 + i : 4 + i] = jnp.sum(sums[i], axis=0, keepdims=True)
        loc["lo"].start()

    act["norm2"] = norm2
    put("d2", D2L, SD2, sd)
    put("lo", LOB, LO.at[m], yd)
    put("los", LOB, LO.at[m], sd)
    put("lof", LO.at[yq], LO.at[yq], sd)
    local("lo", LOB, LO.at[m])
    act["lo_fwd"] = lambda: need("lo")

    def d_hidden(k):
        q = qk[k]

        def chunk(j, _):
            at = pl.ds(pl.multiple_of(j * cw, 128), cw)
            dh = (mm(D2L[...], DA[q, at, :], 1, 1) * GP[q, :, at].astype(F32)).astype(BF)
            GP[q, :, at] = dh
            SG[pl.ds(8 + q, 1), at] = jnp.sum(dh.astype(F32), axis=0, keepdims=True)
            return 0

        lax.fori_loop(0, 3, chunk, 0)

    for k in range(4):
        act["dh.%d" % k] = lambda k=k: d_hidden(k)
    put("sh1", GP.at[qk[1]], SH.at[yb], sd)
    put("sh3", GP.at[qk[3]], SH.at[1 - yb], sd)

    def down_grad(i):
        need("d2", "sa1", "sa3")
        n = d // len(DOWN)
        at = slice(i * n, (i + 1) * n)

        def body(h, _):
            q = cb + 2 * h
            GD[h, at] = (mm(ACT[q, :, at], D2L[...], 0, 0) + mm(SA[h, :, at], SD2[...], 0, 0)).astype(BF)
            return 0

        lax.fori_loop(0, 2, body, 0)

    def up_grad(i):
        need("sh1", "sh3", "sfl")
        n = d // len(UP)
        at = slice(i * n, (i + 1) * n)

        def body(h, _):
            q = cb + 2 * h
            GU[h, at] = (mm(FL[:, at], GP[q], 0, 0) + mm(SFL[:, at], SH[h], 0, 0)).astype(BF)
            return 0

        lax.fori_loop(0, 2, body, 0)

    for i in range(len(DOWN)):
        act["gd.%d" % i] = lambda i=i: down_grad(i)
    for i in range(len(UP)):
        act["gu.%d" % i] = lambda i=i: up_grad(i)

    def d_first(k):
        ACC[...] += mm(GP[qk[k]], UA[qk[k]], 1, 1)

    for k in range(4):
        act["d1.%d" % k] = lambda k=k: d_first(k)

    def norm1_back():
        early = ["d2", "sh1", "sh3", "sa1", "sa3"] + ["gs%d" % a for a in range(3)]
        early += ["g%s%d" % (k, p) for k in ("x", "z", "dz", "dx", "t", "y") for p in range(len(parts))]
        for k in early:
            msg[k].wait_send()
            sent.discard(k)

        def body(i, sums):
            at = pl.ds(pl.multiple_of(i * nr, nr), nr)
            d1, n1 = ACC[at], N1[at]
            cg = d1 * f(1)
            dm = I1[at] * (
                cg
                - jnp.mean(cg, axis=-1, keepdims=True)
                - n1 * jnp.mean(cg * n1, axis=-1, keepdims=True)
            )
            ACC[at] = dm
            DML[at] = dm.astype(BF)
            return sums[0] + fold(dm), sums[1] + fold(d1 * n1), sums[2] + fold(d1)

        sums = lax.fori_loop(0, seq // nr, body, (zero,) * 3)
        for i in range(3):
            SG[i : 1 + i] = jnp.sum(sums[i], axis=0, keepdims=True)

    act["norm1b"] = norm1_back
    put("dm", DML, SD2, sd)

    def d_attended(k):
        q = qk[k]
        g = mm(WO[q], DML[...], 1, 1).astype(BF)
        if k == 0:
            DOT[m] = g
        else:
            DTS[q] = g

    for k in range(4):
        act["datt.%d" % k] = lambda k=k: d_attended(k)
    put("h1", DTS.at[qk[1]], DOT.at[m], sd)
    base = len(msg)
    for k in (2, 3):
        msg["h%d" % k] = rcopy(DTS.at[qk[k]], DOT.at[m], r["ms"].at[base + k - 2], r["mr"].at[base + cb], c.mpeer(k))
    for k in (0, 1):
        msg["l%d" % k] = rcopy(DTS.at[0], DOT.at[0], r["ms"].at[base + k], r["mr"].at[base + k], yd)

    def out_grad():
        need("dm", "sat0", "sat1")
        for h in (0, 1):
            q = cb + 2 * h
            GO[h] = (mm(ATO[q], DML[...], 1, 0) + mm(SAT[h], SD2[...], 1, 0)).astype(BF)

    act["go"] = out_grad

    tb = [2 * yb, 2 * yb + 1, 2 * (1 - yb), 3 - 2 * yb]
    mine, theirs = (pl.ds(pl.multiple_of(v * hf, hf), hf) for v in (cb, 1 - cb))

    def back(s, h):
        t = tb[s]
        if h == 0:
            need(*(("h1",) if s < 2 else ("l0", "l1")))
        if s == 0 and h == 0:
            BQ[...] = jnp.zeros(BQ.shape, F32)
        at = slice(h * HD, (h + 1) * HD)
        g = DOT[t, at].astype(F32) * RI[t, h : h + 1]
        dd = jnp.sum(g * ATQ[t, at].astype(F32), axis=0, keepdims=True)
        gl = g.astype(BF)
        e = ET[t, h]
        ds = (e.astype(F32) * (mm(VT[t, at], gl, 0, 0) - dd)).astype(BF)
        dq = mm(KT[t, h, 0:HD], ds, 1, 0) * HD**-0.5
        dk = mm(QT[t, h, 0:HD], ds, 1, 1)
        dv = mm(gl, e, 1, 1)
        for i, x in enumerate((dq, dk, dv)):
            DA[t, i * hw + h * HD : i * hw + (h + 1) * HD, 0:seq] = x.astype(BF)

    def d_tokens(s):
        t = tb[s]
        g = DA[t, 0 : 3 * hw, 0:seq]
        BQ[:, 0 : 3 * hw] += mm(jnp.ones((8, seq), BF), g, 1, 1)
        dx = mm(g, WT[...], 0, 0)
        if s < 2:
            dx += jnp.where(cb == s, 1.0, 0.0) * ACC[...]
        ACT[t] = dx.astype(BF)

    def across(s):
        need("xc%d" % s, "l0", "l1")
        add_rows(ACT.at[tb[s], mine], UA.at[s, 0:hf], hf)

    def settle(s):
        o = (s + 2) % 4
        need("xy%d" % o)
        for k in ("xc%d" % s, "xy%d" % s):
            msg[k].wait_send()
            sent.discard(k)
        add_rows(ACT.at[tb[s], mine], UA.at[s, hf:seq], hf)
        loc["xt%d" % s].start()

    for s in range(4):
        for h in range(nh):
            act["ab.%d.%d" % (s, h)] = lambda s=s, h=h: back(s, h)
        act["dx.%d" % s] = lambda s=s: d_tokens(s)
        act["across.%d" % s] = lambda s=s: across(s)
        act["settle.%d" % s] = lambda s=s: settle(s)
        t = tb[s]
        part = ACT.at[t, mine]
        put("xc%d" % s, ACT.at[t, theirs], UA.at[s, 0:hf], sd)
        put("xt%d" % s, part, TG.at[t, mine], sd)
        local("xt%d" % s, part, TG.at[t, mine])
    base = len(msg)
    for s in range(4):
        o = (s + 2) % 4
        msg["xy%d" % s] = Both(
            rcopy(ACT.at[tb[s], mine], UA.at[o, hf:seq], r["ms"].at[base + s], r["mr"].at[base + o], yd),
            rcopy(ACT.at[tb[o], mine], UA.at[o, hf:seq], r["ms"].at[base + s], r["mr"].at[base + o], yd),
        )

    def qkv_grad(i):
        at = slice(i * hw, (i + 1) * hw)
        g = mm(DA[0, at, 0:seq], TOK[0], 1, 0)
        for t in range(1, 4):
            g += mm(DA[t, at, 0:seq], TOK[t], 1, 0)
        GQ[0, at] = g.astype(BF)

    for i in range(3):
        act["gq.%d" % i] = lambda i=i: qkv_grad(i)

    def view(G, base):
        def at(h, off, n):
            if isinstance(off, int):
                return G.at[h, base + off : base + off + n]
            return G.at[h, pl.ds(pl.multiple_of(base + off, 16), n)]

        return at

    def rows_of(O, base):
        def at(off, n):
            return O.at[pl.ds(pl.multiple_of(base + off, 16), n)]

        return at

    units = {}
    for j, (name, order, rows, base) in enumerate(unit_list(d, hw)):
        G, O = {"D": (GD, r["o_OD"]), "U": (GU, r["o_OU"]), "O": (GO, r["o_OO"]), "Q": (GQ, r["o_OQ"])}[name[1]]
        slots = [r["R%d%d" % (j, i)] for i in range(len(order))] + [r["X%d" % j].at[e] for e in range(nbits - 2)]
        units[name] = Unit(
            c, view(G, base), rows, order, slots, r["us"].at[j], r["ur"].at[j], rows_of(O, base), r["ul"].at[j]
        )
    dps = [c.dpeer(b) for b in range(nbits)]
    swaps = {
        "S": Swap(SG, r["SGR"], r["ws"], r["wr"], [sd, yd] + dps, 5),
        "B": Swap(BQ, r["BQR"], r["zs"], r["zr"], dps, 3),
    }

    sent = set()
    for k in SCHEDULE:
        if k in act:
            act[k]()
        elif k[0] == ">":
            w = k[1:].split(".")
            if w[0] in units:
                units[w[0]].send(int(w[1]), int(w[2]))
            elif w[0] in swaps:
                swaps[w[0]].send(int(w[1]))
            else:
                msg[k[1:]].start()
                sent.add(k[1:])
        else:
            w = k.split("/")
            (units[w[0]] if w[0] in units else swaps[w[0]]).finish(int(w[1]) - 1)

    r["o_OS"][...] = SG[...]
    r["o_OB"][...] = BQ[...]
    for k in ["v1", "v2", "v3", "sat0", "sat1", "sfl"] + [k for k in msg if k in sent]:
        msg[k].wait_send()
    need("los", "lof", "xt0", "xt1", "xt2", "xt3")
    for k in ("lo", "xt0", "xt1", "xt2", "xt3"):
        loc[k].wait()
    for u in units.values():
        u.drain()


class Both:
    def __init__(self, out, into):
        self.start, self.wait_send, self.wait_recv = out.start, out.wait_send, into.wait_recv


def unit_list(d, hw):
    res = [("GD%d" % i, o, d // len(DOWN), i * (d // len(DOWN))) for i, o in enumerate(DOWN)]
    res += [("GU%d" % i, o, d // len(UP), i * (d // len(UP))) for i, o in enumerate(UP)]
    return res + [("GO", OUT, hw, 0), ("GQ", QKV, 3 * hw, 0)]


def layer(tok4, cot4, lengths, vecs, wq, wk, wv, wo, wu, wd, nbits):
    nt, seq, d = tok4.shape
    hw = wq.shape[0]
    ff = wu.shape[1]
    nh = hw // HD
    V = pltpu.VMEM
    S = jax.ShapeDtypeStruct
    DMA = pltpu.SemaphoreType.DMA
    nex = nbits - 2
    nu = len(unit_list(d, hw))
    scratch = {
        "TOK": V((nt, seq, d), BF),
        "VEC": V((16, d), F32),
        "BC": V((3 * hw, 1), F32),
        "GQ": V((1, 3 * hw, d), BF),
        "WT": V((3 * hw, d), BF),
        "QT": V((nt, nh, HD + 16, seq), BF),
        "KT": V((nt, nh, HD + 16, seq), BF),
        "VT": V((nt, hw, seq), BF),
        "ET": V((nt, nh, seq, seq), BF),
        "RI": V((nt, 8, seq), F32),
        "ATQ": V((nt, hw, seq), BF),
        "ATO": V((nt, hw, seq), BF),
        "N1": V((seq, d), F32),
        "I1": V((seq, 1), F32),
        "FL": V((seq, d), BF),
        "ACT": V((nt, seq, ff), BF),
        "GP": V((nt, seq, ff), BF),
        "WOA": V((nt, hw, d), BF),
        "UA": V((nt, d, ff), BF),
        "DA": V((nt, ff, d), BF),
        "VA": V((nt, 16, d), F32),
        "ACC": V((seq, d), F32),
        "COT": V((seq, d), BF),
        "SA": V((2, seq, ff), BF),
        "SH": V((2, seq, ff), BF),
        "SFL": V((seq, d), BF),
        "SD2": V((seq, d), BF),
        "D2L": V((seq, d), BF),
        "SAT": V((2, hw, seq), BF),
        "DOT": V((nt, hw, seq), BF),
        "DTS": V((nt, hw, seq), BF),
        "SG": V((16, d), F32),
        "SGR": V((nbits + 2, 16, d), F32),
        "BQ": V((8, d), F32),
        "BQR": V((nbits, 8, d), F32),
        "GD": V((2, ff, d), BF),
        "GU": V((2, d, ff), BF),
        "GO": V((2, hw, d), BF),
        "ls": DMA((16,)),
        "ms": DMA((96,)),
        "mr": DMA((96,)),
        "us": DMA((nu, 8 + nex)),
        "ur": DMA((nu, 8 + nex)),
        "ul": DMA((nu,)),
        "ws": DMA((nbits + 2,)),
        "wr": DMA((nbits + 2,)),
        "zs": DMA((nbits,)),
        "zr": DMA((nbits,)),
    }
    for j, (_, order, rows, _) in enumerate(unit_list(d, hw)):
        n, h = rows, 2 if "y" in order else 1
        for i, ax in enumerate(order):
            if ax == "y":
                h = 1
            else:
                n //= 2
            scratch["R%d%d" % (j, i)] = V((h, n, d), BF)
        scratch["X%d" % j] = V((max(nex, 1), 1, n, d), BF)
    ins = {
        "len": lengths, **vecs, "tok": tok4, "cot": cot4,
        "wq": wq, "wk": wk, "wv": wv, "wo": wo, "wu": wu, "wd": wd,
    }
    A = pl.BlockSpec(memory_space=pl.ANY)
    B = pl.BlockSpec(memory_space=V)
    specs = [pl.BlockSpec(memory_space=pltpu.SMEM)] + [B] * len(vecs)
    specs += [A] * (len(ins) - len(specs))
    outs = {
        "LO": (S((nt, seq, d), BF), A),
        "TG": (S((nt, seq, d), BF), A),
        "OU": (S((d, ff), BF), A),
        "OD": (S((ff, d), BF), A),
        "OO": (S((hw, d), BF), A),
        "OQ": (S((3 * hw, d), BF), A),
        "OS": (S((16, d), F32), B),
        "OB": (S((8, d), F32), B),
    }
    names = list(ins) + ["o_" + n for n in outs] + list(scratch)

    def kernel(*refs):
        layer_kernel(nbits, names, *refs)

    res = pl.pallas_call(
        kernel,
        out_shape=[o[0] for o in outs.values()],
        in_specs=specs,
        out_specs=[o[1] for o in outs.values()],
        scratch_shapes=list(scratch.values()),
        compiler_params=pltpu.CompilerParams(
            collective_id=0, has_side_effects=True, vmem_limit_bytes=60 * 2**20
        ),
    )(*ins.values())
    return dict(zip(outs, res))


def shards(
    tokens, lengths, wq, bq, wk, wv, bv, wo, bo, g1, s1, wu, bu, wd, bd, g2, s2, cot
):
    n = lengths.shape[0]
    rows, d = tokens.shape
    seq = rows // n
    hw = wq.shape[1]
    m = lax.axis_index("mp")
    nbits = lax.axis_size("dp").bit_length() - 1
    f = lambda a: a.astype(F32)
    vecs = {
        "bo": bo, "g1": g1, "s1": s1, "bd": bd, "g2": g2, "s2": s2, "bu": bu, "bq": bq, "bv": bv
    }
    o = layer(
        tokens.reshape(n, seq, d), cot.reshape(n, seq, d), lengths, vecs, wq.T, wk.T, wv.T, wo, wu, wd, nbits
    )
    res = finish([o[k] for k in ("LO", "TG", "OU", "OD", "OO", "OQ", "OS", "OB")])
    lo, tg, du, dd, do, dq, dk, dv, dbq, dbv, dbu, dbo, dg1, ds1, dbd, dg2, ds2 = res
    return (
        lo.reshape(rows, d), tg.reshape(rows, d), dq.T, dbq, dk.T, dv.T, dbv, do, dbo, dg1, ds1,
        du, dbu, dd, dbd, dg2, ds2,
    )


def finish_kernel(*refs):
    ins, outs, bufs, wide, (si, so) = refs[:8], refs[8:25], refs[25:31], refs[31:35], refs[35:37]
    loads = []
    for i in range(2):
        loads.append([pltpu.make_async_copy(ins[i].at[t], bufs[i].at[t], si.at[i * 4 + t]) for t in range(4)])
    loads += [[pltpu.make_async_copy(ins[i], bufs[i], si.at[6 + i])] for i in range(2, 6)]
    for i in (2, 3, 5, 4, 0, 1):
        for x in loads[i]:
            x.start()
    stores = []

    def store(src, dst):
        stores.append(pltpu.make_async_copy(src, dst, so.at[len(stores)]))
        stores[-1].start()

    sg, b = ins[6], ins[7]
    m = lax.axis_index("mp")
    hw = ins[5].shape[0] // 3
    d = ins[5].shape[1]
    outs[8][...] = b[0:1, 0:hw].reshape(hw)
    outs[9][...] = b[0:1, 2 * hw : 3 * hw].reshape(hw)
    outs[10][...] = sg[pl.ds(8 + m, 1)].reshape(d)
    for i in range(6):
        outs[11 + i][...] = sg[i : i + 1].reshape(d)
    for i in (2, 3, 5, 4):
        loads[i][0].wait()
        h = 192
        for k in range(bufs[i].shape[0] // h):
            at = slice(k * h, (k + 1) * h)
            wide[i - 2][at] = bufs[i][at].astype(F32)
            store(wide[i - 2].at[at], outs[5 + k] if i == 5 else outs[i].at[at])
    for i in range(2):
        for t in range(4):
            loads[i][t].wait()
            store(bufs[i].at[t], outs[i].at[t])
    for x in stores:
        x.wait()


def finish(vals):
    S = jax.ShapeDtypeStruct
    V = pltpu.VMEM
    A = pl.BlockSpec(memory_space=pl.ANY)
    B = pl.BlockSpec(memory_space=V)
    shapes = [v.shape for v in vals]
    d = shapes[5][1]
    hw = shapes[5][0] // 3
    outs = [S(shapes[0], BF), S(shapes[1], BF)] + [S(s, F32) for s in shapes[2:5]]
    outs += [S((hw, d), F32)] * 3 + [S((hw,), F32)] * 2 + [S((d,), F32)] * 7
    return pl.pallas_call(
        finish_kernel,
        out_shape=outs,
        in_specs=[A] * 6 + [B] * 2,
        out_specs=[A] * 8 + [B] * 9,
        scratch_shapes=[V(s, BF) for s in shapes[:6]]
        + [V(s, F32) for s in shapes[2:6]]
        + [pltpu.SemaphoreType.DMA((12,)), pltpu.SemaphoreType.DMA((24,))],
        compiler_params=pltpu.CompilerParams(vmem_limit_bytes=60 * 2**20),
    )(*vals)


def solution(mesh):
    row, col, one, rep = P("dp", None), P(None, "mp"), P("mp"), P()
    low = P("mp", None)
    in_specs = (
        row, P("dp"), col, one, col, col, one, low, rep, rep, rep, col, one, low, rep, rep, rep, row,
    )
    out_specs = (
        row, row, col, one, col, col, one, low, rep, rep, rep, col, one, low, rep, rep, rep,
    )
    return jax.shard_map(shards, mesh=mesh, in_specs=in_specs, out_specs=out_specs, check_vma=False)
```

```python
import jax
import jax.numpy as jnp
from jax import lax
from jax.experimental import pallas as pl
from jax.experimental.pallas import tpu as pltpu
from jax.sharding import PartitionSpec as P

HD = 64
EPS = 1e-06
BF = jnp.bfloat16
F32 = jnp.float32
MESH = pl.DeviceIdType.MESH


DOWN = ("xzy", "zxy", "xzy", "xzy")
UP = ("xzy", "yzx", "zyx", "yzx")
OUT = "yxz"
QKV = "xz"
GATHER = ((0, 1), (1, 3), (2, 3))


class Step:
    def __init__(self, lead, join):
        self.lead, self.join = lead, join

    def __getattr__(self, name):
        return lambda *at: self.lead + name + "".join(self.join + str(a) for a in at)


step, send, end = Step("", "."), Step(">", "."), Step("", "/")
SCHEDULE = (
    step.start(), send.gy0(), send.gy2(), send.gs0(), send.gs2(), send.gs1(), step.ready(),
    step.qkv(0), step.head(0, 0), step.head(0, 1), send.gy3(), step.head(0, 2), step.qkv(1),
    send.gy1(), step.head(1, 0), step.gy(0), send.gx0(), send.gz0(), step.head(1, 1),
    step.head(1, 2), send.at1(), step.gy(2), send.gx2(), send.gz2(), step.qkv(2), send.gy4(),
    step.head(2, 0), step.gy(3), send.gz3(), send.gx3(), step.head(2, 1), step.gx(0), send.gdz0(),
    step.gz(0), send.gdx0(), step.head(2, 2), send.at2(), step.gy(1), step.qkv(3), send.gx1(),
    send.gz1(), step.gx(2), step.head(3, 0), send.gdz2(), send.gy5(), step.gz(2), send.gdx2(),
    step.head(3, 1), step.head(3, 2), send.gy6(), step.gt(0), send.gt0(), step.gx(3), send.gdz3(),
    step.gz(3), step.gy(4), send.gdx3(), send.gx4(), send.gz4(), send.at0(), step.gt(2),
    send.gt2(), step.gx(1), send.gdz1(), step.gz(1), send.gdx1(), step.gy(5), send.gx5(),
    send.gz5(), step.gt(3), send.gt3(), step.gx(4), send.gdz4(), step.gy(6), send.gx6(),
    step.gz(4), send.gdx4(), step.gt(1), send.gt1(), send.gz6(), step.gx(5), send.gdz5(),
    step.proj(), step.gz(5), send.gdx5(), step.norm1(), step.gt(4), send.gt4(), step.gx(6),
    send.gdz6(), step.ffn(0, 0), step.gz(6), send.gdx6(), step.ffn(0, 1), step.ffn(0, 2),
    step.down(0), step.ffn(1, 0), step.gt(5), send.gt5(), step.ffn(1, 1), step.ffn(1, 2),
    send.sa1(), step.down(1), step.gt(6), send.gt6(), step.ffn(2, 0), step.ffn(2, 1),
    step.ffn(2, 2), step.down(2), step.ffn(3, 0), step.ffn(3, 1), step.ffn(3, 2), send.sa3(),
    step.down(3), step.norm2(), send.d2(), send.los(), send.lo(), step.dh(1), send.sh1(),
    step.dh(0), step.gd(0), send.GD0(0, 0), send.GD0(0, 1), step.gd(1), send.GD1(0, 0),
    send.GD1(0, 1), step.gd(2), step.gd(3), step.dh(3), send.sh3(), step.dh(2), step.d1(0),
    send.GD2(0, 1), step.d1(1), send.GD2(0, 0), step.d1(2), step.d1(3), step.norm1b(), send.dm(),
    end.GD0(1), send.GD0(1, 0), send.GD0(1, 1), end.GD1(1), step.datt(1), send.h1(), step.datt(2),
    send.h2(), step.datt(3), step.datt(0), send.S(0), step.gu(0), send.GU0(0, 0), send.h3(),
    step.gu(2), send.GD1(1, 0), send.GU2(0, 1), send.GU2(0, 0), end.S(1), step.gu(3),
    step.lo_fwd(), send.lof(), step.ab(0, 0), end.GD0(2), end.GD2(1), step.ab(0, 1),
    send.GD1(1, 1), step.ab(0, 2), send.GU0(0, 1), step.dx(0), send.GD0(2, 0), send.xc0(),
    step.go(), send.GD2(1, 0), send.GD3(0, 0), send.GD2(1, 1), step.ab(1, 0), send.GO(0, 0),
    step.ab(1, 1), send.S(1), end.GD1(2), end.GU2(1), step.ab(1, 2), step.across(0),
    send.GD3(0, 1), step.dx(1), send.GD1(2, 0), send.xc1(), end.GD0(3), send.GD0(3, 0),
    step.gu(1), end.GD2(2), step.ab(2, 0), end.GU0(1), send.GU0(1, 1), end.S(2), send.S(2),
    step.across(1), step.ab(2, 1), send.GD2(2, 0), send.GU0(1, 0), step.ab(2, 2), step.dx(2),
    send.xc2(), end.GD1(3), send.GD1(3, 0), step.ab(3, 0), send.xy1(), send.GU1(0, 0), end.GD0(4),
    send.GD0(4, 1), send.GD0(4, 0), end.S(3), end.GD3(1), step.ab(3, 1), end.GU0(2),
    step.across(2), end.GO(1), send.GO(1, 0), send.S(3), end.GD2(3), step.ab(3, 2),
    send.GD3(1, 0), step.dx(3), send.xc3(), send.GD3(1, 1), step.gq(0), step.gq(1), end.GD1(4),
    send.GD1(4, 0), end.GD0(5), send.GD0(5, 0), step.gq(2), send.GD1(4, 1), end.S(4),
    step.across(3), send.S(4), end.GO(2), send.B(0), send.GQ(0, 0), send.GO(2, 0), end.GD3(2),
    send.GD2(3, 0), end.GD1(5), end.GD0(6), send.GD1(5, 0), end.B(1), send.xy3(), end.S(5),
    send.B(1), end.GO(3), send.GO(3, 0), end.GU1(1), send.GU1(1, 0), end.GD2(4), send.GD2(4, 1),
    end.B(2), send.GU0(2, 0), end.GD1(6), send.B(2), send.GD2(4, 0), send.GD3(2, 0), end.GO(4),
    send.GO(4, 1), send.GO(4, 0), end.GU0(3), send.GU0(3, 0), end.B(3), send.GU3(0, 0), end.GQ(1),
    end.GU1(2), send.GU1(2, 0), send.GQ(1, 0), end.GD2(5), send.GD2(5, 0), end.GD3(3),
    send.GD3(3, 0), end.GO(5), send.GO(5, 0), end.GU0(4), send.GU0(4, 1), send.GU0(4, 0),
    end.GU1(3), send.GU2(1, 0), end.GD2(6), end.GO(6), step.settle(1), send.xt1(), send.GU1(3, 0),
    step.settle(3), send.xt3(), end.GD3(4), send.GD3(4, 1), send.GD3(4, 0), end.GU0(5),
    send.GU0(5, 0), send.xy2(), send.xy0(), end.GQ(2), send.GQ(2, 0), end.GU3(1), send.GU3(1, 0),
    end.GU2(2), send.GU2(2, 0), end.GD3(5), send.GD3(5, 0), end.GU1(4), end.GU0(6),
    send.GU1(4, 0), end.GU2(3), end.GD3(6), send.GU1(4, 1), end.GU1(5), send.GU2(3, 0),
    end.GU3(2), send.GU3(2, 0), send.GU1(5, 0), end.GQ(3), send.GQ(3, 0), send.GQ(3, 1),
    end.GU3(3), send.GU3(3, 0), end.GU2(4), send.GU2(4, 0), end.GU1(6), send.GU2(4, 1),
    step.settle(0), send.xt0(), step.settle(2), send.xt2(), end.GU3(4), send.GU3(4, 0),
    send.GU3(4, 1), end.GU2(5), send.GU2(5, 0), end.GQ(4), send.GQ(4, 0), end.GU3(5),
    send.GU3(5, 0), end.GU2(6), end.GU3(6), end.GQ(5),
)


def mm(a, b, ca, cb):
    return lax.dot_general(a, b, (((ca,), (cb,)), ((), ())), preferred_element_type=F32)


def flip(v, b):
    return v + b - 2 * b * lax.rem(v // b, 2)


def gelu_pair(h):
    x = h * 0.7071067811865476
    e = jnp.exp(-(x * x))
    t = 1.0 / (1.0 + 0.3275911 * jnp.abs(x))
    poly = t * (
        0.254829592
        + t * (-0.284496736 + t * (1.421413741 + t * (-1.453152027 + t * 1.061405429)))
    )
    tail = 0.5 * poly * e
    phi = jnp.where(h > 0, 1.0 - tail, tail)
    return h * phi, phi + h * e * 0.3989422804014327


def add_rows(dst, src, n):
    step = 48 if n % 48 == 0 else 64

    def body(i, _):
        at = pl.ds(pl.multiple_of(i * step, 16), step)
        a, b = dst.at[at], src.at[at]
        a[...] = (a[...].astype(F32) + b[...].astype(F32)).astype(BF)
        return 0

    lax.fori_loop(0, n // step, body, 0)


def norm_rows(x):
    center = x - jnp.mean(x, axis=-1, keepdims=True)
    inv = lax.rsqrt(jnp.mean(center * center, axis=-1, keepdims=True) + EPS)
    return center * inv, inv


class Comm:
    def __init__(self, nbits):
        self.dp, self.mp = lax.axis_index("dp"), lax.axis_index("mp")
        self.nbits = nbits

    def mpeer(self, k):
        v = self.mp
        for b in (1, 2):
            if k & b:
                v = flip(v, b)
        return (self.dp, v)

    def dpeer(self, bit):
        return (flip(self.dp, 1 << bit), self.mp)

    def announce(self):
        bar = pltpu.get_barrier_semaphore()
        peers = [self.mpeer(k) for k in (1, 2, 3)] + [self.dpeer(b) for b in range(self.nbits)]
        for p in peers:
            pl.semaphore_signal(bar, inc=1, device_id=p, device_id_type=MESH)
        return lambda: pl.semaphore_wait(bar, len(peers))


def rcopy(src, dst, ss, rs, dev):
    return pltpu.make_async_remote_copy(
        src_ref=src, dst_ref=dst, send_sem=ss, recv_sem=rs, device_id=dev, device_id_type=MESH
    )


class Unit:
    def __init__(self, c, view, rows, order, slots, ss, rs, out, loc):
        y = c.mp // 2
        hs, own = ([0, 1], 0) if "y" in order else ([0], 0)
        off, n, k = 0, rows, 0
        spans = []

        def put(a, b, dev):
            nonlocal k
            cp = rcopy(a, b, ss.at[k], rs.at[k], dev)
            k += 1
            return cp

        self.steps = steps = []
        for i, ax in enumerate(order):
            if ax == "y":
                cps = [put(view(1 - y, off, n), slots[i].at[0], c.mpeer(2))]
                hs, own = [y], y
                adds = [(view(y, off, n), slots[i].at[0], n)]
            else:
                b = "xz".index(ax)
                bit = lax.rem(c.dp // (1 << b), 2)
                spans.append((b, off, n))
                n //= 2
                mine, theirs = off + bit * n, off + (1 - bit) * n
                cps, adds = [], []
                for j, h in enumerate(hs):
                    cps.append(put(view(h, theirs, n), slots[i].at[j], c.dpeer(b)))
                    adds.append((view(h, mine, n), slots[i].at[j], n))
                off = mine
            steps.append((cps, adds))
        mine = view(own, off, n)
        self.swaps = []
        for b in range(2, c.nbits):
            sl = slots[len(order) + b - 2].at[0]
            self.swaps.append((put(mine, sl, c.dpeer(b)), (mine, sl, n)))
        steps.append(([self.swaps[0][0]] if self.swaps else [], []))
        (b2, _, _), (b1, o1, _) = spans
        bit = lax.rem(c.dp // (1 << b1), 2)
        theirs = o1 + (1 - bit) * n
        self.local = pltpu.make_async_copy(mine, out(off, n), loc)
        first = put(mine, out(off, n), c.dpeer(b1))
        self.hold = put(mine, out(off, n), c.dpeer(b2))
        third = put(out(theirs, n), out(theirs, n), c.dpeer(b2))
        steps.append(([first, self.hold], []))
        steps.append(([third], []))

    def send(self, i, j):
        cps = self.steps[i][0]
        if j < len(cps):
            cps[j].start()

    def finish(self, i):
        cps, adds = self.steps[i]
        last = len(self.steps)
        if i == last - 3:
            for e, (cp, add) in enumerate(self.swaps):
                if e:
                    cp.start()
                cp.wait()
                add_rows(*add)
            self.local.start()
            return
        for cp in cps:
            if cp is not self.hold:
                cp.wait_recv()
        for a in adds:
            add_rows(*a)
        if i == last - 1:
            self.hold.wait_recv()

    def drain(self):
        for i, (cps, _) in enumerate(self.steps):
            if i != len(self.steps) - 3:
                for cp in cps:
                    cp.wait_send()
        self.local.wait()


class Swap:
    def __init__(self, ref, slots, ss, rs, peers, count):
        self.ref, self.slots, self.count = ref, slots, count
        self.cps = [rcopy(ref, slots.at[i], ss.at[i], rs.at[i], p) for i, p in enumerate(peers)]

    def send(self, i):
        self.cps[i].start()

    def finish(self, i):
        self.cps[i].wait()
        self.ref[...] += self.slots[i]
        if i == self.count - 1:
            for e in range(self.count, len(self.cps)):
                self.cps[e].start()
                self.cps[e].wait()
                self.ref[...] += self.slots[e]


def layer_kernel(nbits, names, *refs):
    r = dict(zip(names, refs))
    ln, vec, tok = r["len"], r["VEC"], r["tok"]
    TOK, WT, QT, KT, VT, ET, RI = (r[k] for k in ("TOK", "WT", "QT", "KT", "VT", "ET", "RI"))
    ATQ, ATO, N1, I1, FL, ACT, GP = (r[k] for k in ("ATQ", "ATO", "N1", "I1", "FL", "ACT", "GP"))
    VA, ACC, COT, SA, SFL, SAT = (r[k] for k in ("VA", "ACC", "COT", "SA", "SFL", "SAT"))
    D2L, SD2, SH, DOT, DTS, SG, BQ = (r[k] for k in ("D2L", "SD2", "SH", "DOT", "DTS", "SG", "BQ"))
    GD, GU, GO, GQ, LO, TG = (r[k] for k in ("GD", "GU", "GO", "GQ", "o_LO", "o_TG"))
    WA = WO, UA, DA = (r["WOA"], r["UA"], r["DA"])
    DML, LOB = D2L, COT
    wsrc = (r["wo"], r["wu"], r["wd"])
    c = Comm(nbits)
    m = c.mp
    cb, yb = lax.rem(m, 2), m // 2
    seq, d = TOK.shape[1], TOK.shape[2]
    hw = VT.shape[1]
    nh = hw // HD
    aug = QT.shape[2]
    hf = seq // 2
    cw = d // 3
    nr = 64
    yd, sd, xd, zd = c.mpeer(2), c.mpeer(1), c.dpeer(0), c.dpeer(1)
    qk = [c.mpeer(k)[1] for k in range(4)]
    yq = qk[2]
    f = lambda i: vec[i : i + 1]
    act, msg, loc = {}, {}, {}
    waited = set()

    def need(*ks):
        for k in ks:
            if k not in waited:
                waited.add(k)
                msg[k].wait_recv()

    def put(k, src, dst, dev):
        i = len(msg)
        msg[k] = rcopy(src, dst, r["ms"].at[i], r["mr"].at[i], dev)

    def local(k, src, dst):
        loc[k] = pltpu.make_async_copy(src, dst, r["ls"].at[len(loc)])

    ta = [qk[k] for k in (2, 3, 1, 0)]
    for i, k in enumerate(("wq", "wk", "wv")):
        local(k, r[k], WT.at[i * hw : (i + 1) * hw])
    for i in range(4):
        local("tok%d" % i, tok.at[ta[i]], TOK.at[ta[i]])
    for i in range(3):
        local("own%d" % i, wsrc[i], WA[i].at[m])
    local("cot", r["cot"].at[m], COT)
    loads = list(loc)

    x0, z0 = lax.rem(c.dp, 2), lax.rem(c.dp // 2, 2)
    pc = [x0 + 2 * z0, (1 - x0) + 2 * z0, x0 + 2 * (1 - z0)]
    parts = [(a, i, n) for a, n in GATHER for i in range(n)]
    of = lambda a: [p for p in range(len(parts)) if parts[p][0] == a]

    def gather(p):
        a, i, n = parts[p]
        W = WA[a]
        whole = W.shape[1] // n
        quarter = whole // 4

        def at(k):
            return pl.ds(pl.multiple_of(i * whole + pc[k] * quarter, 16), quarter)

        def w(k, half=None):
            if half is None:
                return W.at[yq, at(k)]
            return W.at[yq, at(k), half * (d // 2) : (half + 1) * (d // 2)]

        full = W.at[yq, i * whole : (i + 1) * whole]
        put("gy%d" % p, wsrc[a].at[at(0)], W.at[m, at(0)], yd)
        put("gx%d" % p, w(0), w(0), xd)
        put("gz%d" % p, w(0), w(0), zd)
        put("gdz%d" % p, w(1, 0), w(1, 0), zd)
        put("gdx%d" % p, w(2, 1), w(2, 1), xd)
        put("gt%d" % p, full, full, sd)
        act["gy.%d" % p] = lambda: need("gy%d" % p)
        act["gx.%d" % p] = lambda: need("gx%d" % p)
        act["gz.%d" % p] = lambda: need("gz%d" % p)
        act["gt.%d" % p] = lambda: need("gdx%d" % p, "gdz%d" % p)

    for p in range(len(parts)):
        gather(p)
    for a in range(3):
        put("gs%d" % a, wsrc[a], WA[a].at[m], sd)
    for k in (1, 2, 3):
        put("v%d" % k, vec, VA.at[m], c.mpeer(k))
    got = lambda a: ["gt%d" % p for p in of(a)]

    def start():
        everyone = c.announce()
        for k in loads:
            loc[k].start()
        vec[...] = jnp.zeros(vec.shape, F32)
        for i, k in enumerate(("bo", "g1", "s1", "bd", "g2", "s2", "bu")):
            vec[i : i + 1] = r[k][...].astype(F32).reshape(1, d)
        vec[7:8, 0:hw] = r["bq"][...].astype(F32).reshape(1, hw)
        vec[8:9, 0:hw] = r["bv"][...].astype(F32).reshape(1, hw)
        VA[m] = vec[...]
        everyone()

    def ready():
        for k in (1, 2, 3):
            msg["v%d" % k].start()
        sub = lax.broadcasted_iota(jnp.int32, (aug - HD, seq), 0)
        ones = jnp.where(sub == 0, 1.0, 0.0).astype(BF)
        cols = vec[...].T[0:hw]
        r["BC"][0:hw] = cols[:, 7:8]
        r["BC"][hw : 2 * hw] = jnp.zeros((hw, 1), F32)
        r["BC"][2 * hw : 3 * hw] = cols[:, 8:9]
        for t in range(4):
            for h in range(nh):
                QT[t, h, HD:aug] = ones
        for k in ("wq", "wk", "wv"):
            loc[k].wait()

    act["ready"] = ready
    act["start"] = start

    def qkv(s):
        t = ta[s]
        loc["tok%d" % s].wait()
        g = (mm(WT[...], TOK[t], 1, 1) + r["BC"][...]).astype(BF)
        sub = lax.broadcasted_iota(jnp.int32, (aug - HD, seq), 0)
        lane = lax.broadcasted_iota(jnp.int32, (aug - HD, seq), 1)
        dead = jnp.where(sub == 0, jnp.where(lane < ln[t], 0.0, -1e30), 0.0).astype(BF)
        for h in range(nh):
            QT[t, h, 0:HD] = g[h * HD : (h + 1) * HD] * jnp.asarray(HD**-0.5, BF)
            KT[t, h, 0:HD] = g[hw + h * HD : hw + (h + 1) * HD]
            KT[t, h, HD:aug] = dead
        VT[t] = g[2 * hw : 3 * hw]

    def head(s, h):
        t = ta[s]
        at = slice(h * HD, (h + 1) * HD)
        sc = mm(KT[t, h], QT[t, h], 0, 0)
        e = jnp.exp(sc - jnp.max(sc, axis=0, keepdims=True))
        ri = 1.0 / jnp.sum(e, axis=0, keepdims=True)
        el = e.astype(BF)
        ET[t, h] = el
        RI[t, h : h + 1] = ri
        o = (mm(VT[t, at], el, 1, 0) * ri).astype(BF)
        ATQ[t, at] = o
        if s == 3:
            ATO[m, at] = o

    for s in range(4):
        act["qkv.%d" % s] = lambda s=s: qkv(s)
        for h in range(nh):
            act["head.%d.%d" % (s, h)] = lambda s=s, h=h: head(s, h)
        if s < 3:
            put("at%d" % s, ATQ.at[ta[s]], ATO.at[m], c.mpeer((2, 3, 1)[s]))

    for h in (0, 1):
        put("sat%d" % h, ATO.at[1 - cb + 2 * h], SAT.at[h], sd)
    put("sfl", FL, SFL, sd)
    for k, h in ((1, yb), (3, 1 - yb)):
        put("sa%d" % k, ACT.at[1 - cb + 2 * h], SA.at[h], sd)

    def proj():
        need("gs0", "at0", "at1", "at2", *got(0))
        loc["own0"].wait()
        mixed = TOK[m].astype(F32) + f(0)
        for q in range(4):
            mixed += mm(ATO[q], WO[q], 0, 0)
        ACC[...] = mixed
        msg["sat0"].start()
        msg["sat1"].start()

    def norm1():
        def body(i, _):
            at = pl.ds(pl.multiple_of(i * nr, nr), nr)
            n1, i1 = norm_rows(ACC[at])
            N1[at] = n1
            I1[at] = i1
            FL[at] = (n1 * f(1) + f(2)).astype(BF)
            return 0

        lax.fori_loop(0, seq // nr, body, 0)
        msg["sfl"].start()
        need("v1", "v2", "v3")

    act["proj"], act["norm1"] = proj, norm1

    def ffn(k, j):
        if j == 0:
            if k == 0:
                loc["own1"].wait()
            elif k == 1:
                need("gs1")
            elif k == 3:
                need(*got(1))
        q = qk[k]
        at = slice(j * cw, (j + 1) * cw)
        h = mm(FL[...], UA[q, :, at], 1, 0) + VA[q, 6:7, at]
        g, gp = gelu_pair(h)
        ACT[q, :, at] = g.astype(BF)
        GP[q, :, at] = gp.astype(BF)

    def down(k):
        if k == 0:
            loc["own2"].wait()
        elif k == 1:
            need("gs2")
        elif k == 3:
            need(*got(2))
        y = mm(ACT[qk[k]], DA[qk[k]], 1, 0)
        if k == 0:
            ACC[...] = y
        else:
            ACC[...] += y

    for k in range(4):
        for j in range(3):
            act["ffn.%d.%d" % (k, j)] = lambda k=k, j=j: ffn(k, j)
        act["down.%d" % k] = lambda k=k: down(k)

    def fold(x):
        return jnp.sum(x.reshape(x.shape[0] // 8, 8, x.shape[1]), axis=0)

    zero = jnp.zeros((8, d), F32)

    def norm2():
        loc["cot"].wait()

        def body(i, sums):
            at = pl.ds(pl.multiple_of(i * nr, nr), nr)
            n2, i2 = norm_rows(N1[at] * f(1) + f(2) + ACC[at] + f(3))
            ct = COT[at].astype(F32)
            LOB[at] = (n2 * f(4) + f(5)).astype(BF)
            cg = ct * f(4)
            d2 = i2 * (
                cg
                - jnp.mean(cg, axis=-1, keepdims=True)
                - n2 * jnp.mean(cg * n2, axis=-1, keepdims=True)
            )
            ACC[at] = d2
            D2L[at] = d2.astype(BF)
            return sums[0] + fold(d2), sums[1] + fold(ct * n2), sums[2] + fold(ct)

        sums = lax.fori_loop(0, seq // nr, body, (zero,) * 3)
        SG[...] = jnp.zeros(SG.shape, F32)
        for i in range(3):
            SG[3 + i : 4 + i] = jnp.sum(sums[i], axis=0, keepdims=True)
        loc["lo"].start()

    act["norm2"] = norm2
    put("d2", D2L, SD2, sd)
    put("lo", LOB, LO.at[m], yd)
    put("los", LOB, LO.at[m], sd)
    put("lof", LO.at[yq], LO.at[yq], sd)
    local("lo", LOB, LO.at[m])
    act["lo_fwd"] = lambda: need("lo")

    def d_hidden(k):
        q = qk[k]

        def chunk(j, _):
            at = pl.ds(pl.multiple_of(j * cw, 128), cw)
            dh = (mm(D2L[...], DA[q, at, :], 1, 1) * GP[q, :, at].astype(F32)).astype(BF)
            GP[q, :, at] = dh
            SG[pl.ds(8 + q, 1), at] = jnp.sum(dh.astype(F32), axis=0, keepdims=True)
            return 0

        lax.fori_loop(0, 3, chunk, 0)

    for k in range(4):
        act["dh.%d" % k] = lambda k=k: d_hidden(k)
    put("sh1", GP.at[qk[1]], SH.at[yb], sd)
    put("sh3", GP.at[qk[3]], SH.at[1 - yb], sd)

    def down_grad(i):
        need("d2", "sa1", "sa3")
        n = d // len(DOWN)
        at = slice(i * n, (i + 1) * n)

        def body(h, _):
            q = cb + 2 * h
            GD[h, at] = (mm(ACT[q, :, at], D2L[...], 0, 0) + mm(SA[h, :, at], SD2[...], 0, 0)).astype(BF)
            return 0

        lax.fori_loop(0, 2, body, 0)

    def up_grad(i):
        need("sh1", "sh3", "sfl")
        n = d // len(UP)
        at = slice(i * n, (i + 1) * n)

        def body(h, _):
            q = cb + 2 * h
            GU[h, at] = (mm(FL[:, at], GP[q], 0, 0) + mm(SFL[:, at], SH[h], 0, 0)).astype(BF)
            return 0

        lax.fori_loop(0, 2, body, 0)

    for i in range(len(DOWN)):
        act["gd.%d" % i] = lambda i=i: down_grad(i)
    for i in range(len(UP)):
        act["gu.%d" % i] = lambda i=i: up_grad(i)

    def d_first(k):
        ACC[...] += mm(GP[qk[k]], UA[qk[k]], 1, 1)

    for k in range(4):
        act["d1.%d" % k] = lambda k=k: d_first(k)

    def norm1_back():
        need("sh1", "sh3")
        early = ["d2", "sh1", "sh3", "sa1", "sa3"] + ["gs%d" % a for a in range(3)]
        early += ["g%s%d" % (k, p) for k in ("x", "z", "dz", "dx", "t", "y") for p in range(len(parts))]
        for k in early:
            msg[k].wait_send()
            sent.discard(k)

        def body(i, sums):
            at = pl.ds(pl.multiple_of(i * nr, nr), nr)
            d1, n1 = ACC[at], N1[at]
            cg = d1 * f(1)
            dm = I1[at] * (
                cg
                - jnp.mean(cg, axis=-1, keepdims=True)
                - n1 * jnp.mean(cg * n1, axis=-1, keepdims=True)
            )
            ACC[at] = dm
            DML[at] = dm.astype(BF)
            return sums[0] + fold(dm), sums[1] + fold(d1 * n1), sums[2] + fold(d1)

        sums = lax.fori_loop(0, seq // nr, body, (zero,) * 3)
        for i in range(3):
            SG[i : 1 + i] = jnp.sum(sums[i], axis=0, keepdims=True)

    act["norm1b"] = norm1_back
    put("dm", DML, SD2, sd)

    def d_attended(k):
        q = qk[k]
        g = mm(WO[q], DML[...], 1, 1).astype(BF)
        if k == 0:
            DOT[m] = g
        else:
            DTS[q] = g

    for k in range(4):
        act["datt.%d" % k] = lambda k=k: d_attended(k)
    put("h1", DTS.at[qk[1]], DOT.at[m], sd)
    base = len(msg)
    for k in (2, 3):
        msg["h%d" % k] = rcopy(DTS.at[qk[k]], DOT.at[m], r["ms"].at[base + k - 2], r["mr"].at[base + cb], c.mpeer(k))
    for k in (0, 1):
        msg["l%d" % k] = rcopy(DTS.at[0], DOT.at[0], r["ms"].at[base + k], r["mr"].at[base + k], yd)

    def out_grad():
        need("dm", "sat0", "sat1")
        for h in (0, 1):
            q = cb + 2 * h
            GO[h] = (mm(ATO[q], DML[...], 1, 0) + mm(SAT[h], SD2[...], 1, 0)).astype(BF)

    act["go"] = out_grad

    tb = [2 * yb, 2 * yb + 1, 2 * (1 - yb), 3 - 2 * yb]
    mine, theirs = (pl.ds(pl.multiple_of(v * hf, hf), hf) for v in (cb, 1 - cb))

    def back(s, h):
        t = tb[s]
        if h == 0:
            need(*(("h1", "dm") if s < 2 else ("l0", "l1")))
        if s == 0 and h == 0:
            BQ[...] = jnp.zeros(BQ.shape, F32)
        at = slice(h * HD, (h + 1) * HD)
        g = DOT[t, at].astype(F32) * RI[t, h : h + 1]
        dd = jnp.sum(g * ATQ[t, at].astype(F32), axis=0, keepdims=True)
        gl = g.astype(BF)
        e = ET[t, h]
        ds = (e.astype(F32) * (mm(VT[t, at], gl, 0, 0) - dd)).astype(BF)
        dq = mm(KT[t, h, 0:HD], ds, 1, 0) * HD**-0.5
        dk = mm(QT[t, h, 0:HD], ds, 1, 1)
        dv = mm(gl, e, 1, 1)
        for i, x in enumerate((dq, dk, dv)):
            DA[t, i * hw + h * HD : i * hw + (h + 1) * HD, 0:seq] = x.astype(BF)

    def d_tokens(s):
        t = tb[s]
        g = DA[t, 0 : 3 * hw, 0:seq]
        BQ[:, 0 : 3 * hw] += mm(jnp.ones((8, seq), BF), g, 1, 1)
        dx = mm(g, WT[...], 0, 0)
        if s < 2:
            dx += jnp.where(cb == s, 1.0, 0.0) * ACC[...]
        ACT[t] = dx.astype(BF)

    def across(s):
        need("xc%d" % s, "l0", "l1")
        add_rows(ACT.at[tb[s], mine], UA.at[s, 0:hf], hf)

    def settle(s):
        o = (s + 2) % 4
        need("xy%d" % o)
        for k in ("xc%d" % s, "xy%d" % s):
            msg[k].wait_send()
            sent.discard(k)
        add_rows(ACT.at[tb[s], mine], UA.at[s, hf:seq], hf)
        loc["xt%d" % s].start()

    for s in range(4):
        for h in range(nh):
            act["ab.%d.%d" % (s, h)] = lambda s=s, h=h: back(s, h)
        act["dx.%d" % s] = lambda s=s: d_tokens(s)
        act["across.%d" % s] = lambda s=s: across(s)
        act["settle.%d" % s] = lambda s=s: settle(s)
        t = tb[s]
        part = ACT.at[t, mine]
        put("xc%d" % s, ACT.at[t, theirs], UA.at[s, 0:hf], sd)
        put("xt%d" % s, part, TG.at[t, mine], sd)
        local("xt%d" % s, part, TG.at[t, mine])
    base = len(msg)
    for s in range(4):
        o = (s + 2) % 4
        msg["xy%d" % s] = Both(
            rcopy(ACT.at[tb[s], mine], UA.at[o, hf:seq], r["ms"].at[base + s], r["mr"].at[base + o], yd),
            rcopy(ACT.at[tb[o], mine], UA.at[o, hf:seq], r["ms"].at[base + s], r["mr"].at[base + o], yd),
        )

    def qkv_grad(i):
        at = slice(i * hw, (i + 1) * hw)
        g = mm(DA[0, at, 0:seq], TOK[0], 1, 0)
        for t in range(1, 4):
            g += mm(DA[t, at, 0:seq], TOK[t], 1, 0)
        GQ[0, at] = g.astype(BF)

    for i in range(3):
        act["gq.%d" % i] = lambda i=i: qkv_grad(i)

    def view(G, base):
        def at(h, off, n):
            if isinstance(off, int):
                return G.at[h, base + off : base + off + n]
            return G.at[h, pl.ds(pl.multiple_of(base + off, 16), n)]

        return at

    def rows_of(O, base):
        def at(off, n):
            return O.at[pl.ds(pl.multiple_of(base + off, 16), n)]

        return at

    units = {}
    for j, (name, order, rows, base) in enumerate(unit_list(d, hw)):
        G, O = {"D": (GD, r["o_OD"]), "U": (GU, r["o_OU"]), "O": (GO, r["o_OO"]), "Q": (GQ, r["o_OQ"])}[name[1]]
        slots = [r["R%d%d" % (j, i)] for i in range(len(order))] + [r["X%d" % j].at[e] for e in range(nbits - 2)]
        units[name] = Unit(
            c, view(G, base), rows, order, slots, r["us"].at[j], r["ur"].at[j], rows_of(O, base), r["ul"].at[j]
        )
    dps = [c.dpeer(b) for b in range(nbits)]
    swaps = {
        "S": Swap(SG, r["SGR"], r["ws"], r["wr"], [sd, yd] + dps, 5),
        "B": Swap(BQ, r["BQR"], r["zs"], r["zr"], dps, 3),
    }

    sent = set()
    for k in SCHEDULE:
        if k in act:
            act[k]()
        elif k[0] == ">":
            w = k[1:].split(".")
            if w[0] in units:
                units[w[0]].send(int(w[1]), int(w[2]))
            elif w[0] in swaps:
                swaps[w[0]].send(int(w[1]))
            else:
                msg[k[1:]].start()
                sent.add(k[1:])
        else:
            w = k.split("/")
            (units[w[0]] if w[0] in units else swaps[w[0]]).finish(int(w[1]) - 1)

    r["o_OS"][...] = SG[...]
    r["o_OB"][...] = BQ[...]
    for k in ["v1", "v2", "v3", "sat0", "sat1", "sfl"] + [k for k in msg if k in sent]:
        msg[k].wait_send()
    need("los", "lof", "xt0", "xt1", "xt2", "xt3")
    for k in ("lo", "xt0", "xt1", "xt2", "xt3"):
        loc[k].wait()
    for u in units.values():
        u.drain()


class Both:
    def __init__(self, out, into):
        self.start, self.wait_send, self.wait_recv = out.start, out.wait_send, into.wait_recv


def unit_list(d, hw):
    res = [("GD%d" % i, o, d // len(DOWN), i * (d // len(DOWN))) for i, o in enumerate(DOWN)]
    res += [("GU%d" % i, o, d // len(UP), i * (d // len(UP))) for i, o in enumerate(UP)]
    return res + [("GO", OUT, hw, 0), ("GQ", QKV, 3 * hw, 0)]


def layer(tok4, cot4, lengths, vecs, wq, wk, wv, wo, wu, wd, nbits):
    nt, seq, d = tok4.shape
    hw = wq.shape[0]
    ff = wu.shape[1]
    nh = hw // HD
    V = pltpu.VMEM
    S = jax.ShapeDtypeStruct
    DMA = pltpu.SemaphoreType.DMA
    nex = nbits - 2
    nu = len(unit_list(d, hw))
    scratch = {
        "TOK": V((nt, seq, d), BF),
        "VEC": V((16, d), F32),
        "BC": V((3 * hw, 1), F32),
        "GQ": V((1, 3 * hw, d), BF),
        "WT": V((3 * hw, d), BF),
        "QT": V((nt, nh, HD + 16, seq), BF),
        "KT": V((nt, nh, HD + 16, seq), BF),
        "VT": V((nt, hw, seq), BF),
        "ET": V((nt, nh, seq, seq), BF),
        "RI": V((nt, 8, seq), F32),
        "ATQ": V((nt, hw, seq), BF),
        "ATO": V((nt, hw, seq), BF),
        "N1": V((seq, d), F32),
        "I1": V((seq, 1), F32),
        "FL": V((seq, d), BF),
        "ACT": V((nt, seq, ff), BF),
        "GP": V((nt, seq, ff), BF),
        "WOA": V((nt, hw, d), BF),
        "UA": V((nt, d, ff), BF),
        "DA": V((nt, ff, d), BF),
        "VA": V((nt, 16, d), F32),
        "ACC": V((seq, d), F32),
        "COT": V((seq, d), BF),
        "SA": V((2, seq, ff), BF),
        "SH": V((2, seq, ff), BF),
        "SFL": V((seq, d), BF),
        "SD2": V((seq, d), BF),
        "D2L": V((seq, d), BF),
        "SAT": V((2, hw, seq), BF),
        "DOT": V((nt, hw, seq), BF),
        "DTS": V((nt, hw, seq), BF),
        "SG": V((16, d), F32),
        "SGR": V((nbits + 2, 16, d), F32),
        "BQ": V((8, d), F32),
        "BQR": V((nbits, 8, d), F32),
        "GD": V((2, ff, d), BF),
        "GU": V((2, d, ff), BF),
        "GO": V((2, hw, d), BF),
        "ls": DMA((16,)),
        "ms": DMA((96,)),
        "mr": DMA((96,)),
        "us": DMA((nu, 8 + nex)),
        "ur": DMA((nu, 8 + nex)),
        "ul": DMA((nu,)),
        "ws": DMA((nbits + 2,)),
        "wr": DMA((nbits + 2,)),
        "zs": DMA((nbits,)),
        "zr": DMA((nbits,)),
    }
    for j, (_, order, rows, _) in enumerate(unit_list(d, hw)):
        n, h = rows, 2 if "y" in order else 1
        for i, ax in enumerate(order):
            if ax == "y":
                h = 1
            else:
                n //= 2
            scratch["R%d%d" % (j, i)] = V((h, n, d), BF)
        scratch["X%d" % j] = V((max(nex, 1), 1, n, d), BF)
    ins = {
        "len": lengths, **vecs, "tok": tok4, "cot": cot4,
        "wq": wq, "wk": wk, "wv": wv, "wo": wo, "wu": wu, "wd": wd,
    }
    A = pl.BlockSpec(memory_space=pl.ANY)
    B = pl.BlockSpec(memory_space=V)
    specs = [pl.BlockSpec(memory_space=pltpu.SMEM)] + [B] * len(vecs)
    specs += [A] * (len(ins) - len(specs))
    outs = {
        "LO": (S((nt, seq, d), BF), A),
        "TG": (S((nt, seq, d), BF), A),
        "OU": (S((d, ff), BF), A),
        "OD": (S((ff, d), BF), A),
        "OO": (S((hw, d), BF), A),
        "OQ": (S((3 * hw, d), BF), A),
        "OS": (S((16, d), F32), B),
        "OB": (S((8, d), F32), B),
    }
    names = list(ins) + ["o_" + n for n in outs] + list(scratch)

    def kernel(*refs):
        layer_kernel(nbits, names, *refs)

    res = pl.pallas_call(
        kernel,
        out_shape=[o[0] for o in outs.values()],
        in_specs=specs,
        out_specs=[o[1] for o in outs.values()],
        scratch_shapes=list(scratch.values()),
        compiler_params=pltpu.CompilerParams(
            collective_id=0, has_side_effects=True, vmem_limit_bytes=60 * 2**20
        ),
    )(*ins.values())
    return dict(zip(outs, res))


def shards(
    tokens, lengths, wq, bq, wk, wv, bv, wo, bo, g1, s1, wu, bu, wd, bd, g2, s2, cot
):
    n = lengths.shape[0]
    rows, d = tokens.shape
    seq = rows // n
    hw = wq.shape[1]
    m = lax.axis_index("mp")
    nbits = lax.axis_size("dp").bit_length() - 1
    f = lambda a: a.astype(F32)
    vecs = {
        "bo": bo, "g1": g1, "s1": s1, "bd": bd, "g2": g2, "s2": s2, "bu": bu, "bq": bq, "bv": bv
    }
    o = layer(
        tokens.reshape(n, seq, d), cot.reshape(n, seq, d), lengths, vecs, wq.T, wk.T, wv.T, wo, wu, wd, nbits
    )
    res = finish([o[k] for k in ("LO", "TG", "OU", "OD", "OO", "OQ", "OS", "OB")])
    lo, tg, du, dd, do, dq, dk, dv, dbq, dbv, dbu, dbo, dg1, ds1, dbd, dg2, ds2 = res
    return (
        lo.reshape(rows, d), tg.reshape(rows, d), dq.T, dbq, dk.T, dv.T, dbv, do, dbo, dg1, ds1,
        du, dbu, dd, dbd, dg2, ds2,
    )


def finish_kernel(*refs):
    ins, outs, bufs, wide, (si, so) = refs[:8], refs[8:25], refs[25:31], refs[31:35], refs[35:37]
    loads = []
    for i in range(2):
        loads.append([pltpu.make_async_copy(ins[i].at[t], bufs[i].at[t], si.at[i * 4 + t]) for t in range(4)])
    loads += [[pltpu.make_async_copy(ins[i], bufs[i], si.at[6 + i])] for i in range(2, 6)]
    for i in (0, 1, 2, 3, 5, 4):
        for x in loads[i]:
            x.start()
    stores = []

    def store(src, dst):
        stores.append(pltpu.make_async_copy(src, dst, so.at[len(stores)]))
        stores[-1].start()

    sg, b = ins[6], ins[7]
    m = lax.axis_index("mp")
    hw = ins[5].shape[0] // 3
    d = ins[5].shape[1]
    outs[8][...] = b[0:1, 0:hw].reshape(hw)
    outs[9][...] = b[0:1, 2 * hw : 3 * hw].reshape(hw)
    outs[10][...] = sg[pl.ds(8 + m, 1)].reshape(d)
    for i in range(6):
        outs[11 + i][...] = sg[i : i + 1].reshape(d)
    for i in range(2):
        for t in range(4):
            loads[i][t].wait()
            store(bufs[i].at[t], outs[i].at[t])
    for i in (2, 3, 5, 4):
        loads[i][0].wait()
        h = 192
        for k in range(bufs[i].shape[0] // h):
            at = slice(k * h, (k + 1) * h)
            wide[i - 2][at] = bufs[i][at].astype(F32)
            store(wide[i - 2].at[at], outs[5 + k] if i == 5 else outs[i].at[at])
    for x in stores:
        x.wait()


def finish(vals):
    S = jax.ShapeDtypeStruct
    V = pltpu.VMEM
    A = pl.BlockSpec(memory_space=pl.ANY)
    B = pl.BlockSpec(memory_space=V)
    shapes = [v.shape for v in vals]
    d = shapes[5][1]
    hw = shapes[5][0] // 3
    outs = [S(shapes[0], BF), S(shapes[1], BF)] + [S(s, F32) for s in shapes[2:5]]
    outs += [S((hw, d), F32)] * 3 + [S((hw,), F32)] * 2 + [S((d,), F32)] * 7
    return pl.pallas_call(
        finish_kernel,
        out_shape=outs,
        in_specs=[A] * 6 + [B] * 2,
        out_specs=[A] * 8 + [B] * 9,
        scratch_shapes=[V(s, BF) for s in shapes[:6]]
        + [V(s, F32) for s in shapes[2:6]]
        + [pltpu.SemaphoreType.DMA((12,)), pltpu.SemaphoreType.DMA((24,))],
        compiler_params=pltpu.CompilerParams(vmem_limit_bytes=60 * 2**20),
    )(*vals)


def solution(mesh):
    row, col, one, rep = P("dp", None), P(None, "mp"), P("mp"), P()
    low = P("mp", None)
    in_specs = (
        row, P("dp"), col, one, col, col, one, low, rep, rep, rep, col, one, low, rep, rep, rep, row,
    )
    out_specs = (
        row, row, col, one, col, col, one, low, rep, rep, rep, col, one, low, rep, rep, rep,
    )
    return jax.shard_map(shards, mesh=mesh, in_specs=in_specs, out_specs=out_specs, check_vma=False)
```

```python
import jax
import jax.numpy as jnp
from jax import lax
from jax.experimental import pallas as pl
from jax.experimental.pallas import tpu as pltpu
from jax.sharding import PartitionSpec as P

HD = 64
EPS = 1e-06
BF = jnp.bfloat16
F32 = jnp.float32
MESH = pl.DeviceIdType.MESH


DOWN = (("xzy", 192), ("zxy", 192), ("xzy", 192), ("xzy", 192),)
UP = (("xzy", 192), ("yzx", 192), ("zyx", 192), ("yzx", 192),)
OUT = "yxz"
QKV = "xz"
GATHER = ((0, 1), (1, 3), (2, 3))


class Step:
    def __init__(self, lead, join):
        self.lead, self.join = lead, join

    def __getattr__(self, name):
        return lambda *at: self.lead + name + "".join(self.join + str(a) for a in at)


step, send, end = Step("", "."), Step(">", "."), Step("", "/")
SCHEDULE = (
    step.start(), send.gy0(), send.gy1(), send.gs0(), send.gs1(), send.gs2(), step.ready(),
    step.qkv(0), step.head(0, 0), step.head(0, 1), send.gy3(), step.head(0, 2), step.qkv(1),
    send.gy4(), step.head(1, 0), step.gy(0), send.gx0(), send.gz0(), step.head(1, 1),
    step.head(1, 2), send.gy2(), step.gy(1), send.gx1(), send.gz1(), step.qkv(2), send.at1(),
    step.head(2, 0), step.gy(3), send.gz3(), send.gx3(), step.head(2, 1), step.gx(0), send.gdz0(),
    step.gz(0), send.gdx0(), step.head(2, 2), send.at2(), send.gy5(), step.gy(4), step.qkv(3),
    send.gx4(), send.gz4(), step.gx(1), step.gz(1), send.gdx1(), step.head(3, 0), send.gdz1(),
    step.head(3, 1), step.gy(2), step.head(3, 2), send.gx2(), step.gt(0), send.gt0(), step.gx(3),
    step.gz(3), send.gz2(), send.gy6(), send.gdz3(), send.gdx3(), send.at0(), step.gt(1),
    send.gt1(), step.gy(5), send.gx5(), send.gz5(), step.gz(4), step.gx(4), send.gdx4(),
    send.gdz4(), step.gt(3), send.gt3(), step.gx(2), send.gdz2(), step.gz(2), send.gdx2(),
    step.gy(6), send.gx6(), send.gz6(), step.gt(4), send.gt4(), step.gx(5), send.gdz5(),
    step.gz(5), send.gdx5(), step.proj(), step.gt(2), send.gt2(), step.norm1(), step.ffn(0, 0),
    step.gx(6), send.gdz6(), step.ffn(0, 1), step.gz(6), send.gdx6(), step.gt(5), send.gt5(),
    step.ffn(0, 2), step.down(0), step.ffn(1, 0), step.ffn(1, 1), step.ffn(1, 2), send.sa1(),
    step.down(1), step.gt(6), send.gt6(), step.ffn(2, 0), step.ffn(2, 1), step.ffn(2, 2),
    step.down(2), step.ffn(3, 0), step.ffn(3, 1), step.ffn(3, 2), send.sa3(), step.down(3),
    step.norm2(), send.d2(), send.lo(), send.los(), step.dh(1), send.sh1(), step.dh(0),
    step.gd(0), send.GD0(0, 0), send.GD0(0, 1), step.gd(1), send.GD1(0, 0), send.GD1(0, 1),
    step.gd(2), step.gd(3), step.dh(3), send.sh3(), step.dh(2), step.d1(0), send.GD2(0, 0),
    step.d1(1), send.GD2(0, 1), step.d1(2), step.d1(3), step.norm1b(), send.dm(), end.GD0(1),
    send.GD0(1, 0), send.GD0(1, 1), end.GD1(1), step.datt(1), send.h1(), step.datt(2), send.h2(),
    step.datt(3), step.datt(0), send.S(0), step.gu(2), send.GD1(1, 0), send.h3(), end.S(1),
    step.go(), send.GD1(1, 1), send.GU2(0, 1), send.GU2(0, 0), step.gu(0), step.lo_fwd(),
    send.lof(), step.gu(3), send.GU0(0, 0), end.GD0(2), end.GD2(1), send.GU0(0, 1), step.ab(0, 0),
    step.ab(0, 1), step.ab(0, 2), send.GD0(2, 0), end.GD1(2), step.dx(0), send.GD2(1, 0),
    send.xc0(), send.GD2(1, 1), step.ab(1, 0), send.GD1(2, 0), step.ab(1, 1), send.GO(0, 0),
    send.GD3(0, 0), send.GD3(0, 1), end.GU2(1), step.ab(1, 2), send.S(1), step.across(0),
    end.GD0(3), send.GD0(3, 0), step.dx(1), send.xc1(), end.GU0(1), send.GU0(1, 1), step.gu(1),
    send.GU1(0, 0), end.GD1(3), end.GD2(2), step.ab(2, 0), send.GD1(3, 0), step.across(1),
    step.ab(2, 1), send.GU0(1, 0), end.S(2), send.S(2), step.ab(2, 2), step.dx(2), send.xc2(),
    end.GD0(4), send.GD0(4, 1), send.GD0(4, 0), end.GD3(1), send.GD3(1, 0), step.ab(3, 0),
    step.ab(3, 1), end.S(3), step.across(2), send.GD2(2, 0), step.ab(3, 2), send.S(3),
    send.GD3(1, 1), end.GD1(4), send.GD1(4, 0), end.GU0(2), step.dx(3), send.xc3(), end.GO(1),
    send.GO(1, 0), step.gq(0), send.GU0(2, 0), send.GD1(4, 1), end.GD0(5), send.GD0(5, 0),
    step.gq(1), step.across(3), send.xy3(), step.gq(2), end.GD1(5), send.GD1(5, 0), end.S(4),
    send.S(4), end.GD2(3), end.GD3(2), send.xy1(), send.B(0), end.GU1(1), send.GD2(3, 0),
    send.GQ(0, 0), send.GU1(1, 0), end.GU0(3), end.GD0(6), end.B(1), end.GO(2), send.GU0(3, 0),
    end.GD1(6), end.S(5), send.GO(2, 0), end.GD2(4), send.GD2(4, 1), send.B(1), send.GD2(4, 0),
    end.GU1(2), end.GU0(4), send.GU0(4, 1), send.GU0(4, 0), end.B(2), send.B(2), end.GO(3),
    send.GO(3, 0), send.GU1(2, 0), end.GD2(5), send.GD2(5, 0), send.GU3(0, 0), end.GQ(1),
    send.GQ(1, 0), send.GD3(2, 0), end.GU0(5), send.GU0(5, 0), end.B(3), end.GU1(3),
    send.GU1(3, 0), step.settle(1), send.xt1(), step.settle(3), send.xt3(), end.GO(4),
    send.GO(4, 1), end.GD2(6), send.GU2(1, 0), end.GU0(6), send.GO(4, 0), end.GD3(3),
    send.GD3(3, 0), end.GU1(4), send.GU1(4, 1), send.GU1(4, 0), send.xy2(), end.GQ(2), send.xy0(),
    send.GQ(2, 0), end.GO(5), send.GO(5, 0), end.GU2(2), send.GU2(2, 0), end.GU3(1),
    send.GU3(1, 0), end.GU1(5), end.GD3(4), send.GD3(4, 1), end.GO(6), end.GU2(3), send.GD3(4, 0),
    send.GU2(3, 0), end.GU3(2), send.GU3(2, 0), send.GU1(5, 0), end.GQ(3), send.GQ(3, 0),
    send.GQ(3, 1), end.GD3(5), send.GD3(5, 0), end.GU3(3), send.GU3(3, 0), end.GU2(4), end.GU1(6),
    send.GU2(4, 0), step.settle(0), send.xt0(), send.GU2(4, 1), step.settle(2), send.xt2(),
    end.GD3(6), end.GU3(4), send.GU3(4, 0), send.GU3(4, 1), end.GU2(5), send.GU2(5, 0), end.GQ(4),
    send.GQ(4, 0), end.GU3(5), send.GU3(5, 0), end.GU2(6), end.GU3(6), end.GQ(5),
)


def mm(a, b, ca, cb):
    return lax.dot_general(a, b, (((ca,), (cb,)), ((), ())), preferred_element_type=F32)


def flip(v, b):
    return v + b - 2 * b * lax.rem(v // b, 2)


def gelu_pair(h):
    x = h * 0.7071067811865476
    e = jnp.exp(-(x * x))
    t = 1.0 / (1.0 + 0.3275911 * jnp.abs(x))
    poly = t * (
        0.254829592
        + t * (-0.284496736 + t * (1.421413741 + t * (-1.453152027 + t * 1.061405429)))
    )
    tail = 0.5 * poly * e
    phi = jnp.where(h > 0, 1.0 - tail, tail)
    return h * phi, phi + h * e * 0.3989422804014327


def add_rows(dst, src, n):
    step = 48 if n % 48 == 0 else 64

    def body(i, _):
        at = pl.ds(pl.multiple_of(i * step, 16), step)
        a, b = dst.at[at], src.at[at]
        a[...] = (a[...].astype(F32) + b[...].astype(F32)).astype(BF)
        return 0

    lax.fori_loop(0, n // step, body, 0)


def norm_rows(x):
    center = x - jnp.mean(x, axis=-1, keepdims=True)
    inv = lax.rsqrt(jnp.mean(center * center, axis=-1, keepdims=True) + EPS)
    return center * inv, inv


class Comm:
    def __init__(self, nbits):
        self.dp, self.mp = lax.axis_index("dp"), lax.axis_index("mp")
        self.nbits = nbits

    def mpeer(self, k):
        v = self.mp
        for b in (1, 2):
            if k & b:
                v = flip(v, b)
        return (self.dp, v)

    def dpeer(self, bit):
        return (flip(self.dp, 1 << bit), self.mp)

    def announce(self):
        bar = pltpu.get_barrier_semaphore()
        peers = [self.mpeer(k) for k in (1, 2, 3)] + [self.dpeer(b) for b in range(self.nbits)]
        for p in peers:
            pl.semaphore_signal(bar, inc=1, device_id=p, device_id_type=MESH)
        return lambda: pl.semaphore_wait(bar, len(peers))


def rcopy(src, dst, ss, rs, dev):
    return pltpu.make_async_remote_copy(
        src_ref=src, dst_ref=dst, send_sem=ss, recv_sem=rs, device_id=dev, device_id_type=MESH
    )


class Unit:
    def __init__(self, c, view, rows, order, slots, ss, rs, out, loc):
        y = c.mp // 2
        hs, own = ([0, 1], 0) if "y" in order else ([0], 0)
        off, n, k = 0, rows, 0
        spans = []

        def put(a, b, dev):
            nonlocal k
            cp = rcopy(a, b, ss.at[k], rs.at[k], dev)
            k += 1
            return cp

        self.steps = steps = []
        for i, ax in enumerate(order):
            if ax == "y":
                cps = [put(view(1 - y, off, n), slots[i].at[0], c.mpeer(2))]
                hs, own = [y], y
                adds = [(view(y, off, n), slots[i].at[0], n)]
            else:
                b = "xz".index(ax)
                bit = lax.rem(c.dp // (1 << b), 2)
                spans.append((b, off, n))
                n //= 2
                mine, theirs = off + bit * n, off + (1 - bit) * n
                cps, adds = [], []
                for j, h in enumerate(hs):
                    cps.append(put(view(h, theirs, n), slots[i].at[j], c.dpeer(b)))
                    adds.append((view(h, mine, n), slots[i].at[j], n))
                off = mine
            steps.append((cps, adds))
        mine = view(own, off, n)
        self.swaps = []
        for b in range(2, c.nbits):
            sl = slots[len(order) + b - 2].at[0]
            self.swaps.append((put(mine, sl, c.dpeer(b)), (mine, sl, n)))
        steps.append(([self.swaps[0][0]] if self.swaps else [], []))
        (b2, _, _), (b1, o1, _) = spans
        bit = lax.rem(c.dp // (1 << b1), 2)
        theirs = o1 + (1 - bit) * n
        self.local = pltpu.make_async_copy(mine, out(off, n), loc)
        first = put(mine, out(off, n), c.dpeer(b1))
        self.hold = put(mine, out(off, n), c.dpeer(b2))
        third = put(out(theirs, n), out(theirs, n), c.dpeer(b2))
        steps.append(([first, self.hold], []))
        steps.append(([third], []))

    def send(self, i, j):
        cps = self.steps[i][0]
        if j < len(cps):
            cps[j].start()

    def finish(self, i):
        cps, adds = self.steps[i]
        last = len(self.steps)
        if i == last - 3:
            for e, (cp, add) in enumerate(self.swaps):
                if e:
                    cp.start()
                cp.wait()
                add_rows(*add)
            self.local.start()
            return
        for cp in cps:
            if cp is not self.hold:
                cp.wait_recv()
        for a in adds:
            add_rows(*a)
        if i == last - 1:
            self.hold.wait_recv()

    def drain(self):
        for i, (cps, _) in enumerate(self.steps):
            if i != len(self.steps) - 3:
                for cp in cps:
                    cp.wait_send()
        self.local.wait()


class Swap:
    def __init__(self, ref, slots, ss, rs, peers, count):
        self.ref, self.slots, self.count = ref, slots, count
        self.cps = [rcopy(ref, slots.at[i], ss.at[i], rs.at[i], p) for i, p in enumerate(peers)]

    def send(self, i):
        self.cps[i].start()

    def finish(self, i):
        self.cps[i].wait()
        self.ref[...] += self.slots[i]
        if i == self.count - 1:
            for e in range(self.count, len(self.cps)):
                self.cps[e].start()
                self.cps[e].wait()
                self.ref[...] += self.slots[e]


def layer_kernel(nbits, names, *refs):
    r = dict(zip(names, refs))
    ln, vec, tok = r["len"], r["VEC"], r["tok"]
    TOK, WT, QT, KT, VT, ET, RI = (r[k] for k in ("TOK", "WT", "QT", "KT", "VT", "ET", "RI"))
    ATQ, ATO, N1, I1, FL, ACT, GP = (r[k] for k in ("ATQ", "ATO", "N1", "I1", "FL", "ACT", "GP"))
    VA, ACC, COT, SA, SFL, SAT = (r[k] for k in ("VA", "ACC", "COT", "SA", "SFL", "SAT"))
    D2L, SD2, SH, DOT, DTS, SG, BQ = (r[k] for k in ("D2L", "SD2", "SH", "DOT", "DTS", "SG", "BQ"))
    GD, GU, GO, GQ, LO, TG = (r[k] for k in ("GD", "GU", "GO", "GQ", "o_LO", "o_TG"))
    WA = WO, UA, DA = (r["WOA"], r["UA"], r["DA"])
    DML, LOB = D2L, COT
    wsrc = (r["wo"], r["wu"], r["wd"])
    c = Comm(nbits)
    m = c.mp
    cb, yb = lax.rem(m, 2), m // 2
    seq, d = TOK.shape[1], TOK.shape[2]
    hw = VT.shape[1]
    nh = hw // HD
    aug = QT.shape[2]
    hf = seq // 2
    cw = d // 3
    nr = 64
    yd, sd, xd, zd = c.mpeer(2), c.mpeer(1), c.dpeer(0), c.dpeer(1)
    qk = [c.mpeer(k)[1] for k in range(4)]
    yq = qk[2]
    f = lambda i: vec[i : i + 1]
    act, msg, loc = {}, {}, {}
    waited = set()

    def need(*ks):
        for k in ks:
            if k not in waited:
                waited.add(k)
                msg[k].wait_recv()

    def put(k, src, dst, dev):
        i = len(msg)
        msg[k] = rcopy(src, dst, r["ms"].at[i], r["mr"].at[i], dev)

    def local(k, src, dst):
        loc[k] = pltpu.make_async_copy(src, dst, r["ls"].at[len(loc)])

    ta = [qk[k] for k in (2, 3, 1, 0)]
    for i, k in enumerate(("wq", "wk", "wv")):
        local(k, r[k], WT.at[i * hw : (i + 1) * hw])
    for i in range(4):
        local("tok%d" % i, tok.at[ta[i]], TOK.at[ta[i]])
    for i in range(3):
        local("own%d" % i, wsrc[i], WA[i].at[m])
    local("cot", r["cot"].at[m], COT)
    loads = list(loc)

    x0, z0 = lax.rem(c.dp, 2), lax.rem(c.dp // 2, 2)
    pc = [x0 + 2 * z0, (1 - x0) + 2 * z0, x0 + 2 * (1 - z0)]
    parts = [(a, i, n) for a, n in GATHER for i in range(n)]
    of = lambda a: [p for p in range(len(parts)) if parts[p][0] == a]

    def gather(p):
        a, i, n = parts[p]
        W = WA[a]
        whole = W.shape[1] // n
        quarter = whole // 4

        def at(k):
            return pl.ds(pl.multiple_of(i * whole + pc[k] * quarter, 16), quarter)

        def w(k, half=None):
            if half is None:
                return W.at[yq, at(k)]
            return W.at[yq, at(k), half * (d // 2) : (half + 1) * (d // 2)]

        full = W.at[yq, i * whole : (i + 1) * whole]
        put("gy%d" % p, wsrc[a].at[at(0)], W.at[m, at(0)], yd)
        put("gx%d" % p, w(0), w(0), xd)
        put("gz%d" % p, w(0), w(0), zd)
        put("gdz%d" % p, w(1, 0), w(1, 0), zd)
        put("gdx%d" % p, w(2, 1), w(2, 1), xd)
        put("gt%d" % p, full, full, sd)
        act["gy.%d" % p] = lambda: need("gy%d" % p)
        act["gx.%d" % p] = lambda: need("gx%d" % p)
        act["gz.%d" % p] = lambda: need("gz%d" % p)
        act["gt.%d" % p] = lambda: need("gdx%d" % p, "gdz%d" % p)

    for p in range(len(parts)):
        gather(p)
    for a in range(3):
        put("gs%d" % a, wsrc[a], WA[a].at[m], sd)
    for k in (1, 2, 3):
        put("v%d" % k, vec, VA.at[m], c.mpeer(k))
    got = lambda a: ["gt%d" % p for p in of(a)]

    def start():
        everyone = c.announce()
        for k in loads:
            loc[k].start()
        vec[...] = jnp.zeros(vec.shape, F32)
        for i, k in enumerate(("bo", "g1", "s1", "bd", "g2", "s2", "bu")):
            vec[i : i + 1] = r[k][...].astype(F32).reshape(1, d)
        vec[7:8, 0:hw] = r["bq"][...].astype(F32).reshape(1, hw)
        vec[8:9, 0:hw] = r["bv"][...].astype(F32).reshape(1, hw)
        VA[m] = vec[...]
        everyone()

    def ready():
        for k in (1, 2, 3):
            msg["v%d" % k].start()
        sub = lax.broadcasted_iota(jnp.int32, (aug - HD, seq), 0)
        ones = jnp.where(sub == 0, 1.0, 0.0).astype(BF)
        cols = vec[...].T[0:hw]
        r["BC"][0:hw] = cols[:, 7:8]
        r["BC"][hw : 2 * hw] = jnp.zeros((hw, 1), F32)
        r["BC"][2 * hw : 3 * hw] = cols[:, 8:9]
        for t in range(4):
            for h in range(nh):
                QT[t, h, HD:aug] = ones
        for k in ("wq", "wk", "wv"):
            loc[k].wait()

    act["ready"] = ready
    act["start"] = start

    def qkv(s):
        t = ta[s]
        loc["tok%d" % s].wait()
        g = (mm(WT[...], TOK[t], 1, 1) + r["BC"][...]).astype(BF)
        sub = lax.broadcasted_iota(jnp.int32, (aug - HD, seq), 0)
        lane = lax.broadcasted_iota(jnp.int32, (aug - HD, seq), 1)
        dead = jnp.where(sub == 0, jnp.where(lane < ln[t], 0.0, -1e30), 0.0).astype(BF)
        for h in range(nh):
            QT[t, h, 0:HD] = g[h * HD : (h + 1) * HD] * jnp.asarray(HD**-0.5, BF)
            KT[t, h, 0:HD] = g[hw + h * HD : hw + (h + 1) * HD]
            KT[t, h, HD:aug] = dead
        VT[t] = g[2 * hw : 3 * hw]

    def head(s, h):
        t = ta[s]
        at = slice(h * HD, (h + 1) * HD)
        sc = mm(KT[t, h], QT[t, h], 0, 0)
        e = jnp.exp(sc - jnp.max(sc, axis=0, keepdims=True))
        ri = 1.0 / jnp.sum(e, axis=0, keepdims=True)
        el = e.astype(BF)
        ET[t, h] = el
        RI[t, h : h + 1] = ri
        o = (mm(VT[t, at], el, 1, 0) * ri).astype(BF)
        ATQ[t, at] = o
        if s == 3:
            ATO[m, at] = o

    for s in range(4):
        act["qkv.%d" % s] = lambda s=s: qkv(s)
        for h in range(nh):
            act["head.%d.%d" % (s, h)] = lambda s=s, h=h: head(s, h)
        if s < 3:
            put("at%d" % s, ATQ.at[ta[s]], ATO.at[m], c.mpeer((2, 3, 1)[s]))

    for h in (0, 1):
        put("sat%d" % h, ATO.at[1 - cb + 2 * h], SAT.at[h], sd)
    put("sfl", FL, SFL, sd)
    for k, h in ((1, yb), (3, 1 - yb)):
        put("sa%d" % k, ACT.at[1 - cb + 2 * h], SA.at[h], sd)

    def proj():
        need("gs0", "at0", "at1", "at2", *got(0))
        loc["own0"].wait()
        mixed = TOK[m].astype(F32) + f(0)
        for q in range(4):
            mixed += mm(ATO[q], WO[q], 0, 0)
        ACC[...] = mixed
        msg["sat0"].start()
        msg["sat1"].start()

    def norm1():
        def body(i, _):
            at = pl.ds(pl.multiple_of(i * nr, nr), nr)
            n1, i1 = norm_rows(ACC[at])
            N1[at] = n1
            I1[at] = i1
            FL[at] = (n1 * f(1) + f(2)).astype(BF)
            return 0

        lax.fori_loop(0, seq // nr, body, 0)
        msg["sfl"].start()
        need("v1", "v2", "v3")

    act["proj"], act["norm1"] = proj, norm1

    def ffn(k, j):
        if j == 0:
            if k == 0:
                loc["own1"].wait()
            elif k == 1:
                need("gs1")
            elif k == 3:
                need(*got(1))
        q = qk[k]
        at = slice(j * cw, (j + 1) * cw)
        h = mm(FL[...], UA[q, :, at], 1, 0) + VA[q, 6:7, at]
        g, gp = gelu_pair(h)
        ACT[q, :, at] = g.astype(BF)
        GP[q, :, at] = gp.astype(BF)

    def down(k):
        if k == 0:
            loc["own2"].wait()
        elif k == 1:
            need("gs2")
        elif k == 3:
            need(*got(2))
        y = mm(ACT[qk[k]], DA[qk[k]], 1, 0)
        if k == 0:
            ACC[...] = y
        else:
            ACC[...] += y

    for k in range(4):
        for j in range(3):
            act["ffn.%d.%d" % (k, j)] = lambda k=k, j=j: ffn(k, j)
        act["down.%d" % k] = lambda k=k: down(k)

    def fold(x):
        return jnp.sum(x.reshape(x.shape[0] // 8, 8, x.shape[1]), axis=0)

    zero = jnp.zeros((8, d), F32)

    def norm2():
        loc["cot"].wait()

        def body(i, sums):
            at = pl.ds(pl.multiple_of(i * nr, nr), nr)
            n2, i2 = norm_rows(N1[at] * f(1) + f(2) + ACC[at] + f(3))
            ct = COT[at].astype(F32)
            LOB[at] = (n2 * f(4) + f(5)).astype(BF)
            cg = ct * f(4)
            d2 = i2 * (
                cg
                - jnp.mean(cg, axis=-1, keepdims=True)
                - n2 * jnp.mean(cg * n2, axis=-1, keepdims=True)
            )
            ACC[at] = d2
            D2L[at] = d2.astype(BF)
            return sums[0] + fold(d2), sums[1] + fold(ct * n2), sums[2] + fold(ct)

        sums = lax.fori_loop(0, seq // nr, body, (zero,) * 3)
        SG[...] = jnp.zeros(SG.shape, F32)
        for i in range(3):
            SG[3 + i : 4 + i] = jnp.sum(sums[i], axis=0, keepdims=True)
        loc["lo"].start()

    act["norm2"] = norm2
    put("d2", D2L, SD2, sd)
    put("lo", LOB, LO.at[m], yd)
    put("los", LOB, LO.at[m], sd)
    put("lof", LO.at[yq], LO.at[yq], sd)
    local("lo", LOB, LO.at[m])
    act["lo_fwd"] = lambda: need("lo")

    def d_hidden(k):
        q = qk[k]

        def chunk(j, _):
            at = pl.ds(pl.multiple_of(j * cw, 128), cw)
            dh = (mm(D2L[...], DA[q, at, :], 1, 1) * GP[q, :, at].astype(F32)).astype(BF)
            GP[q, :, at] = dh
            SG[pl.ds(8 + q, 1), at] = jnp.sum(dh.astype(F32), axis=0, keepdims=True)
            return 0

        lax.fori_loop(0, 3, chunk, 0)

    for k in range(4):
        act["dh.%d" % k] = lambda k=k: d_hidden(k)
    put("sh1", GP.at[qk[1]], SH.at[yb], sd)
    put("sh3", GP.at[qk[3]], SH.at[1 - yb], sd)

    def down_grad(i):
        need("d2", "sa1", "sa3")
        _, at = cut(DOWN, i)

        def body(h, _):
            q = cb + 2 * h
            GD[h, at] = (mm(ACT[q, :, at], D2L[...], 0, 0) + mm(SA[h, :, at], SD2[...], 0, 0)).astype(BF)
            return 0

        lax.fori_loop(0, 2, body, 0)

    def up_grad(i):
        need("sh1", "sh3", "sfl")
        _, at = cut(UP, i)

        def body(h, _):
            q = cb + 2 * h
            GU[h, at] = (mm(FL[:, at], GP[q], 0, 0) + mm(SFL[:, at], SH[h], 0, 0)).astype(BF)
            return 0

        lax.fori_loop(0, 2, body, 0)

    for i in range(len(DOWN)):
        act["gd.%d" % i] = lambda i=i: down_grad(i)
    for i in range(len(UP)):
        act["gu.%d" % i] = lambda i=i: up_grad(i)

    def d_first(k):
        ACC[...] += mm(GP[qk[k]], UA[qk[k]], 1, 1)

    for k in range(4):
        act["d1.%d" % k] = lambda k=k: d_first(k)

    def norm1_back():
        need("sh1", "sh3")
        early = ["d2", "sh1", "sh3", "sa1", "sa3"] + ["gs%d" % a for a in range(3)]
        early += ["g%s%d" % (k, p) for k in ("x", "z", "dz", "dx", "t", "y") for p in range(len(parts))]
        for k in early:
            msg[k].wait_send()
            sent.discard(k)

        def body(i, sums):
            at = pl.ds(pl.multiple_of(i * nr, nr), nr)
            d1, n1 = ACC[at], N1[at]
            cg = d1 * f(1)
            dm = I1[at] * (
                cg
                - jnp.mean(cg, axis=-1, keepdims=True)
                - n1 * jnp.mean(cg * n1, axis=-1, keepdims=True)
            )
            ACC[at] = dm
            DML[at] = dm.astype(BF)
            return sums[0] + fold(dm), sums[1] + fold(d1 * n1), sums[2] + fold(d1)

        sums = lax.fori_loop(0, seq // nr, body, (zero,) * 3)
        for i in range(3):
            SG[i : 1 + i] = jnp.sum(sums[i], axis=0, keepdims=True)

    act["norm1b"] = norm1_back
    put("dm", DML, SD2, sd)

    def d_attended(k):
        q = qk[k]
        g = mm(WO[q], DML[...], 1, 1).astype(BF)
        if k == 0:
            DOT[m] = g
        else:
            DTS[q] = g

    for k in range(4):
        act["datt.%d" % k] = lambda k=k: d_attended(k)
    put("h1", DTS.at[qk[1]], DOT.at[m], sd)
    base = len(msg)
    for k in (2, 3):
        msg["h%d" % k] = rcopy(DTS.at[qk[k]], DOT.at[m], r["ms"].at[base + k - 2], r["mr"].at[base + cb], c.mpeer(k))
    for k in (0, 1):
        msg["l%d" % k] = rcopy(DTS.at[0], DOT.at[0], r["ms"].at[base + k], r["mr"].at[base + k], yd)

    def out_grad():
        need("dm", "sat0", "sat1")
        for h in (0, 1):
            q = cb + 2 * h
            GO[h] = (mm(ATO[q], DML[...], 1, 0) + mm(SAT[h], SD2[...], 1, 0)).astype(BF)

    act["go"] = out_grad

    tb = [2 * yb, 2 * yb + 1, 2 * (1 - yb), 3 - 2 * yb]
    mine, theirs = (pl.ds(pl.multiple_of(v * hf, hf), hf) for v in (cb, 1 - cb))

    def back(s, h):
        t = tb[s]
        if h == 0:
            need(*(("h1", "dm") if s < 2 else ("l0", "l1")))
        if s == 0 and h == 0:
            BQ[...] = jnp.zeros(BQ.shape, F32)
        at = slice(h * HD, (h + 1) * HD)
        g = DOT[t, at].astype(F32) * RI[t, h : h + 1]
        dd = jnp.sum(g * ATQ[t, at].astype(F32), axis=0, keepdims=True)
        gl = g.astype(BF)
        e = ET[t, h]
        ds = (e.astype(F32) * (mm(VT[t, at], gl, 0, 0) - dd)).astype(BF)
        dq = mm(KT[t, h, 0:HD], ds, 1, 0) * HD**-0.5
        dk = mm(QT[t, h, 0:HD], ds, 1, 1)
        dv = mm(gl, e, 1, 1)
        for i, x in enumerate((dq, dk, dv)):
            DA[t, i * hw + h * HD : i * hw + (h + 1) * HD, 0:seq] = x.astype(BF)

    def d_tokens(s):
        t = tb[s]
        g = DA[t, 0 : 3 * hw, 0:seq]
        BQ[:, 0 : 3 * hw] += mm(jnp.ones((8, seq), BF), g, 1, 1)
        dx = mm(g, WT[...], 0, 0)
        if s < 2:
            dx += jnp.where(cb == s, 1.0, 0.0) * ACC[...]
        ACT[t] = dx.astype(BF)

    def across(s):
        need("xc%d" % s, "l0", "l1")
        add_rows(ACT.at[tb[s], mine], UA.at[s, 0:hf], hf)

    def settle(s):
        o = (s + 2) % 4
        need("xy%d" % o)
        for k in ("xc%d" % s, "xy%d" % s):
            msg[k].wait_send()
            sent.discard(k)
        add_rows(ACT.at[tb[s], mine], UA.at[s, hf:seq], hf)
        loc["xt%d" % s].start()

    for s in range(4):
        for h in range(nh):
            act["ab.%d.%d" % (s, h)] = lambda s=s, h=h: back(s, h)
        act["dx.%d" % s] = lambda s=s: d_tokens(s)
        act["across.%d" % s] = lambda s=s: across(s)
        act["settle.%d" % s] = lambda s=s: settle(s)
        t = tb[s]
        part = ACT.at[t, mine]
        put("xc%d" % s, ACT.at[t, theirs], UA.at[s, 0:hf], sd)
        put("xt%d" % s, part, TG.at[t, mine], sd)
        local("xt%d" % s, part, TG.at[t, mine])
    base = len(msg)
    for s in range(4):
        o = (s + 2) % 4
        msg["xy%d" % s] = Both(
            rcopy(ACT.at[tb[s], mine], UA.at[o, hf:seq], r["ms"].at[base + s], r["mr"].at[base + o], yd),
            rcopy(ACT.at[tb[o], mine], UA.at[o, hf:seq], r["ms"].at[base + s], r["mr"].at[base + o], yd),
        )

    def qkv_grad(i):
        at = slice(i * hw, (i + 1) * hw)
        g = mm(DA[0, at, 0:seq], TOK[0], 1, 0)
        for t in range(1, 4):
            g += mm(DA[t, at, 0:seq], TOK[t], 1, 0)
        GQ[0, at] = g.astype(BF)

    for i in range(3):
        act["gq.%d" % i] = lambda i=i: qkv_grad(i)

    def view(G, base):
        def at(h, off, n):
            if isinstance(off, int):
                return G.at[h, base + off : base + off + n]
            return G.at[h, pl.ds(pl.multiple_of(base + off, 16), n)]

        return at

    def rows_of(O, base):
        def at(off, n):
            return O.at[pl.ds(pl.multiple_of(base + off, 16), n)]

        return at

    units = {}
    for j, (name, order, rows, base) in enumerate(unit_list(d, hw)):
        G, O = {"D": (GD, r["o_OD"]), "U": (GU, r["o_OU"]), "O": (GO, r["o_OO"]), "Q": (GQ, r["o_OQ"])}[name[1]]
        slots = [r["R%d%d" % (j, i)] for i in range(len(order))] + [r["X%d" % j].at[e] for e in range(nbits - 2)]
        units[name] = Unit(
            c, view(G, base), rows, order, slots, r["us"].at[j], r["ur"].at[j], rows_of(O, base), r["ul"].at[j]
        )
    dps = [c.dpeer(b) for b in range(nbits)]
    swaps = {
        "S": Swap(SG, r["SGR"], r["ws"], r["wr"], [sd, yd] + dps, 5),
        "B": Swap(BQ, r["BQR"], r["zs"], r["zr"], dps, 3),
    }

    sent = set()
    for k in SCHEDULE:
        if k in act:
            act[k]()
        elif k[0] == ">":
            w = k[1:].split(".")
            if w[0] in units:
                units[w[0]].send(int(w[1]), int(w[2]))
            elif w[0] in swaps:
                swaps[w[0]].send(int(w[1]))
            else:
                msg[k[1:]].start()
                sent.add(k[1:])
        else:
            w = k.split("/")
            (units[w[0]] if w[0] in units else swaps[w[0]]).finish(int(w[1]) - 1)

    r["o_OS"][...] = SG[...]
    r["o_OB"][...] = BQ[...]
    for k in ["v1", "v2", "v3", "sat0", "sat1", "sfl"] + [k for k in msg if k in sent]:
        msg[k].wait_send()
    need("los", "lof", "xt0", "xt1", "xt2", "xt3")
    for k in ("lo", "xt0", "xt1", "xt2", "xt3"):
        loc[k].wait()
    for u in units.values():
        u.drain()


class Both:
    def __init__(self, out, into):
        self.start, self.wait_send, self.wait_recv = out.start, out.wait_send, into.wait_recv


def cut(parts, i):
    base = sum(n for _, n in parts[:i])
    return parts[i][0], slice(base, base + parts[i][1])


def unit_list(d, hw):
    assert sum(n for _, n in DOWN) == d and sum(n for _, n in UP) == d
    res = []
    for name, parts in (("GD", DOWN), ("GU", UP)):
        for i in range(len(parts)):
            o, at = cut(parts, i)
            res.append((name + str(i), o, at.stop - at.start, at.start))
    return res + [("GO", OUT, hw, 0), ("GQ", QKV, 3 * hw, 0)]


def layer(tok4, cot4, lengths, vecs, wq, wk, wv, wo, wu, wd, nbits):
    nt, seq, d = tok4.shape
    hw = wq.shape[0]
    ff = wu.shape[1]
    nh = hw // HD
    V = pltpu.VMEM
    S = jax.ShapeDtypeStruct
    DMA = pltpu.SemaphoreType.DMA
    nex = nbits - 2
    nu = len(unit_list(d, hw))
    scratch = {
        "TOK": V((nt, seq, d), BF),
        "VEC": V((16, d), F32),
        "BC": V((3 * hw, 1), F32),
        "GQ": V((1, 3 * hw, d), BF),
        "WT": V((3 * hw, d), BF),
        "QT": V((nt, nh, HD + 16, seq), BF),
        "KT": V((nt, nh, HD + 16, seq), BF),
        "VT": V((nt, hw, seq), BF),
        "ET": V((nt, nh, seq, seq), BF),
        "RI": V((nt, 8, seq), F32),
        "ATQ": V((nt, hw, seq), BF),
        "ATO": V((nt, hw, seq), BF),
        "N1": V((seq, d), F32),
        "I1": V((seq, 1), F32),
        "FL": V((seq, d), BF),
        "ACT": V((nt, seq, ff), BF),
        "GP": V((nt, seq, ff), BF),
        "WOA": V((nt, hw, d), BF),
        "UA": V((nt, d, ff), BF),
        "DA": V((nt, ff, d), BF),
        "VA": V((nt, 16, d), F32),
        "ACC": V((seq, d), F32),
        "COT": V((seq, d), BF),
        "SA": V((2, seq, ff), BF),
        "SH": V((2, seq, ff), BF),
        "SFL": V((seq, d), BF),
        "SD2": V((seq, d), BF),
        "D2L": V((seq, d), BF),
        "SAT": V((2, hw, seq), BF),
        "DOT": V((nt, hw, seq), BF),
        "DTS": V((nt, hw, seq), BF),
        "SG": V((16, d), F32),
        "SGR": V((nbits + 2, 16, d), F32),
        "BQ": V((8, d), F32),
        "BQR": V((nbits, 8, d), F32),
        "GD": V((2, ff, d), BF),
        "GU": V((2, d, ff), BF),
        "GO": V((2, hw, d), BF),
        "ls": DMA((16,)),
        "ms": DMA((96,)),
        "mr": DMA((96,)),
        "us": DMA((nu, 8 + nex)),
        "ur": DMA((nu, 8 + nex)),
        "ul": DMA((nu,)),
        "ws": DMA((nbits + 2,)),
        "wr": DMA((nbits + 2,)),
        "zs": DMA((nbits,)),
        "zr": DMA((nbits,)),
    }
    for j, (_, order, rows, _) in enumerate(unit_list(d, hw)):
        n, h = rows, 2 if "y" in order else 1
        for i, ax in enumerate(order):
            if ax == "y":
                h = 1
            else:
                n //= 2
            scratch["R%d%d" % (j, i)] = V((h, n, d), BF)
        scratch["X%d" % j] = V((max(nex, 1), 1, n, d), BF)
    ins = {
        "len": lengths, **vecs, "tok": tok4, "cot": cot4,
        "wq": wq, "wk": wk, "wv": wv, "wo": wo, "wu": wu, "wd": wd,
    }
    A = pl.BlockSpec(memory_space=pl.ANY)
    B = pl.BlockSpec(memory_space=V)
    specs = [pl.BlockSpec(memory_space=pltpu.SMEM)] + [B] * len(vecs)
    specs += [A] * (len(ins) - len(specs))
    outs = {
        "LO": (S((nt, seq, d), BF), A),
        "TG": (S((nt, seq, d), BF), A),
        "OU": (S((d, ff), BF), A),
        "OD": (S((ff, d), BF), A),
        "OO": (S((hw, d), BF), A),
        "OQ": (S((3 * hw, d), BF), A),
        "OS": (S((16, d), F32), B),
        "OB": (S((8, d), F32), B),
    }
    names = list(ins) + ["o_" + n for n in outs] + list(scratch)

    def kernel(*refs):
        layer_kernel(nbits, names, *refs)

    res = pl.pallas_call(
        kernel,
        out_shape=[o[0] for o in outs.values()],
        in_specs=specs,
        out_specs=[o[1] for o in outs.values()],
        scratch_shapes=list(scratch.values()),
        compiler_params=pltpu.CompilerParams(
            collective_id=0, has_side_effects=True, vmem_limit_bytes=60 * 2**20
        ),
    )(*ins.values())
    return dict(zip(outs, res))


def shards(
    tokens, lengths, wq, bq, wk, wv, bv, wo, bo, g1, s1, wu, bu, wd, bd, g2, s2, cot
):
    n = lengths.shape[0]
    rows, d = tokens.shape
    seq = rows // n
    hw = wq.shape[1]
    m = lax.axis_index("mp")
    nbits = lax.axis_size("dp").bit_length() - 1
    f = lambda a: a.astype(F32)
    vecs = {
        "bo": bo, "g1": g1, "s1": s1, "bd": bd, "g2": g2, "s2": s2, "bu": bu, "bq": bq, "bv": bv
    }
    o = layer(
        tokens.reshape(n, seq, d), cot.reshape(n, seq, d), lengths, vecs, wq.T, wk.T, wv.T, wo, wu, wd, nbits
    )
    res = finish([o[k] for k in ("LO", "TG", "OU", "OD", "OO", "OQ", "OS", "OB")])
    lo, tg, du, dd, do, dq, dk, dv, dbq, dbv, dbu, dbo, dg1, ds1, dbd, dg2, ds2 = res
    return (
        lo.reshape(rows, d), tg.reshape(rows, d), dq.T, dbq, dk.T, dv.T, dbv, do, dbo, dg1, ds1,
        du, dbu, dd, dbd, dg2, ds2,
    )


def finish_kernel(*refs):
    ins, outs, bufs, wide, (si, so) = refs[:8], refs[8:25], refs[25:31], refs[31:35], refs[35:37]
    loads = []
    for i in range(2):
        loads.append([pltpu.make_async_copy(ins[i].at[t], bufs[i].at[t], si.at[i * 4 + t]) for t in range(4)])
    loads += [[pltpu.make_async_copy(ins[i], bufs[i], si.at[6 + i])] for i in range(2, 6)]
    for i in (0, 1, 2, 3, 5, 4):
        for x in loads[i]:
            x.start()
    stores = []

    def store(src, dst):
        stores.append(pltpu.make_async_copy(src, dst, so.at[len(stores)]))
        stores[-1].start()

    sg, b = ins[6], ins[7]
    m = lax.axis_index("mp")
    hw = ins[5].shape[0] // 3
    d = ins[5].shape[1]
    outs[8][...] = b[0:1, 0:hw].reshape(hw)
    outs[9][...] = b[0:1, 2 * hw : 3 * hw].reshape(hw)
    outs[10][...] = sg[pl.ds(8 + m, 1)].reshape(d)
    for i in range(6):
        outs[11 + i][...] = sg[i : i + 1].reshape(d)
    for i in range(2):
        for t in range(4):
            loads[i][t].wait()
            store(bufs[i].at[t], outs[i].at[t])
    for i in (2, 3, 5, 4):
        loads[i][0].wait()
        h = 192
        for k in range(bufs[i].shape[0] // h):
            at = slice(k * h, (k + 1) * h)
            wide[i - 2][at] = bufs[i][at].astype(F32)
            store(wide[i - 2].at[at], outs[5 + k] if i == 5 else outs[i].at[at])
    for x in stores:
        x.wait()


def finish(vals):
    S = jax.ShapeDtypeStruct
    V = pltpu.VMEM
    A = pl.BlockSpec(memory_space=pl.ANY)
    B = pl.BlockSpec(memory_space=V)
    shapes = [v.shape for v in vals]
    d = shapes[5][1]
    hw = shapes[5][0] // 3
    outs = [S(shapes[0], BF), S(shapes[1], BF)] + [S(s, F32) for s in shapes[2:5]]
    outs += [S((hw, d), F32)] * 3 + [S((hw,), F32)] * 2 + [S((d,), F32)] * 7
    return pl.pallas_call(
        finish_kernel,
        out_shape=outs,
        in_specs=[A] * 6 + [B] * 2,
        out_specs=[A] * 8 + [B] * 9,
        scratch_shapes=[V(s, BF) for s in shapes[:6]]
        + [V(s, F32) for s in shapes[2:6]]
        + [pltpu.SemaphoreType.DMA((12,)), pltpu.SemaphoreType.DMA((24,))],
        compiler_params=pltpu.CompilerParams(vmem_limit_bytes=60 * 2**20),
    )(*vals)


def solution(mesh):
    row, col, one, rep = P("dp", None), P(None, "mp"), P("mp"), P()
    low = P("mp", None)
    in_specs = (
        row, P("dp"), col, one, col, col, one, low, rep, rep, rep, col, one, low, rep, rep, rep, row,
    )
    out_specs = (
        row, row, col, one, col, col, one, low, rep, rep, rep, col, one, low, rep, rep, rep,
    )
    return jax.shard_map(shards, mesh=mesh, in_specs=in_specs, out_specs=out_specs, check_vma=False)
```

```python
import jax
import jax.numpy as jnp
from jax import lax
from jax.experimental import pallas as pl
from jax.experimental.pallas import tpu as pltpu
from jax.sharding import PartitionSpec as P

HD = 64
EPS = 1e-06
BF = jnp.bfloat16
F32 = jnp.float32
MESH = pl.DeviceIdType.MESH


DOWN = (("zyx", 192), ("zxy", 192), ("xzy", 384),)
UP = (("zxy", 192), ("zxy", 192), ("xzy", 192), ("xyz", 192),)
OUT = "zyx"
QKV = "xz"
GATHER = ((0, 1), (1, 2), (2, 3))


class Step:
    def __init__(self, lead, join):
        self.lead, self.join = lead, join

    def __getattr__(self, name):
        return lambda *at: self.lead + name + "".join(self.join + str(a) for a in at)


step, send, end = Step("", "."), Step(">", "."), Step("", "/")
SCHEDULE = (
    step.start(), send.gy2(), send.gy0(), send.gs0(), send.gs2(), send.gs1(), step.ready(),
    step.qkv(0), step.head(0, 0), step.head(0, 1), step.head(0, 2), send.gy5(), step.qkv(1),
    step.head(1, 0), send.gy1(), step.head(1, 1), step.gy(0), send.gx0(), send.gz0(),
    step.head(1, 2), step.qkv(2), send.at1(), step.gy(2), send.gx2(), send.gz2(), step.head(2, 0),
    step.head(2, 1), step.head(2, 2), send.at2(), step.gx(0), send.gdz0(), step.gz(0),
    send.gdx0(), step.gy(5), step.qkv(3), send.gx5(), send.gy3(), send.gz5(), step.head(3, 0),
    step.head(3, 1), step.head(3, 2), step.gy(1), send.gx1(), send.gz1(), step.gx(2), send.gdz2(),
    step.gz(2), send.gdx2(), step.gt(0), send.gt0(), send.at0(), send.gy4(), step.gx(5),
    step.gz(5), send.gdz5(), send.gdx5(), step.gy(3), send.gz3(), send.gx3(), step.gt(2),
    send.gt2(), step.gt(5), send.gt5(), step.gy(4), send.gx4(), send.gz4(), step.gx(1),
    send.gdz1(), step.gz(1), send.gdx1(), step.gx(3), step.gz(3), step.proj(), send.gdz3(),
    step.norm1(), send.gdx3(), step.ffn(0, 0), step.ffn(0, 1), step.ffn(0, 2), step.down(0),
    step.gt(1), send.gt1(), step.gx(4), send.gdz4(), step.gz(4), send.gdx4(), step.ffn(1, 0),
    step.ffn(1, 1), step.ffn(1, 2), send.sa1(), step.gt(3), send.gt3(), step.down(1),
    step.ffn(2, 0), step.ffn(2, 1), step.ffn(2, 2), step.gt(4), send.gt4(), step.down(2),
    step.ffn(3, 0), step.ffn(3, 1), step.ffn(3, 2), send.sa3(), step.down(3), step.norm2(),
    send.d2(), send.los(), send.lo(), step.dh(1), send.sh1(), step.dh(0), step.gd(0),
    send.GD0(0, 0), send.GD0(0, 1), step.gd(1), step.gd(2), send.GD2(0, 1), send.GD2(0, 0),
    step.dh(3), send.sh3(), step.dh(2), send.GD1(0, 0), send.GD1(0, 1), step.gu(1), step.d1(0),
    step.d1(1), end.GD0(1), send.GD0(1, 0), step.d1(2), step.d1(3), step.norm1b(), send.dm(),
    step.datt(1), send.h1(), step.datt(2), send.GU1(0, 0), send.GU1(0, 1), step.datt(3),
    step.datt(0), send.S(0), step.gu(3), send.h2(), step.gu(0), send.h3(), end.S(1), end.GD1(1),
    send.GU3(0, 0), send.GU3(0, 1), step.gu(2), step.lo_fwd(), send.lof(), step.ab(0, 0),
    end.GD0(2), step.ab(0, 1), send.GU0(0, 1), send.GU0(0, 0), end.GD2(1), step.ab(0, 2),
    step.dx(0), send.xc0(), end.GU1(1), step.go(), send.GU2(0, 1), send.GU2(0, 0), send.S(1),
    step.ab(1, 0), step.ab(1, 1), end.GU3(1), send.GU3(1, 0), step.ab(1, 2), send.GD2(1, 0),
    send.GD2(1, 1), step.across(0), send.xy0(), step.dx(1), send.xc1(), end.S(2), step.ab(2, 0),
    end.GU0(1), send.GD0(2, 0), send.S(2), step.ab(2, 1), step.across(1), send.xy1(),
    step.ab(2, 2), send.GU1(1, 0), step.dx(2), send.xc2(), send.GO(0, 1), send.GU1(1, 1),
    send.GO(0, 0), end.GU3(2), end.GU2(1), step.ab(3, 0), send.GD1(1, 0), end.S(3), step.ab(3, 1),
    step.across(2), send.GD1(1, 1), end.GD0(3), end.GD2(2), step.ab(3, 2), step.dx(3), send.xc3(),
    send.GU0(1, 1), step.gq(0), send.GU0(1, 0), end.GU1(2), send.GU3(2, 0), step.gq(1),
    send.GD0(3, 0), step.gq(2), step.across(3), send.B(0), end.GD1(2), send.GU2(1, 0),
    send.GQ(0, 0), end.GO(1), send.S(3), send.xy2(), end.GU3(3), end.B(1), end.GU0(2),
    send.GU3(3, 0), send.B(1), send.GU2(1, 1), end.GD0(4), send.GD0(4, 0), send.GU1(2, 0),
    end.S(4), send.GD0(4, 1), end.B(2), send.B(2), send.S(4), send.GD2(2, 0), end.GU3(4),
    send.GU3(4, 0), send.GU3(4, 1), end.GU2(2), end.GD0(5), send.GD0(5, 0), end.GU1(3), end.B(3),
    send.GU1(3, 0), end.S(5), end.GQ(1), send.GU2(2, 0), send.GQ(1, 0), end.GU3(5),
    send.GU3(5, 0), end.GD0(6), end.GD2(3), send.GD2(3, 0), send.GU0(2, 0), send.GO(1, 0),
    end.GU1(4), send.GU1(4, 0), end.GU3(6), step.settle(0), send.xt0(), step.settle(2),
    send.xt2(), send.GD1(2, 0), end.GU2(3), send.GU2(3, 0), end.GU1(5), end.GU0(3), send.xy3(),
    send.GU1(5, 0), end.GQ(2), end.GD1(3), send.GQ(2, 0), end.GO(2), send.GO(2, 0),
    send.GU1(4, 1), end.GD2(4), send.GD2(4, 1), end.GU2(4), send.GU2(4, 1), send.GU2(4, 0),
    end.GO(3), end.GU1(6), send.GD2(4, 0), step.settle(1), send.xt1(), step.settle(3), send.xt3(),
    send.GD1(3, 0), end.GU2(5), send.GU2(5, 0), send.GO(3, 0), end.GQ(3), send.GQ(3, 1),
    send.GQ(3, 0), end.GU2(6), send.GU0(3, 0), end.GD1(4), send.GD1(4, 0), end.GD2(5),
    send.GD1(4, 1), end.GO(4), send.GD2(5, 0), send.GO(4, 0), end.GD1(5), send.GD1(5, 0),
    end.GU0(4), send.GU0(4, 0), send.GO(4, 1), end.GO(5), send.GU0(4, 1), end.GQ(4),
    send.GQ(4, 0), send.GO(5, 0), end.GD1(6), end.GD2(6), end.GU0(5), send.GU0(5, 0), end.GO(6),
    end.GQ(5), end.GU0(6),
)


def mm(a, b, ca, cb):
    return lax.dot_general(a, b, (((ca,), (cb,)), ((), ())), preferred_element_type=F32)


def flip(v, b):
    return v + b - 2 * b * lax.rem(v // b, 2)


def gelu_pair(h):
    x = h * 0.7071067811865476
    e = jnp.exp(-(x * x))
    t = 1.0 / (1.0 + 0.3275911 * jnp.abs(x))
    poly = t * (
        0.254829592
        + t * (-0.284496736 + t * (1.421413741 + t * (-1.453152027 + t * 1.061405429)))
    )
    tail = 0.5 * poly * e
    phi = jnp.where(h > 0, 1.0 - tail, tail)
    return h * phi, phi + h * e * 0.3989422804014327


def add_rows(dst, src, n):
    step = 48 if n % 48 == 0 else 64

    def body(i, _):
        at = pl.ds(pl.multiple_of(i * step, 16), step)
        a, b = dst.at[at], src.at[at]
        a[...] = (a[...].astype(F32) + b[...].astype(F32)).astype(BF)
        return 0

    lax.fori_loop(0, n // step, body, 0)


def norm_rows(x):
    center = x - jnp.mean(x, axis=-1, keepdims=True)
    inv = lax.rsqrt(jnp.mean(center * center, axis=-1, keepdims=True) + EPS)
    return center * inv, inv


class Comm:
    def __init__(self, nbits):
        self.dp, self.mp = lax.axis_index("dp"), lax.axis_index("mp")
        self.nbits = nbits

    def mpeer(self, k):
        v = self.mp
        for b in (1, 2):
            if k & b:
                v = flip(v, b)
        return (self.dp, v)

    def dpeer(self, bit):
        return (flip(self.dp, 1 << bit), self.mp)

    def announce(self):
        bar = pltpu.get_barrier_semaphore()
        peers = [self.mpeer(k) for k in (1, 2, 3)] + [self.dpeer(b) for b in range(self.nbits)]
        for p in peers:
            pl.semaphore_signal(bar, inc=1, device_id=p, device_id_type=MESH)
        return lambda: pl.semaphore_wait(bar, len(peers))


def rcopy(src, dst, ss, rs, dev):
    return pltpu.make_async_remote_copy(
        src_ref=src, dst_ref=dst, send_sem=ss, recv_sem=rs, device_id=dev, device_id_type=MESH
    )


class Unit:
    def __init__(self, c, view, rows, order, slots, ss, rs, out, loc):
        y = c.mp // 2
        hs, own = ([0, 1], 0) if "y" in order else ([0], 0)
        off, n, k = 0, rows, 0
        spans = []

        def put(a, b, dev):
            nonlocal k
            cp = rcopy(a, b, ss.at[k], rs.at[k], dev)
            k += 1
            return cp

        self.steps = steps = []
        for i, ax in enumerate(order):
            if ax == "y":
                cps = [put(view(1 - y, off, n), slots[i].at[0], c.mpeer(2))]
                hs, own = [y], y
                adds = [(view(y, off, n), slots[i].at[0], n)]
            else:
                b = "xz".index(ax)
                bit = lax.rem(c.dp // (1 << b), 2)
                spans.append((b, off, n))
                n //= 2
                mine, theirs = off + bit * n, off + (1 - bit) * n
                cps, adds = [], []
                for j, h in enumerate(hs):
                    cps.append(put(view(h, theirs, n), slots[i].at[j], c.dpeer(b)))
                    adds.append((view(h, mine, n), slots[i].at[j], n))
                off = mine
            steps.append((cps, adds))
        mine = view(own, off, n)
        self.swaps = []
        for b in range(2, c.nbits):
            sl = slots[len(order) + b - 2].at[0]
            self.swaps.append((put(mine, sl, c.dpeer(b)), (mine, sl, n)))
        steps.append(([self.swaps[0][0]] if self.swaps else [], []))
        (b2, _, _), (b1, o1, _) = spans
        bit = lax.rem(c.dp // (1 << b1), 2)
        theirs = o1 + (1 - bit) * n
        self.local = pltpu.make_async_copy(mine, out(off, n), loc)
        first = put(mine, out(off, n), c.dpeer(b1))
        self.hold = put(mine, out(off, n), c.dpeer(b2))
        third = put(out(theirs, n), out(theirs, n), c.dpeer(b2))
        steps.append(([first, self.hold], []))
        steps.append(([third], []))

    def send(self, i, j):
        cps = self.steps[i][0]
        if j < len(cps):
            cps[j].start()

    def finish(self, i):
        cps, adds = self.steps[i]
        last = len(self.steps)
        if i == last - 3:
            for e, (cp, add) in enumerate(self.swaps):
                if e:
                    cp.start()
                cp.wait()
                add_rows(*add)
            self.local.start()
            return
        for cp in cps:
            if cp is not self.hold:
                cp.wait_recv()
        for a in adds:
            add_rows(*a)
        if i == last - 1:
            self.hold.wait_recv()

    def drain(self):
        for i, (cps, _) in enumerate(self.steps):
            if i != len(self.steps) - 3:
                for cp in cps:
                    cp.wait_send()
        self.local.wait()


class Swap:
    def __init__(self, ref, slots, ss, rs, peers, count):
        self.ref, self.slots, self.count = ref, slots, count
        self.cps = [rcopy(ref, slots.at[i], ss.at[i], rs.at[i], p) for i, p in enumerate(peers)]

    def send(self, i):
        self.cps[i].start()

    def finish(self, i):
        self.cps[i].wait()
        self.ref[...] += self.slots[i]
        if i == self.count - 1:
            for e in range(self.count, len(self.cps)):
                self.cps[e].start()
                self.cps[e].wait()
                self.ref[...] += self.slots[e]


def layer_kernel(nbits, names, *refs):
    r = dict(zip(names, refs))
    ln, vec, tok = r["len"], r["VEC"], r["tok"]
    TOK, WT, QT, KT, VT, ET, RI = (r[k] for k in ("TOK", "WT", "QT", "KT", "VT", "ET", "RI"))
    ATQ, ATO, N1, I1, FL, ACT, GP = (r[k] for k in ("ATQ", "ATO", "N1", "I1", "FL", "ACT", "GP"))
    VA, ACC, COT, SA, SFL, SAT = (r[k] for k in ("VA", "ACC", "COT", "SA", "SFL", "SAT"))
    D2L, SD2, SH, DOT, DTS, SG, BQ = (r[k] for k in ("D2L", "SD2", "SH", "DOT", "DTS", "SG", "BQ"))
    GD, GU, GO, GQ, LO, TG = (r[k] for k in ("GD", "GU", "GO", "GQ", "o_LO", "o_TG"))
    WA = WO, UA, DA = (r["WOA"], r["UA"], r["DA"])
    DML, LOB = D2L, COT
    wsrc = (r["wo"], r["wu"], r["wd"])
    c = Comm(nbits)
    m = c.mp
    cb, yb = lax.rem(m, 2), m // 2
    seq, d = TOK.shape[1], TOK.shape[2]
    hw = VT.shape[1]
    nh = hw // HD
    aug = QT.shape[2]
    hf = seq // 2
    cw = d // 3
    nr = 64
    yd, sd, xd, zd = c.mpeer(2), c.mpeer(1), c.dpeer(0), c.dpeer(1)
    qk = [c.mpeer(k)[1] for k in range(4)]
    yq = qk[2]
    f = lambda i: vec[i : i + 1]
    act, msg, loc = {}, {}, {}
    waited = set()

    def need(*ks):
        for k in ks:
            if k not in waited:
                waited.add(k)
                msg[k].wait_recv()

    def put(k, src, dst, dev):
        i = len(msg)
        msg[k] = rcopy(src, dst, r["ms"].at[i], r["mr"].at[i], dev)

    def local(k, src, dst):
        loc[k] = pltpu.make_async_copy(src, dst, r["ls"].at[len(loc)])

    ta = [qk[k] for k in (2, 3, 1, 0)]
    for i, k in enumerate(("wq", "wk", "wv")):
        local(k, r[k], WT.at[i * hw : (i + 1) * hw])
    for i in range(4):
        local("tok%d" % i, tok.at[ta[i]], TOK.at[ta[i]])
    for i in range(3):
        local("own%d" % i, wsrc[i], WA[i].at[m])
    local("cot", r["cot"].at[m], COT)
    loads = list(loc)

    x0, z0 = lax.rem(c.dp, 2), lax.rem(c.dp // 2, 2)
    pc = [x0 + 2 * z0, (1 - x0) + 2 * z0, x0 + 2 * (1 - z0)]
    parts = [(a, i, n) for a, n in GATHER for i in range(n)]
    of = lambda a: [p for p in range(len(parts)) if parts[p][0] == a]

    def gather(p):
        a, i, n = parts[p]
        W = WA[a]
        whole = W.shape[1] // n
        quarter = whole // 4

        def at(k):
            return pl.ds(pl.multiple_of(i * whole + pc[k] * quarter, 16), quarter)

        def w(k, half=None):
            if half is None:
                return W.at[yq, at(k)]
            return W.at[yq, at(k), half * (d // 2) : (half + 1) * (d // 2)]

        full = W.at[yq, i * whole : (i + 1) * whole]
        put("gy%d" % p, wsrc[a].at[at(0)], W.at[m, at(0)], yd)
        put("gx%d" % p, w(0), w(0), xd)
        put("gz%d" % p, w(0), w(0), zd)
        put("gdz%d" % p, w(1, 0), w(1, 0), zd)
        put("gdx%d" % p, w(2, 1), w(2, 1), xd)
        put("gt%d" % p, full, full, sd)
        act["gy.%d" % p] = lambda: need("gy%d" % p)
        act["gx.%d" % p] = lambda: need("gx%d" % p)
        act["gz.%d" % p] = lambda: need("gz%d" % p)
        act["gt.%d" % p] = lambda: need("gdx%d" % p, "gdz%d" % p)

    for p in range(len(parts)):
        gather(p)
    for a in range(3):
        put("gs%d" % a, wsrc[a], WA[a].at[m], sd)
    for k in (1, 2, 3):
        put("v%d" % k, vec, VA.at[m], c.mpeer(k))
    got = lambda a: ["gt%d" % p for p in of(a)]

    def start():
        everyone = c.announce()
        for k in loads:
            loc[k].start()
        vec[...] = jnp.zeros(vec.shape, F32)
        for i, k in enumerate(("bo", "g1", "s1", "bd", "g2", "s2", "bu")):
            vec[i : i + 1] = r[k][...].astype(F32).reshape(1, d)
        vec[7:8, 0:hw] = r["bq"][...].astype(F32).reshape(1, hw)
        vec[8:9, 0:hw] = r["bv"][...].astype(F32).reshape(1, hw)
        VA[m] = vec[...]
        everyone()

    def ready():
        for k in (1, 2, 3):
            msg["v%d" % k].start()
        sub = lax.broadcasted_iota(jnp.int32, (aug - HD, seq), 0)
        ones = jnp.where(sub == 0, 1.0, 0.0).astype(BF)
        cols = vec[...].T[0:hw]
        r["BC"][0:hw] = cols[:, 7:8]
        r["BC"][hw : 2 * hw] = jnp.zeros((hw, 1), F32)
        r["BC"][2 * hw : 3 * hw] = cols[:, 8:9]
        for t in range(4):
            for h in range(nh):
                QT[t, h, HD:aug] = ones
        for k in ("wq", "wk", "wv"):
            loc[k].wait()

    act["ready"] = ready
    act["start"] = start

    def qkv(s):
        t = ta[s]
        loc["tok%d" % s].wait()
        g = (mm(WT[...], TOK[t], 1, 1) + r["BC"][...]).astype(BF)
        sub = lax.broadcasted_iota(jnp.int32, (aug - HD, seq), 0)
        lane = lax.broadcasted_iota(jnp.int32, (aug - HD, seq), 1)
        dead = jnp.where(sub == 0, jnp.where(lane < ln[t], 0.0, -1e30), 0.0).astype(BF)
        for h in range(nh):
            QT[t, h, 0:HD] = g[h * HD : (h + 1) * HD] * jnp.asarray(HD**-0.5, BF)
            KT[t, h, 0:HD] = g[hw + h * HD : hw + (h + 1) * HD]
            KT[t, h, HD:aug] = dead
        VT[t] = g[2 * hw : 3 * hw]

    def head(s, h):
        t = ta[s]
        at = slice(h * HD, (h + 1) * HD)
        sc = mm(KT[t, h], QT[t, h], 0, 0)
        e = jnp.exp(sc - jnp.max(sc, axis=0, keepdims=True))
        ri = 1.0 / jnp.sum(e, axis=0, keepdims=True)
        el = e.astype(BF)
        ET[t, h] = el
        RI[t, h : h + 1] = ri
        o = (mm(VT[t, at], el, 1, 0) * ri).astype(BF)
        ATQ[t, at] = o
        if s == 3:
            ATO[m, at] = o

    for s in range(4):
        act["qkv.%d" % s] = lambda s=s: qkv(s)
        for h in range(nh):
            act["head.%d.%d" % (s, h)] = lambda s=s, h=h: head(s, h)
        if s < 3:
            put("at%d" % s, ATQ.at[ta[s]], ATO.at[m], c.mpeer((2, 3, 1)[s]))

    for h in (0, 1):
        put("sat%d" % h, ATO.at[1 - cb + 2 * h], SAT.at[h], sd)
    put("sfl", FL, SFL, sd)
    for k, h in ((1, yb), (3, 1 - yb)):
        put("sa%d" % k, ACT.at[1 - cb + 2 * h], SA.at[h], sd)

    def proj():
        need("gs0", "at0", "at1", "at2", *got(0))
        loc["own0"].wait()
        mixed = TOK[m].astype(F32) + f(0)
        for q in range(4):
            mixed += mm(ATO[q], WO[q], 0, 0)
        ACC[...] = mixed
        msg["sat0"].start()
        msg["sat1"].start()

    def norm1():
        def body(i, _):
            at = pl.ds(pl.multiple_of(i * nr, nr), nr)
            n1, i1 = norm_rows(ACC[at])
            N1[at] = n1
            I1[at] = i1
            FL[at] = (n1 * f(1) + f(2)).astype(BF)
            return 0

        lax.fori_loop(0, seq // nr, body, 0)
        msg["sfl"].start()
        need("v1", "v2", "v3")

    act["proj"], act["norm1"] = proj, norm1

    def ffn(k, j):
        if j == 0:
            if k == 0:
                loc["own1"].wait()
            elif k == 1:
                need("gs1")
            elif k == 3:
                need(*got(1))
        q = qk[k]
        at = slice(j * cw, (j + 1) * cw)
        h = mm(FL[...], UA[q, :, at], 1, 0) + VA[q, 6:7, at]
        g, gp = gelu_pair(h)
        ACT[q, :, at] = g.astype(BF)
        GP[q, :, at] = gp.astype(BF)

    def down(k):
        if k == 0:
            loc["own2"].wait()
        elif k == 1:
            need("gs2")
        elif k == 3:
            need(*got(2))
        y = mm(ACT[qk[k]], DA[qk[k]], 1, 0)
        if k == 0:
            ACC[...] = y
        else:
            ACC[...] += y

    for k in range(4):
        for j in range(3):
            act["ffn.%d.%d" % (k, j)] = lambda k=k, j=j: ffn(k, j)
        act["down.%d" % k] = lambda k=k: down(k)

    def fold(x):
        return jnp.sum(x.reshape(x.shape[0] // 8, 8, x.shape[1]), axis=0)

    zero = jnp.zeros((8, d), F32)

    def norm2():
        loc["cot"].wait()

        def body(i, sums):
            at = pl.ds(pl.multiple_of(i * nr, nr), nr)
            n2, i2 = norm_rows(N1[at] * f(1) + f(2) + ACC[at] + f(3))
            ct = COT[at].astype(F32)
            LOB[at] = (n2 * f(4) + f(5)).astype(BF)
            cg = ct * f(4)
            d2 = i2 * (
                cg
                - jnp.mean(cg, axis=-1, keepdims=True)
                - n2 * jnp.mean(cg * n2, axis=-1, keepdims=True)
            )
            ACC[at] = d2
            D2L[at] = d2.astype(BF)
            return sums[0] + fold(d2), sums[1] + fold(ct * n2), sums[2] + fold(ct)

        sums = lax.fori_loop(0, seq // nr, body, (zero,) * 3)
        SG[...] = jnp.zeros(SG.shape, F32)
        for i in range(3):
            SG[3 + i : 4 + i] = jnp.sum(sums[i], axis=0, keepdims=True)
        loc["lo"].start()

    act["norm2"] = norm2
    put("d2", D2L, SD2, sd)
    put("lo", LOB, LO.at[m], yd)
    put("los", LOB, LO.at[m], sd)
    put("lof", LO.at[yq], LO.at[yq], sd)
    local("lo", LOB, LO.at[m])
    act["lo_fwd"] = lambda: need("lo")

    def d_hidden(k):
        q = qk[k]

        def chunk(j, _):
            at = pl.ds(pl.multiple_of(j * cw, 128), cw)
            dh = (mm(D2L[...], DA[q, at, :], 1, 1) * GP[q, :, at].astype(F32)).astype(BF)
            GP[q, :, at] = dh
            SG[pl.ds(8 + q, 1), at] = jnp.sum(dh.astype(F32), axis=0, keepdims=True)
            return 0

        lax.fori_loop(0, 3, chunk, 0)

    for k in range(4):
        act["dh.%d" % k] = lambda k=k: d_hidden(k)
    put("sh1", GP.at[qk[1]], SH.at[yb], sd)
    put("sh3", GP.at[qk[3]], SH.at[1 - yb], sd)

    def down_grad(i):
        need("d2", "sa1", "sa3")
        _, at = cut(DOWN, i)

        def body(h, _):
            q = cb + 2 * h
            GD[h, at] = (mm(ACT[q, :, at], D2L[...], 0, 0) + mm(SA[h, :, at], SD2[...], 0, 0)).astype(BF)
            return 0

        lax.fori_loop(0, 2, body, 0)

    def up_grad(i):
        need("sh1", "sh3", "sfl")
        _, at = cut(UP, i)

        def body(h, _):
            q = cb + 2 * h
            GU[h, at] = (mm(FL[:, at], GP[q], 0, 0) + mm(SFL[:, at], SH[h], 0, 0)).astype(BF)
            return 0

        lax.fori_loop(0, 2, body, 0)

    for i in range(len(DOWN)):
        act["gd.%d" % i] = lambda i=i: down_grad(i)
    for i in range(len(UP)):
        act["gu.%d" % i] = lambda i=i: up_grad(i)

    def d_first(k):
        ACC[...] += mm(GP[qk[k]], UA[qk[k]], 1, 1)

    for k in range(4):
        act["d1.%d" % k] = lambda k=k: d_first(k)

    def norm1_back():
        need("sh1", "sh3")
        early = ["d2", "sh1", "sh3", "sa1", "sa3"] + ["gs%d" % a for a in range(3)]
        early += ["g%s%d" % (k, p) for k in ("x", "z", "dz", "dx", "t", "y") for p in range(len(parts))]
        for k in early:
            msg[k].wait_send()
            sent.discard(k)

        def body(i, sums):
            at = pl.ds(pl.multiple_of(i * nr, nr), nr)
            d1, n1 = ACC[at], N1[at]
            cg = d1 * f(1)
            dm = I1[at] * (
                cg
                - jnp.mean(cg, axis=-1, keepdims=True)
                - n1 * jnp.mean(cg * n1, axis=-1, keepdims=True)
            )
            ACC[at] = dm
            DML[at] = dm.astype(BF)
            return sums[0] + fold(dm), sums[1] + fold(d1 * n1), sums[2] + fold(d1)

        sums = lax.fori_loop(0, seq // nr, body, (zero,) * 3)
        for i in range(3):
            SG[i : 1 + i] = jnp.sum(sums[i], axis=0, keepdims=True)

    act["norm1b"] = norm1_back
    put("dm", DML, SD2, sd)

    def d_attended(k):
        q = qk[k]
        g = mm(WO[q], DML[...], 1, 1).astype(BF)
        if k == 0:
            DOT[m] = g
        else:
            DTS[q] = g

    for k in range(4):
        act["datt.%d" % k] = lambda k=k: d_attended(k)
    put("h1", DTS.at[qk[1]], DOT.at[m], sd)
    base = len(msg)
    for k in (2, 3):
        msg["h%d" % k] = rcopy(DTS.at[qk[k]], DOT.at[m], r["ms"].at[base + k - 2], r["mr"].at[base + cb], c.mpeer(k))
    for k in (0, 1):
        msg["l%d" % k] = rcopy(DTS.at[0], DOT.at[0], r["ms"].at[base + k], r["mr"].at[base + k], yd)

    def out_grad():
        need("dm", "sat0", "sat1")
        for h in (0, 1):
            q = cb + 2 * h
            GO[h] = (mm(ATO[q], DML[...], 1, 0) + mm(SAT[h], SD2[...], 1, 0)).astype(BF)

    act["go"] = out_grad

    tb = [2 * yb, 2 * yb + 1, 2 * (1 - yb), 3 - 2 * yb]
    mine, theirs = (pl.ds(pl.multiple_of(v * hf, hf), hf) for v in (cb, 1 - cb))

    def back(s, h):
        t = tb[s]
        if h == 0:
            need(*(("h1", "dm") if s < 2 else ("l0", "l1")))
        if s == 0 and h == 0:
            BQ[...] = jnp.zeros(BQ.shape, F32)
        at = slice(h * HD, (h + 1) * HD)
        g = DOT[t, at].astype(F32) * RI[t, h : h + 1]
        dd = jnp.sum(g * ATQ[t, at].astype(F32), axis=0, keepdims=True)
        gl = g.astype(BF)
        e = ET[t, h]
        ds = (e.astype(F32) * (mm(VT[t, at], gl, 0, 0) - dd)).astype(BF)
        dq = mm(KT[t, h, 0:HD], ds, 1, 0) * HD**-0.5
        dk = mm(QT[t, h, 0:HD], ds, 1, 1)
        dv = mm(gl, e, 1, 1)
        for i, x in enumerate((dq, dk, dv)):
            DA[t, i * hw + h * HD : i * hw + (h + 1) * HD, 0:seq] = x.astype(BF)

    def d_tokens(s):
        t = tb[s]
        g = DA[t, 0 : 3 * hw, 0:seq]
        BQ[:, 0 : 3 * hw] += mm(jnp.ones((8, seq), BF), g, 1, 1)
        dx = mm(g, WT[...], 0, 0)
        if s < 2:
            dx += jnp.where(cb == s, 1.0, 0.0) * ACC[...]
        ACT[t] = dx.astype(BF)

    def across(s):
        need("xc%d" % s, "l0", "l1")
        add_rows(ACT.at[tb[s], mine], UA.at[s, 0:hf], hf)

    def settle(s):
        o = (s + 2) % 4
        need("xy%d" % o)
        for k in ("xc%d" % s, "xy%d" % s):
            msg[k].wait_send()
            sent.discard(k)
        add_rows(ACT.at[tb[s], mine], UA.at[s, hf:seq], hf)
        loc["xt%d" % s].start()

    for s in range(4):
        for h in range(nh):
            act["ab.%d.%d" % (s, h)] = lambda s=s, h=h: back(s, h)
        act["dx.%d" % s] = lambda s=s: d_tokens(s)
        act["across.%d" % s] = lambda s=s: across(s)
        act["settle.%d" % s] = lambda s=s: settle(s)
        t = tb[s]
        part = ACT.at[t, mine]
        put("xc%d" % s, ACT.at[t, theirs], UA.at[s, 0:hf], sd)
        put("xt%d" % s, part, TG.at[t, mine], sd)
        local("xt%d" % s, part, TG.at[t, mine])
    base = len(msg)
    for s in range(4):
        o = (s + 2) % 4
        msg["xy%d" % s] = Both(
            rcopy(ACT.at[tb[s], mine], UA.at[o, hf:seq], r["ms"].at[base + s], r["mr"].at[base + o], yd),
            rcopy(ACT.at[tb[o], mine], UA.at[o, hf:seq], r["ms"].at[base + s], r["mr"].at[base + o], yd),
        )

    def qkv_grad(i):
        at = slice(i * hw, (i + 1) * hw)
        g = mm(DA[0, at, 0:seq], TOK[0], 1, 0)
        for t in range(1, 4):
            g += mm(DA[t, at, 0:seq], TOK[t], 1, 0)
        GQ[0, at] = g.astype(BF)

    for i in range(3):
        act["gq.%d" % i] = lambda i=i: qkv_grad(i)

    def view(G, base):
        def at(h, off, n):
            if isinstance(off, int):
                return G.at[h, base + off : base + off + n]
            return G.at[h, pl.ds(pl.multiple_of(base + off, 16), n)]

        return at

    def rows_of(O, base):
        def at(off, n):
            return O.at[pl.ds(pl.multiple_of(base + off, 16), n)]

        return at

    units = {}
    for j, (name, order, rows, base) in enumerate(unit_list(d, hw)):
        G, O = {"D": (GD, r["o_OD"]), "U": (GU, r["o_OU"]), "O": (GO, r["o_OO"]), "Q": (GQ, r["o_OQ"])}[name[1]]
        slots = [r["R%d%d" % (j, i)] for i in range(len(order))] + [r["X%d" % j].at[e] for e in range(nbits - 2)]
        units[name] = Unit(
            c, view(G, base), rows, order, slots, r["us"].at[j], r["ur"].at[j], rows_of(O, base), r["ul"].at[j]
        )
    dps = [c.dpeer(b) for b in range(nbits)]
    swaps = {
        "S": Swap(SG, r["SGR"], r["ws"], r["wr"], [sd, yd] + dps, 5),
        "B": Swap(BQ, r["BQR"], r["zs"], r["zr"], dps, 3),
    }

    sent = set()
    for k in SCHEDULE:
        if k in act:
            act[k]()
        elif k[0] == ">":
            w = k[1:].split(".")
            if w[0] in units:
                units[w[0]].send(int(w[1]), int(w[2]))
            elif w[0] in swaps:
                swaps[w[0]].send(int(w[1]))
            else:
                msg[k[1:]].start()
                sent.add(k[1:])
        else:
            w = k.split("/")
            (units[w[0]] if w[0] in units else swaps[w[0]]).finish(int(w[1]) - 1)

    r["o_OS"][...] = SG[...]
    r["o_OB"][...] = BQ[...]
    for k in ["v1", "v2", "v3", "sat0", "sat1", "sfl"] + [k for k in msg if k in sent]:
        msg[k].wait_send()
    need("los", "lof", "xt0", "xt1", "xt2", "xt3")
    for k in ("lo", "xt0", "xt1", "xt2", "xt3"):
        loc[k].wait()
    for u in units.values():
        u.drain()


class Both:
    def __init__(self, out, into):
        self.start, self.wait_send, self.wait_recv = out.start, out.wait_send, into.wait_recv


def cut(parts, i):
    base = sum(n for _, n in parts[:i])
    return parts[i][0], slice(base, base + parts[i][1])


def unit_list(d, hw):
    assert sum(n for _, n in DOWN) == d and sum(n for _, n in UP) == d
    res = []
    for name, parts in (("GD", DOWN), ("GU", UP)):
        for i in range(len(parts)):
            o, at = cut(parts, i)
            res.append((name + str(i), o, at.stop - at.start, at.start))
    return res + [("GO", OUT, hw, 0), ("GQ", QKV, 3 * hw, 0)]


def layer(tok4, cot4, lengths, vecs, wq, wk, wv, wo, wu, wd, nbits):
    nt, seq, d = tok4.shape
    hw = wq.shape[0]
    ff = wu.shape[1]
    nh = hw // HD
    V = pltpu.VMEM
    S = jax.ShapeDtypeStruct
    DMA = pltpu.SemaphoreType.DMA
    nex = nbits - 2
    nu = len(unit_list(d, hw))
    scratch = {
        "TOK": V((nt, seq, d), BF),
        "VEC": V((16, d), F32),
        "BC": V((3 * hw, 1), F32),
        "GQ": V((1, 3 * hw, d), BF),
        "WT": V((3 * hw, d), BF),
        "QT": V((nt, nh, HD + 16, seq), BF),
        "KT": V((nt, nh, HD + 16, seq), BF),
        "VT": V((nt, hw, seq), BF),
        "ET": V((nt, nh, seq, seq), BF),
        "RI": V((nt, 8, seq), F32),
        "ATQ": V((nt, hw, seq), BF),
        "ATO": V((nt, hw, seq), BF),
        "N1": V((seq, d), F32),
        "I1": V((seq, 1), F32),
        "FL": V((seq, d), BF),
        "ACT": V((nt, seq, ff), BF),
        "GP": V((nt, seq, ff), BF),
        "WOA": V((nt, hw, d), BF),
        "UA": V((nt, d, ff), BF),
        "DA": V((nt, ff, d), BF),
        "VA": V((nt, 16, d), F32),
        "ACC": V((seq, d), F32),
        "COT": V((seq, d), BF),
        "SA": V((2, seq, ff), BF),
        "SH": V((2, seq, ff), BF),
        "SFL": V((seq, d), BF),
        "SD2": V((seq, d), BF),
        "D2L": V((seq, d), BF),
        "SAT": V((2, hw, seq), BF),
        "DOT": V((nt, hw, seq), BF),
        "DTS": V((nt, hw, seq), BF),
        "SG": V((16, d), F32),
        "SGR": V((nbits + 2, 16, d), F32),
        "BQ": V((8, d), F32),
        "BQR": V((nbits, 8, d), F32),
        "GD": V((2, ff, d), BF),
        "GU": V((2, d, ff), BF),
        "GO": V((2, hw, d), BF),
        "ls": DMA((16,)),
        "ms": DMA((96,)),
        "mr": DMA((96,)),
        "us": DMA((nu, 8 + nex)),
        "ur": DMA((nu, 8 + nex)),
        "ul": DMA((nu,)),
        "ws": DMA((nbits + 2,)),
        "wr": DMA((nbits + 2,)),
        "zs": DMA((nbits,)),
        "zr": DMA((nbits,)),
    }
    for j, (_, order, rows, _) in enumerate(unit_list(d, hw)):
        n, h = rows, 2 if "y" in order else 1
        for i, ax in enumerate(order):
            if ax == "y":
                h = 1
            else:
                n //= 2
            scratch["R%d%d" % (j, i)] = V((h, n, d), BF)
        scratch["X%d" % j] = V((max(nex, 1), 1, n, d), BF)
    ins = {
        "len": lengths, **vecs, "tok": tok4, "cot": cot4,
        "wq": wq, "wk": wk, "wv": wv, "wo": wo, "wu": wu, "wd": wd,
    }
    A = pl.BlockSpec(memory_space=pl.ANY)
    B = pl.BlockSpec(memory_space=V)
    specs = [pl.BlockSpec(memory_space=pltpu.SMEM)] + [B] * len(vecs)
    specs += [A] * (len(ins) - len(specs))
    outs = {
        "LO": (S((nt, seq, d), BF), A),
        "TG": (S((nt, seq, d), BF), A),
        "OU": (S((d, ff), BF), A),
        "OD": (S((ff, d), BF), A),
        "OO": (S((hw, d), BF), A),
        "OQ": (S((3 * hw, d), BF), A),
        "OS": (S((16, d), F32), B),
        "OB": (S((8, d), F32), B),
    }
    names = list(ins) + ["o_" + n for n in outs] + list(scratch)

    def kernel(*refs):
        layer_kernel(nbits, names, *refs)

    res = pl.pallas_call(
        kernel,
        out_shape=[o[0] for o in outs.values()],
        in_specs=specs,
        out_specs=[o[1] for o in outs.values()],
        scratch_shapes=list(scratch.values()),
        compiler_params=pltpu.CompilerParams(
            collective_id=0, has_side_effects=True, vmem_limit_bytes=60 * 2**20
        ),
    )(*ins.values())
    return dict(zip(outs, res))


def shards(
    tokens, lengths, wq, bq, wk, wv, bv, wo, bo, g1, s1, wu, bu, wd, bd, g2, s2, cot
):
    n = lengths.shape[0]
    rows, d = tokens.shape
    seq = rows // n
    hw = wq.shape[1]
    m = lax.axis_index("mp")
    nbits = lax.axis_size("dp").bit_length() - 1
    f = lambda a: a.astype(F32)
    vecs = {
        "bo": bo, "g1": g1, "s1": s1, "bd": bd, "g2": g2, "s2": s2, "bu": bu, "bq": bq, "bv": bv
    }
    o = layer(
        tokens.reshape(n, seq, d), cot.reshape(n, seq, d), lengths, vecs, wq.T, wk.T, wv.T, wo, wu, wd, nbits
    )
    res = finish([o[k] for k in ("LO", "TG", "OU", "OD", "OO", "OQ", "OS", "OB")])
    lo, tg, du, dd, do, dq, dk, dv, dbq, dbv, dbu, dbo, dg1, ds1, dbd, dg2, ds2 = res
    return (
        lo.reshape(rows, d), tg.reshape(rows, d), dq.T, dbq, dk.T, dv.T, dbv, do, dbo, dg1, ds1,
        du, dbu, dd, dbd, dg2, ds2,
    )


def finish_kernel(*refs):
    ins, outs, bufs, wide, (si, so) = refs[:8], refs[8:25], refs[25:31], refs[31:35], refs[35:37]
    loads = []
    for i in range(2):
        loads.append([pltpu.make_async_copy(ins[i].at[t], bufs[i].at[t], si.at[i * 4 + t]) for t in range(4)])
    loads += [[pltpu.make_async_copy(ins[i], bufs[i], si.at[6 + i])] for i in range(2, 6)]
    for i in (0, 1, 2, 3, 5, 4):
        for x in loads[i]:
            x.start()
    stores = []

    def store(src, dst):
        stores.append(pltpu.make_async_copy(src, dst, so.at[len(stores)]))
        stores[-1].start()

    sg, b = ins[6], ins[7]
    m = lax.axis_index("mp")
    hw = ins[5].shape[0] // 3
    d = ins[5].shape[1]
    outs[8][...] = b[0:1, 0:hw].reshape(hw)
    outs[9][...] = b[0:1, 2 * hw : 3 * hw].reshape(hw)
    outs[10][...] = sg[pl.ds(8 + m, 1)].reshape(d)
    for i in range(6):
        outs[11 + i][...] = sg[i : i + 1].reshape(d)
    for i in range(2):
        for t in range(4):
            loads[i][t].wait()
            store(bufs[i].at[t], outs[i].at[t])
    for i in (2, 3, 5, 4):
        loads[i][0].wait()
        h = 192
        for k in range(bufs[i].shape[0] // h):
            at = slice(k * h, (k + 1) * h)
            wide[i - 2][at] = bufs[i][at].astype(F32)
            store(wide[i - 2].at[at], outs[5 + k] if i == 5 else outs[i].at[at])
    for x in stores:
        x.wait()


def finish(vals):
    S = jax.ShapeDtypeStruct
    V = pltpu.VMEM
    A = pl.BlockSpec(memory_space=pl.ANY)
    B = pl.BlockSpec(memory_space=V)
    shapes = [v.shape for v in vals]
    d = shapes[5][1]
    hw = shapes[5][0] // 3
    outs = [S(shapes[0], BF), S(shapes[1], BF)] + [S(s, F32) for s in shapes[2:5]]
    outs += [S((hw, d), F32)] * 3 + [S((hw,), F32)] * 2 + [S((d,), F32)] * 7
    return pl.pallas_call(
        finish_kernel,
        out_shape=outs,
        in_specs=[A] * 6 + [B] * 2,
        out_specs=[A] * 8 + [B] * 9,
        scratch_shapes=[V(s, BF) for s in shapes[:6]]
        + [V(s, F32) for s in shapes[2:6]]
        + [pltpu.SemaphoreType.DMA((12,)), pltpu.SemaphoreType.DMA((24,))],
        compiler_params=pltpu.CompilerParams(vmem_limit_bytes=60 * 2**20),
    )(*vals)


def solution(mesh):
    row, col, one, rep = P("dp", None), P(None, "mp"), P("mp"), P()
    low = P("mp", None)
    in_specs = (
        row, P("dp"), col, one, col, col, one, low, rep, rep, rep, col, one, low, rep, rep, rep, row,
    )
    out_specs = (
        row, row, col, one, col, col, one, low, rep, rep, rep, col, one, low, rep, rep, rep,
    )
    return jax.shard_map(shards, mesh=mesh, in_specs=in_specs, out_specs=out_specs, check_vma=False)
```
